256 devices in a mesh: lon: 32 (over x, z), lat: 8 (over y, core).
Axes of the slice: x: 4, y: 4, z: 8, core: 2. Of those that a mesh axis runs over, the one named last changes fastest.
Arguments:
- right_side: float32 [4096, 8192], P('lat', 'lon'), may hold values from -60 to 60
- depth: float32 [4096, 8192], P('lat', 'lon'), may hold values from 0.2 to 6
- mask: int32 [4096, 8192], P('lat', 'lon'), may hold values 0 or 1
- basis: float32 [4096, 8192], P('lat', 'lon'), may hold values from 0.5 to 2
- coarse_inverse: float32 [2048, 2048], P(('lon', 'lat')), may hold values from -0.00018310547 to 0.00018310547, as said below
Outputs:
- solution_field: float32 [4096, 8192], P('lat', 'lon')
- residual: float32 [4096, 8192], P('lat', 'lon')
The draws below stay inside these ranges and needn't reach their ends.
Inputs may be any that keep to these rules, and one draw needn't show every extreme that they name: coarse_inverse is exactly symmetric. `mask`: 1 marks an ocean cell, 0 a land cell.
All inputs are finite; a program needn't handle non-finite values. No bound on the sum of `mask` on one device may be relied on, other than what follows from the above.
Results may differ from the reference program's by a relative error of at most 0.0003.
Values sent between devices are 32-bit elements; how exact they have to be, the bound alone decides.
No kernel may reach another device: no remote copies, remote signals or barrier semaphores. Data moves between devices by JAX's collectives and lax.ppermute only.
A program may use at most 64 MiB of HBM per device.

```python
import math
import jax
import jax.numpy as jnp
from jax import lax

CX = 256
CY = 512
ITERS = 2
SWEEPS = 4
AGG_LAT = 4
AGG_LON = 2
K_DEV = 8
NLON = 8192
NLAT = 4096
COARSE = 2048
N_LON = 32
N_LAT = 8


def draw_right_side(key, part):
    key = jax.random.fold_in(key, 11)
    split_keys = jax.random.split(key, 3)
    column_pos = jnp.arange(NLON).astype(jnp.float32) / NLON
    column_scale = jnp.exp(column_pos * math.log(3.0) + jax.random.uniform(split_keys[1], (NLON,), jnp.float32, 0.0, math.log(3.0)))
    row_scale = jnp.exp(jax.random.uniform(split_keys[2], (NLAT, 1), jnp.float32, 0.0, math.log(3.3)))
    values = jnp.clip(jax.random.normal(split_keys[0], (NLAT, NLON), jnp.float32), -4.0, 4.0)
    return (0.5 * values * row_scale * column_scale[None, :]).astype(jnp.float32)


def draw_coarse_inverse(key, part):
    key = jax.random.fold_in(key, 23)
    split_keys = jax.random.split(key, 2)
    raw_values = jnp.clip(jax.random.normal(split_keys[0], (COARSE, COARSE), jnp.float32), -4.0, 4.0)
    off_values = (raw_values + raw_values.T) * (0.6 / math.sqrt(COARSE))
    diagonal = jax.random.uniform(split_keys[1], (COARSE,), jnp.float32, 1.0, 3.0)
    index_list = jnp.arange(COARSE)
    same_index = index_list[:, None] == index_list[None, :]
    matrix = jnp.where(same_index, diagonal[:, None], off_values)
    return (matrix / (CX * CY // K_DEV)).astype(jnp.float32)


def touch_ends(entries, rng, low, high):
    place = [jax.random.randint(jax.random.fold_in(rng, axis), (), 0, length) for axis, length in enumerate(entries.shape)]
    main_axis = entries.shape.index(max(entries.shape))
    beside = place[:main_axis] + [(place[main_axis] + 1) % entries.shape[main_axis]] + place[main_axis + 1:]
    return entries.at[tuple(place)].set(low).at[tuple(beside)].set(high)


def shard_levels(stream_key, dims, pieces, least, largest):
    factor_of, own = 1.0, jax.random.fold_in(stream_key, 6)
    for position, shards_of in pieces:
        draws = jnp.exp(jax.random.uniform(jax.random.fold_in(own, position), (shards_of,), jnp.float32, least / len(pieces), largest / len(pieces)))
        factor_of = factor_of * jnp.repeat(draws, dims[position] // shards_of).reshape([-1 if axis == position else 1 for axis in range(len(dims))])
    return factor_of


def setup_inputs(seed: int = 0) -> dict:
    keys = jax.random.split(jax.random.key(seed), 6)
    right_side = draw_right_side(jax.random.fold_in(keys[5], 71), 0)
    depth = jnp.clip(jnp.exp(math.log(6.0) - 3.4011974 * jax.random.uniform(keys[1], (NLAT, NLON), jnp.float32) ** shard_levels(keys[1], (NLAT, NLON), ((0, 8), (1, 32)), -0.2, 0.2)), 0.2, 6.0)
    mask = touch_ends((jax.random.randint(keys[2], (NLAT, NLON), 0, 8) < 7).astype(jnp.int32), jax.random.fold_in(keys[2], 1), 0, 1)
    basis = jnp.clip(jnp.exp(math.log(2.0) - 1.3862944 * jax.random.uniform(keys[3], (NLAT, NLON), jnp.float32) ** shard_levels(keys[3], (NLAT, NLON), ((0, 8), (1, 32)), -0.2, 0.2)), 0.5, 2.0)
    coarse_inverse = draw_coarse_inverse(jax.random.fold_in(keys[5], 71), 0)
    return {"right_side": right_side, "depth": depth, "mask": mask, "basis": basis, "coarse_inverse": coarse_inverse}


low_edge = 0.1
high_edge = 2.0
shift_scale = 1.0e-5


def chebyshev_plan(sweep_total):
    interval_mid = (high_edge + low_edge) / 2.0
    interval_half = (high_edge - low_edge) / 2.0
    mid_ratio = interval_mid / interval_half
    previous = 1.0 / mid_ratio
    sweep_pairs = []
    for sweep_number in range(sweep_total - 1):
        fresh_rho = 1.0 / (2.0 * mid_ratio - previous)
        sweep_pairs.append((fresh_rho * previous, 2.0 * fresh_rho / interval_half))
        previous = fresh_rho
    return 1.0 / interval_mid, sweep_pairs


def reference(right_side, depth, mask, basis, coarse_inverse):
    mask_float = mask.astype(jnp.float32)
    wet_depth = depth * mask_float
    row_index = jnp.arange(NLAT, dtype=jnp.int32)
    latitude = (row_index.astype(jnp.float32) + 0.5) * (2.6 / NLAT) - 1.3
    east_face = jnp.minimum(wet_depth, jnp.roll(wet_depth, -1, 1)) / jnp.cos(latitude)[:, None]
    inside = (row_index <= NLAT - 2).astype(jnp.float32)
    north_face = jnp.minimum(wet_depth, jnp.roll(wet_depth, -1, 0)) * jnp.cos(latitude + 1.3 / NLAT)[:, None] * inside[:, None]
    shift_column = (shift_scale * jnp.cos(latitude))[:, None]
    west_face = jnp.roll(east_face, 1, 1)
    south_face = jnp.roll(north_face, 1, 0)
    inverse_diag = 1.0 / (shift_column + east_face + west_face + north_face + south_face)

    def operate(field_values):
        return (shift_column * field_values
                + east_face * (field_values - jnp.roll(field_values, -1, 1))
                + west_face * (field_values - jnp.roll(field_values, 1, 1))
                + north_face * (field_values - jnp.roll(field_values, -1, 0))
                + south_face * (field_values - jnp.roll(field_values, 1, 0)))

    sweep_start, sweep_pairs = chebyshev_plan(SWEEPS)
    block_rows = CY // AGG_LAT
    block_cols = CX // AGG_LON

    def smooth(residual):
        step_direction = sweep_start * (inverse_diag * residual)
        estimate = step_direction
        for first_coef, second_coef in sweep_pairs:
            remain = residual - operate(estimate)
            step_direction = first_coef * step_direction + second_coef * (inverse_diag * remain)
            estimate = estimate + step_direction
        return estimate

    def restrict(residual):
        blocks = (basis * residual).reshape(N_LAT, AGG_LAT, block_rows, N_LON, AGG_LON, block_cols)
        sums = jnp.sum(blocks, axis=(2, 5))
        return jnp.transpose(sums, (2, 0, 1, 3)).reshape(-1)

    def prolong(solved):
        shaped = jnp.transpose(solved.reshape(N_LON, N_LAT, AGG_LAT, AGG_LON), (1, 2, 0, 3))
        spread = jnp.broadcast_to(shaped[:, :, None, :, :, None], (N_LAT, AGG_LAT, block_rows, N_LON, AGG_LON, block_cols))
        return spread.reshape(NLAT, NLON)

    def precondition(residual):
        solved = jnp.dot(coarse_inverse, restrict(residual), precision=lax.Precision.HIGHEST)
        return mask_float * (smooth(residual) + basis * prolong(solved))

    solution_field = jnp.zeros_like(right_side)
    residual = right_side * mask_float
    update = precondition(residual)
    search = update
    for turn_index in range(ITERS):
        applied = operate(search)
        curvature_sum = jnp.sum(search * applied)
        step_size = jnp.sum(search * residual) / curvature_sum
        solution_field = solution_field + step_size * search
        residual = residual - step_size * applied
        if turn_index + 1 < ITERS:
            update = precondition(residual)
            blend_factor = -jnp.sum(update * applied) / curvature_sum
            search = update + blend_factor * search
    return solution_field, residual
```

```python
import functools

import jax
import jax.numpy as jnp
from jax import lax
from jax.experimental import pallas as pl
from jax.experimental.pallas import tpu as pltpu
from jax.sharding import PartitionSpec as P

SWEEPS = 4
AGG_LAT = 4
AGG_LON = 2
LOW_EDGE = 0.1
HIGH_EDGE = 2.0
SHIFT_SCALE = 1.0e-5

NY = 512
NX = 256
HY = 16
WX = 9
ROWS = NY + 2 * HY
LANES = 128
BLK = 3
BAND = NY // AGG_LAT
STEP = 32
SLOTS = LANES // 8
AXES = ("lon", "lat")
F32 = jnp.float32


def chebyshev_plan(sweep_total):
    interval_mid = (HIGH_EDGE + LOW_EDGE) / 2.0
    interval_half = (HIGH_EDGE - LOW_EDGE) / 2.0
    mid_ratio = interval_mid / interval_half
    previous = 1.0 / mid_ratio
    pairs = []
    for _ in range(sweep_total - 1):
        fresh = 1.0 / (2.0 * mid_ratio - previous)
        pairs.append((fresh * previous, 2.0 * fresh / interval_half))
        previous = fresh
    return 1.0 / interval_mid, pairs


def lane_ids(rows):
    return lax.broadcasted_iota(jnp.int32, (rows, LANES), 1)


def east_of(blocks):
    lane = lane_ids(blocks[0].shape[0])
    rolled = [pltpu.roll(v, LANES - 1, 1) for v in blocks]
    return [jnp.where(lane == LANES - 1, rolled[(b + 1) % BLK], rolled[b]) for b in range(BLK)]


def west_of(blocks):
    lane = lane_ids(blocks[0].shape[0])
    rolled = [pltpu.roll(v, 1, 1) for v in blocks]
    return [jnp.where(lane == 0, rolled[(b + BLK - 1) % BLK], rolled[b]) for b in range(BLK)]


def load(ref, start, rows):
    return [ref[b, pl.ds(start, rows), :] for b in range(BLK)]


def store(ref, start, rows, blocks):
    for b in range(BLK):
        ref[b, pl.ds(start, rows), :] = blocks[b]


def for_strips(fn):
    fn(HY - 8, 8)

    def step(i, carry):
        fn(pl.multiple_of(HY + i * STEP, 8), STEP)
        return carry

    lax.fori_loop(0, NY // STEP, step, 0)
    fn(HY + NY, 8)


def clear_ends(ref):
    zero = jnp.zeros((8, LANES), F32)
    for b in range(BLK):
        ref[b, 0:8, :] = zero
        ref[b, ROWS - 8 : ROWS, :] = zero


def operate(v_ref, east_ref, west_ref, north_ref, shift_ref, start, rows):
    here = load(v_ref, start, rows)
    up, down = load(v_ref, start + 1, rows), load(v_ref, start - 1, rows)
    right, left = east_of(here), west_of(here)
    ef, wf = load(east_ref, start, rows), load(west_ref, start, rows)
    nf, sf = load(north_ref, start, rows), load(north_ref, start - 1, rows)
    shift = shift_ref[pl.ds(start, rows), :]
    out = [
        shift * here[b]
        + ef[b] * (here[b] - right[b])
        + wf[b] * (here[b] - left[b])
        + nf[b] * (here[b] - up[b])
        + sf[b] * (here[b] - down[b])
        for b in range(BLK)
    ]
    return here, out


def fold(x):
    return jnp.sum(x.reshape(-1, 8, LANES), axis=0)


def total(x):
    return jnp.sum(jnp.sum(x, axis=1, keepdims=True), axis=0, keepdims=True)


def own_row(tile_ref, values, scalars=()):
    lane = lane_ids(1)
    base = (tile_ref[0] % SLOTS) * 8
    other = ((tile_ref[0] + SLOTS // 2) % SLOTS) * 8
    row = jnp.zeros((1, LANES), F32)
    for k, value in enumerate(values):
        row = jnp.where(lane == base + k, value, row)
    for k, value in enumerate(scalars):
        row = jnp.where(lane == other + k, value, row)
    return row


def own_row_sums(got_ref, count):
    rows = got_ref.shape[0]
    lane = lane_ids(rows)
    slot = lax.broadcasted_iota(jnp.int32, (rows, LANES), 0) % SLOTS
    other = ((slot + SLOTS // 2) % SLOTS) * 8
    got = got_ref[...]
    return [total(fold(jnp.where(lane == other + k, got, 0.0))) for k in range(count)]


def fill_rows(ref, row):
    ref[...] = jnp.broadcast_to(row, ref.shape)


def pack_kernel(tile_ref, rhs_ref, depth_ref, mask_ref, basis_ref, inverse_ref, gather_ref, west_ref, east_ref):
    groups = inverse_ref.shape[1] // LANES
    lane = lane_ids(STEP)
    sums = []
    for g in range(AGG_LAT):

        def step(i, carry, g=g):
            start = pl.multiple_of(g * BAND + i * STEP, 8)
            out_row = pl.multiple_of(i * STEP, 8)
            accs = []
            fields = []
            for b in range(AGG_LON):
                at = (pl.ds(start, STEP), pl.ds(b * LANES, LANES))
                mask = mask_ref[at].astype(F32)
                wet = depth_ref[at] * mask
                res = rhs_ref[at] * mask
                weight = basis_ref[at] * mask
                accs.append(carry[b] + fold(weight * res))
                fields.append((wet, res, weight))
            for ref, b, extra in ((west_ref, 0, 0), (east_ref, 1, WX)):
                if g == 0:
                    packed = jnp.zeros((STEP, LANES), F32)
                else:
                    packed = ref[pl.ds(out_row, STEP), :]
                for f in range(3):
                    lo = 32 * g + WX * f
                    moved = pltpu.roll(fields[b][f], (lo + extra) % LANES, 1)
                    packed = jnp.where((lane >= lo) & (lane < lo + WX), moved, packed)
                ref[pl.ds(out_row, STEP), :] = packed
            return tuple(accs)

        zero = jnp.zeros((8, LANES), F32)
        for acc in lax.fori_loop(0, BAND // STEP, step, (zero,) * AGG_LON):
            sums.append(total(acc))
    fill_rows(gather_ref, own_row(tile_ref, sums))
    for g in range(groups):
        part = inverse_ref[:, g * LANES : (g + 1) * LANES]
        west_ref[BAND + 8 * g : BAND + 8 * g + 8, :] = part
        east_ref[BAND + 8 * g : BAND + 8 * g + 8, :] = part


def unpack_columns(left_ref, right_ref, g, start, rows):
    lane = lane_ids(rows)
    left, right = left_ref[pl.ds(start, rows), :], right_ref[pl.ds(start, rows), :]
    out = []
    for f in range(3):
        lo = 32 * g + WX * f
        from_right = pltpu.roll(right, (LANES - lo) % LANES, 1)
        from_left = pltpu.roll(left, (2 * LANES - lo - WX) % LANES, 1)
        out.append(jnp.where(lane < WX, from_right, jnp.where(lane >= LANES - WX, from_left, 0.0)))
    return out


def own_fields(rhs_ref, depth_ref, mask_ref, basis_ref, start, rows, b):
    at = (pl.ds(start, rows), pl.ds(b * LANES, LANES))
    mask = mask_ref[at].astype(F32)
    return depth_ref[at] * mask, rhs_ref[at] * mask, basis_ref[at] * mask


def edge_kernel(rhs_ref, depth_ref, mask_ref, basis_ref, inverse_ref, left_ref, right_ref, south_ref, north_ref):
    groups = inverse_ref.shape[1] // LANES
    sub = lax.broadcasted_iota(jnp.int32, (8, LANES), 0)
    for ref, start, g, band in ((south_ref, 0, 0, 0), (north_ref, NY - HY, AGG_LAT - 1, AGG_LAT - 1)):
        blocks = [own_fields(rhs_ref, depth_ref, mask_ref, basis_ref, start, HY, b) for b in range(2)]
        blocks.append(unpack_columns(left_ref, right_ref, g, start % BAND, HY))
        for f in range(3):
            for b in range(BLK):
                at = (f * BLK + b) * HY
                ref[at : at + HY, :] = blocks[b][f]
        base = 3 * BLK * HY
        for i in range(groups):
            own = inverse_ref[:, i * LANES : (i + 1) * LANES]
            left = left_ref[BAND + 8 * i : BAND + 8 * i + 8, :]
            right = right_ref[BAND + 8 * i : BAND + 8 * i + 8, :]
            own = pltpu.roll(own, (8 - 2 * band) % 8, 0) if band else own
            left = pltpu.roll(left, (2 - 2 * band - 1 + 16) % 8, 0)
            right = pltpu.roll(right, (3 - 2 * band + 16) % 8, 0)
            picked = jnp.where(sub < 2, own, jnp.where(sub == 2, left, right))
            ref[base + 8 * i : base + 8 * i + 8, :] = picked


def smooth(res_ref, inv_ref, ops, est_refs, step_ref, finish):
    first, pairs = chebyshev_plan(SWEEPS)

    def start_strip(start, rows):
        inv, res = load(inv_ref, start, rows), load(res_ref, start, rows)
        value = [first * (inv[b] * res[b]) for b in range(BLK)]
        store(step_ref, start, rows, value)
        store(est_refs[0], start, rows, value)

    for_strips(start_strip)
    for k, (c1, c2) in enumerate(pairs):
        src, dst = est_refs[k % 2], est_refs[(k + 1) % 2]

        def strip(start, rows, src=src, dst=dst, c1=c1, c2=c2, last=k == len(pairs) - 1):
            here, applied = operate(src, *ops, start, rows)
            inv, res, step = load(inv_ref, start, rows), load(res_ref, start, rows), load(step_ref, start, rows)
            step = [c1 * step[b] + c2 * (inv[b] * (res[b] - applied[b])) for b in range(BLK)]
            value = [here[b] + step[b] for b in range(BLK)]
            if last:
                finish(start, rows, value)
            else:
                store(step_ref, start, rows, step)
                store(dst, start, rows, value)

        for_strips(strip)


def setup_kernel(
    rhs_ref, depth_ref, mask_ref, basis_ref, left_ref, right_ref, below_ref, above_ref, geo_ref,
    east_ref, west_ref, north_ref, inv_ref, basis_out, res_ref, smooth_ref,
    wet_ref, est_a, est_b, step_ref,
):
    outs = (wet_ref, res_ref, basis_out)
    for f, ref in enumerate(outs):
        for b in range(BLK):
            at = (f * BLK + b) * HY
            ref[b, 0:HY, :] = below_ref[at : at + HY, :]
            ref[b, HY + NY : ROWS, :] = above_ref[at : at + HY, :]
    for g in range(AGG_LAT):

        def fill(i, carry, g=g):
            start = pl.multiple_of(g * BAND + i * STEP, 8)
            for b in range(2):
                for f, value in enumerate(own_fields(rhs_ref, depth_ref, mask_ref, basis_ref, start, STEP, b)):
                    outs[f][b, pl.ds(HY + start, STEP), :] = value
            part = pl.multiple_of(i * STEP, 8)
            for f, value in enumerate(unpack_columns(left_ref, right_ref, g, part, STEP)):
                outs[f][2, pl.ds(HY + start, STEP), :] = value
            return carry

        lax.fori_loop(0, BAND // STEP, fill, 0)

    def east_west(start, rows):
        wet = load(wet_ref, start, rows)
        over = geo_ref[0, pl.ds(start, rows), :]
        nxt = east_of(wet)
        face = [jnp.minimum(wet[b], nxt[b]) * over for b in range(BLK)]
        store(east_ref, start, rows, face)
        store(west_ref, start, rows, west_of(face))

    def north(start, rows):
        wet, nxt = load(wet_ref, start, rows), load(wet_ref, start + 1, rows)
        cosine = geo_ref[1, pl.ds(start, rows), :]
        store(north_ref, start, rows, [jnp.minimum(wet[b], nxt[b]) * cosine for b in range(BLK)])

    for_strips(east_west)
    north(0, 8)
    for_strips(north)
    shift_ref = geo_ref.at[2]

    def diagonal(start, rows):
        ef, wf = load(east_ref, start, rows), load(west_ref, start, rows)
        nf, sf = load(north_ref, start, rows), load(north_ref, start - 1, rows)
        shift = shift_ref[pl.ds(start, rows), :]
        store(inv_ref, start, rows, [1.0 / (shift + ef[b] + wf[b] + nf[b] + sf[b]) for b in range(BLK)])

    for_strips(diagonal)
    for ref in (est_a, est_b, smooth_ref):
        clear_ends(ref)

    def finish(start, rows, value):
        wet = load(wet_ref, start, rows)
        store(smooth_ref, start, rows, [jnp.where(wet[b] > 0.0, value[b], 0.0) for b in range(BLK)])

    smooth(res_ref, inv_ref, (east_ref, west_ref, north_ref, shift_ref), (est_a, est_b), step_ref, finish)


def coarse_solve(got_ref, inverse_ref, left_ref, right_ref, below_ref, above_ref):
    groups = inverse_ref.shape[1] // LANES
    count = got_ref.shape[0] // groups
    base = 3 * BLK * HY
    accs = [jnp.zeros((8, LANES), F32) for _ in range(5)]
    mine = lane_ids(count) // 8 == lax.broadcasted_iota(jnp.int32, (count, LANES), 0)
    for i in range(groups):
        vec = jnp.sum(jnp.where(mine, got_ref[i * count : (i + 1) * count, :], 0.0), axis=0, keepdims=True)
        at = slice(BAND + 8 * i, BAND + 8 * i + 8)
        band = slice(base + 8 * i, base + 8 * i + 8)
        parts = (
            inverse_ref[:, i * LANES : (i + 1) * LANES],
            left_ref[at, :],
            right_ref[at, :],
            below_ref[band, :],
            above_ref[band, :],
        )
        accs = [acc + part * vec for acc, part in zip(accs, parts)]
    own, left, right, below, above = [jnp.sum(acc, axis=1, keepdims=True) for acc in accs]
    low = lane_ids(1) < LANES // 2

    def spread(value):
        return jnp.broadcast_to(value, (1, LANES))

    def edge(x):
        halo = jnp.where(low, spread(x[3:4]), spread(x[2:3]))
        return [spread(x[0:1]), spread(x[1:2]), halo]

    rows = [edge(below)]
    for a in range(AGG_LAT):
        halo = jnp.where(low, spread(right[2 * a : 2 * a + 1]), spread(left[2 * a + 1 : 2 * a + 2]))
        rows.append([spread(own[2 * a : 2 * a + 1]), spread(own[2 * a + 1 : 2 * a + 2]), halo])
    rows.append(edge(above))
    return rows


def for_bands(fn, carry_of=None):
    out = []
    fn(0, HY, 0, None)
    for a in range(AGG_LAT):

        def step(i, carry, a=a):
            return fn(pl.multiple_of(HY + a * BAND + i * STEP, 8), STEP, a + 1, carry)

        out.append(lax.fori_loop(0, BAND // STEP, step, carry_of))
    fn(HY + NY, HY, AGG_LAT + 1, None)
    return out


def search_kernel(
    tile_ref, got_ref, inverse_ref, left_ref, right_ref, below_ref, above_ref,
    east_ref, west_ref, north_ref, basis_ref, smooth_ref, geo_ref, res_ref,
    send_ref, search_ref, applied_ref,
):
    coarse = coarse_solve(got_ref, inverse_ref, left_ref, right_ref, below_ref, above_ref)

    def direction(start, rows, band, carry):
        part, weight = load(smooth_ref, start, rows), load(basis_ref, start, rows)
        store(search_ref, start, rows, [part[b] + weight[b] * coarse[band][b] for b in range(BLK)])
        return 0

    for_bands(direction, 0)
    ops = (east_ref, west_ref, north_ref, geo_ref.at[2])
    clear_ends(applied_ref)

    def apply(start, rows):
        here, out = operate(search_ref, *ops, start, rows)
        store(applied_ref, start, rows, out)
        return here, out

    apply(HY - 8, 8)
    sums = []
    zero = jnp.zeros((8, LANES), F32)
    curvature, projection = zero, zero
    for a in range(AGG_LAT):

        def step(i, carry, a=a):
            start = pl.multiple_of(HY + a * BAND + i * STEP, 8)
            here, out = apply(start, STEP)
            accs = [carry[b] + fold(basis_ref[b, pl.ds(start, STEP), :] * out[b]) for b in range(AGG_LON)]
            curvature, projection = carry[AGG_LON:]
            for b in range(AGG_LON):
                curvature = curvature + fold(here[b] * out[b])
                projection = projection + fold(here[b] * res_ref[b, pl.ds(start, STEP), :])
            return (*accs, curvature, projection)

        *accs, curvature, projection = lax.fori_loop(
            0, BAND // STEP, step, (zero,) * AGG_LON + (curvature, projection)
        )
        sums += [total(x) for x in accs]
    apply(HY + NY, 8)
    fill_rows(send_ref, own_row(tile_ref, sums, (total(curvature), total(projection))))


def second_kernel(
    applied_ref, inv_ref, east_ref, west_ref, north_ref, basis_ref, geo_ref,
    out_ref, est_a, est_b, step_ref,
):
    for ref in (est_a, est_b, out_ref):
        clear_ends(ref)

    def finish(start, rows, value):
        weight = load(basis_ref, start, rows)
        store(out_ref, start, rows, [jnp.where(weight[b] > 0.0, value[b], 0.0) for b in range(BLK)])

    smooth(applied_ref, inv_ref, (east_ref, west_ref, north_ref, geo_ref.at[2]), (est_a, est_b), step_ref, finish)


def sums_kernel(
    got_ref, inverse_ref, left_ref, right_ref, below_ref, above_ref,
    east_ref, west_ref, north_ref, basis_ref, smooth_ref, geo_ref, search_ref, applied_ref, res_ref,
    send_ref, known_ref, update_ref, operated_ref, rest_ref, full_ref,
):
    coarse = coarse_solve(got_ref, inverse_ref, left_ref, right_ref, below_ref, above_ref)
    curvature, projection = own_row_sums(got_ref, 2)
    lane = lane_ids(1)
    alpha = jnp.broadcast_to(projection, (1, LANES)) / jnp.broadcast_to(curvature, (1, LANES))
    known_ref[...] = jnp.broadcast_to(jnp.where(lane == 0, curvature, alpha), (8, LANES))

    def build(start, rows, band, carry):
        part, weight = load(smooth_ref, start, rows), load(basis_ref, start, rows)
        search = load(search_ref, start, rows)
        store(
            full_ref, start, rows,
            [search[b] - alpha * (part[b] + weight[b] * coarse[band][b]) for b in range(BLK)],
        )
        return 0

    for_bands(build, 0)
    ops = (east_ref, west_ref, north_ref, geo_ref.at[2])

    def step(i, carry):
        start = pl.multiple_of(HY + i * STEP, 8)
        own = pl.ds(pl.multiple_of(i * STEP, 8), STEP)
        here, out = operate(full_ref, *ops, start, STEP)
        search, applied, res = load(search_ref, start, STEP), load(applied_ref, start, STEP), load(res_ref, start, STEP)
        carry = list(carry)
        for b in range(AGG_LON):
            rest = res[b] - alpha * applied[b]
            update_ref[b, own, :] = here[b]
            operated_ref[b, own, :] = out[b]
            rest_ref[b, own, :] = rest
            pairs = ((here[b], applied[b]), (here[b], out[b]), (here[b], rest), (search[b], rest))
            carry = [acc + fold(x * y) for acc, (x, y) in zip(carry, pairs)]
        return tuple(carry)

    zero = jnp.zeros((8, LANES), F32)
    accs = lax.fori_loop(0, NY // STEP, step, (zero,) * 4)
    row = jnp.zeros((1, LANES), F32)
    for k, acc in enumerate(accs):
        row = jnp.where(lane == k, total(acc), row)
    fill_rows(send_ref, row)


def final_kernel(got_ref, known_ref, search_ref, applied_ref, update_ref, operated_ref, rest_ref, field_ref, out_ref):
    sums = jnp.sum(got_ref[...], axis=0, keepdims=True)
    lane = lane_ids(1)

    def pick(row, k):
        return jnp.broadcast_to(jnp.sum(jnp.where(lane == k, row, 0.0), axis=1, keepdims=True), (1, LANES))

    u_ap, u_au, u_r, p_r = [pick(sums, k) for k in range(4)]
    p_ap, alpha = pick(known_ref[0:1, :], 0), pick(known_ref[0:1, :], 1)
    beta = -u_ap / p_ap
    curvature = u_au + 2.0 * beta * u_ap + beta * beta * p_ap
    step_size = (u_r + beta * p_r) / curvature
    along = alpha + step_size * beta
    back = step_size * beta

    def step(i, carry):
        start = pl.multiple_of(i * STEP, 8)
        own, halo = pl.ds(start, STEP), pl.ds(pl.multiple_of(HY + i * STEP, 8), STEP)
        for b in range(AGG_LON):
            at = (own, pl.ds(b * LANES, LANES))
            field_ref[at] = along * search_ref[b, halo, :] + step_size * update_ref[b, own, :]
            out_ref[at] = rest_ref[b, own, :] - step_size * operated_ref[b, own, :] - back * applied_ref[b, halo, :]
        return carry

    lax.fori_loop(0, NY // STEP, step, 0)


def call(kernel, outs, scratch=(), scalars=0, ins=0, flops=0):
    specs = [pl.BlockSpec(memory_space=pltpu.SMEM)] * scalars + [pl.BlockSpec(memory_space=pltpu.VMEM)] * ins
    return pl.pallas_call(
        kernel,
        out_shape=[jax.ShapeDtypeStruct(s, F32) for s in outs],
        in_specs=specs,
        out_specs=[pl.BlockSpec(memory_space=pltpu.VMEM)] * len(outs),
        scratch_shapes=[pltpu.VMEM(s, F32) for s in scratch],
        compiler_params=pltpu.CompilerParams(vmem_limit_bytes=40 * 1024 * 1024),
        cost_estimate=pl.CostEstimate(flops=flops, bytes_accessed=4 * 1024 * 1024, transcendentals=0),
    )


def exchange(x):
    return lax.all_to_all(x, AXES, 0, 0, tiled=True)


def body(rhs, depth, mask, basis, inverse):
    n_lon, n_lat = lax.axis_size("lon"), lax.axis_size("lat")
    devices = n_lon * n_lat
    total_rows = NY * n_lat
    lat = lax.axis_index("lat")
    tile = (lax.axis_index("lon") * n_lat + lat).astype(jnp.int32).reshape(1)
    full = (BLK, ROWS, LANES)
    half = (AGG_LON, NY, LANES)
    rows8 = 8 * (inverse.shape[1] // LANES)
    own = (rhs, depth, mask, basis)

    row_index = lat * NY - HY + jnp.arange(ROWS, dtype=jnp.int32)
    latitude = (row_index.astype(F32) + 0.5) * (2.6 / total_rows) - 1.3
    inside = ((row_index >= 0) & (row_index <= total_rows - 2)).astype(F32)
    geo = jnp.stack(
        [1.0 / jnp.cos(latitude), jnp.cos(latitude + 1.3 / total_rows) * inside, SHIFT_SCALE * jnp.cos(latitude)]
    )
    geo = jnp.broadcast_to(geo[:, :, None], (3, ROWS, LANES))

    gather, to_west, to_east = call(
        pack_kernel, [(devices, LANES), (BAND + rows8, LANES), (BAND + rows8, LANES)], scalars=1, ins=5
    )(tile, *own, inverse)
    ring = [(i, (i + 1) % n_lon) for i in range(n_lon)]
    left = lax.ppermute(to_east, "lon", ring)
    right = lax.ppermute(to_west, "lon", [(j, i) for i, j in ring])
    got = exchange(gather)
    edge_rows = 3 * BLK * HY + rows8
    to_south, to_north = call(edge_kernel, [(edge_rows, LANES)] * 2, ins=7)(*own, inverse, left, right)
    line = [(i, i + 1) for i in range(n_lat - 1)]
    below = lax.ppermute(to_north, "lat", line)
    above = lax.ppermute(to_south, "lat", [(j, i) for i, j in line])

    east, west, north, inv, weight, res, smoothed = call(
        setup_kernel, [full] * 7, scratch=[full] * 4, ins=9, flops=40000000
    )(*own, left, right, below, above, geo)
    solver = (inverse, left, right, below, above)
    faces = (east, west, north, weight)
    send, search, applied = call(search_kernel, [(devices, LANES), full, full], scalars=1, ins=13, flops=8000000)(
        tile, got, *solver, *faces, smoothed, geo, res
    )
    got = exchange(send)
    (smoothed,) = call(second_kernel, [full], scratch=[full] * 3, ins=7, flops=20000000)(applied, inv, *faces, geo)
    send, known, *second = call(
        sums_kernel, [(devices, LANES), (8, LANES), half, half, half], scratch=[full], ins=15, flops=8000000
    )(got, *solver, *faces, smoothed, geo, search, applied, res)
    got = exchange(send)
    field, out = call(final_kernel, [(NY, NX)] * 2, ins=7, flops=1000000)(got, known, search, applied, *second)
    return field, out


def solution(mesh):
    tile = P("lat", "lon")
    return jax.shard_map(
        body,
        mesh=mesh,
        in_specs=(tile, tile, tile, tile, P(AXES, None)),
        out_specs=(tile, tile),
        check_vma=False,
    )
```

```python
import functools

import jax
import jax.numpy as jnp
from jax import lax
from jax.experimental import pallas as pl
from jax.experimental.pallas import tpu as pltpu
from jax.sharding import PartitionSpec as P

SWEEPS = 4
AGG_LAT = 4
AGG_LON = 2
LOW_EDGE = 0.1
HIGH_EDGE = 2.0
SHIFT_SCALE = 1.0e-5

NY = 512
NX = 256
HY = 16
WX = 9
ROWS = NY + 2 * HY
LANES = 128
BLK = 3
BAND = NY // AGG_LAT
STEP = 16
SWEEP = 24
SLOTS = LANES // 8
AXES = ("lon", "lat")
F32 = jnp.float32


def chebyshev_plan(sweep_total):
    interval_mid = (HIGH_EDGE + LOW_EDGE) / 2.0
    interval_half = (HIGH_EDGE - LOW_EDGE) / 2.0
    mid_ratio = interval_mid / interval_half
    previous = 1.0 / mid_ratio
    pairs = []
    for _ in range(sweep_total - 1):
        fresh = 1.0 / (2.0 * mid_ratio - previous)
        pairs.append((fresh * previous, 2.0 * fresh / interval_half))
        previous = fresh
    return 1.0 / interval_mid, pairs


def lane_ids(rows):
    return lax.broadcasted_iota(jnp.int32, (rows, LANES), 1)


def east_of(blocks):
    lane = lane_ids(blocks[0].shape[0])
    rolled = [pltpu.roll(v, LANES - 1, 1) for v in blocks]
    return [jnp.where(lane == LANES - 1, rolled[(b + 1) % BLK], rolled[b]) for b in range(BLK)]


def west_of(blocks):
    lane = lane_ids(blocks[0].shape[0])
    rolled = [pltpu.roll(v, 1, 1) for v in blocks]
    return [jnp.where(lane == 0, rolled[(b + BLK - 1) % BLK], rolled[b]) for b in range(BLK)]


def load(ref, start, rows):
    return [ref[b, pl.ds(start, rows), :] for b in range(BLK)]


def store(ref, start, rows, blocks):
    for b in range(BLK):
        ref[b, pl.ds(start, rows), :] = blocks[b]


def for_strips(fn):
    for start in range(8, ROWS - 8, SWEEP):
        fn(start, min(SWEEP, ROWS - 8 - start))


def for_own(fn):
    for start in range(0, NY, STEP):
        fn(start // BAND, start)


def clear_ends(ref):
    zero = jnp.zeros((8, LANES), F32)
    for b in range(BLK):
        ref[b, 0:8, :] = zero
        ref[b, ROWS - 8 : ROWS, :] = zero


def operate(v_ref, east_ref, west_ref, north_ref, shift_ref, start, rows):
    here = load(v_ref, start, rows)
    up, down = load(v_ref, start + 1, rows), load(v_ref, start - 1, rows)
    right, left = east_of(here), west_of(here)
    ef, wf = load(east_ref, start, rows), load(west_ref, start, rows)
    nf, sf = load(north_ref, start, rows), load(north_ref, start - 1, rows)
    shift = shift_ref[pl.ds(start, rows), :]
    out = [
        shift * here[b]
        + ef[b] * (here[b] - right[b])
        + wf[b] * (here[b] - left[b])
        + nf[b] * (here[b] - up[b])
        + sf[b] * (here[b] - down[b])
        for b in range(BLK)
    ]
    return here, out


def fold(x):
    return jnp.sum(x.reshape(-1, 8, LANES), axis=0)


def total(x):
    return jnp.sum(jnp.sum(x, axis=1, keepdims=True), axis=0, keepdims=True)


def own_row(tile_ref, values, scalars=()):
    lane = lane_ids(1)
    base = (tile_ref[0] % SLOTS) * 8
    other = ((tile_ref[0] + SLOTS // 2) % SLOTS) * 8
    row = jnp.zeros((1, LANES), F32)
    for k, value in enumerate(values):
        row = jnp.where(lane == base + k, value, row)
    for k, value in enumerate(scalars):
        row = jnp.where(lane == other + k, value, row)
    return row


def own_row_sums(got_ref, count):
    rows = got_ref.shape[0]
    lane = lane_ids(rows)
    slot = lax.broadcasted_iota(jnp.int32, (rows, LANES), 0) % SLOTS
    other = ((slot + SLOTS // 2) % SLOTS) * 8
    got = got_ref[...]
    return [total(fold(jnp.where(lane == other + k, got, 0.0))) for k in range(count)]


def fill_rows(ref, row):
    ref[...] = jnp.broadcast_to(row, ref.shape)


def pack_kernel(
    tile_ref, rhs_hbm, depth_hbm, mask_hbm, basis_hbm, inverse_hbm,
    gather_ref, west_ref, east_ref, wet_ref, res_ref, weight_ref,
    rhs_ref, depth_ref, mask_ref, basis_ref, inverse_ref, sems,
):
    pairs = ((rhs_hbm, rhs_ref), (mask_hbm, mask_ref), (basis_hbm, basis_ref), (depth_hbm, depth_ref))
    copies = []
    for g in range(AGG_LAT):
        at = pl.ds(g * BAND, BAND)
        copies.append(
            [pltpu.make_async_copy(src.at[at], dst.at[at], sems.at[4 * g + k]) for k, (src, dst) in enumerate(pairs)]
        )
    last = pltpu.make_async_copy(inverse_hbm, inverse_ref, sems.at[4 * AGG_LAT])
    for copy in sum(copies, []) + [last]:
        copy.start()
    groups = inverse_ref.shape[1] // LANES
    lane = lane_ids(STEP)
    sums = []
    zero = jnp.zeros((8, LANES), F32)
    for g in range(AGG_LAT):
        for copy in copies[g]:
            copy.wait()
        accs = [zero] * AGG_LON
        for start in range(g * BAND, (g + 1) * BAND, STEP):
            out_row = start - g * BAND
            fields = []
            for b in range(AGG_LON):
                at = (pl.ds(start, STEP), pl.ds(b * LANES, LANES))
                mask = mask_ref[at].astype(F32)
                wet = depth_ref[at] * mask
                res = rhs_ref[at] * mask
                weight = basis_ref[at] * mask
                accs[b] = accs[b] + fold(weight * res)
                fields.append((wet, res, weight))
                for ref, value in zip((wet_ref, res_ref, weight_ref), fields[b]):
                    ref[b, HY + start : HY + start + STEP, :] = value
            for ref, b, extra in ((west_ref, 0, 0), (east_ref, 1, WX)):
                packed = jnp.zeros((STEP, LANES), F32) if g == 0 else ref[out_row : out_row + STEP, :]
                for f in range(3):
                    lo = 32 * g + WX * f
                    moved = pltpu.roll(fields[b][f], (lo + extra) % LANES, 1)
                    packed = jnp.where((lane >= lo) & (lane < lo + WX), moved, packed)
                ref[out_row : out_row + STEP, :] = packed
        sums += [total(acc) for acc in accs]
    fill_rows(gather_ref, own_row(tile_ref, sums))
    last.wait()
    for g in range(groups):
        part = inverse_ref[:, g * LANES : (g + 1) * LANES]
        west_ref[BAND + 8 * g : BAND + 8 * g + 8, :] = part
        east_ref[BAND + 8 * g : BAND + 8 * g + 8, :] = part


def unpack_columns(left_ref, right_ref, g, start, rows):
    lane = lane_ids(rows)
    left, right = left_ref[pl.ds(start, rows), :], right_ref[pl.ds(start, rows), :]
    out = []
    for f in range(3):
        lo = 32 * g + WX * f
        from_right = pltpu.roll(right, (LANES - lo) % LANES, 1)
        from_left = pltpu.roll(left, (2 * LANES - lo - WX) % LANES, 1)
        out.append(jnp.where(lane < WX, from_right, jnp.where(lane >= LANES - WX, from_left, 0.0)))
    return out


def edge_kernel(wet_ref, res_ref, weight_ref, inverse_ref, left_ref, right_ref, south_ref, north_ref):
    groups = inverse_ref.shape[1] // LANES
    sub = lax.broadcasted_iota(jnp.int32, (8, LANES), 0)
    for ref, start, g, band in ((south_ref, 0, 0, 0), (north_ref, NY - HY, AGG_LAT - 1, AGG_LAT - 1)):
        halo = unpack_columns(left_ref, right_ref, g, start % BAND, HY)
        for f, field in enumerate((wet_ref, res_ref, weight_ref)):
            for b in range(BLK):
                at = (f * BLK + b) * HY
                ref[at : at + HY, :] = field[b, HY + start : 2 * HY + start, :] if b < 2 else halo[f]
        base = 3 * BLK * HY
        for i in range(groups):
            own = inverse_ref[:, i * LANES : (i + 1) * LANES]
            left = left_ref[BAND + 8 * i : BAND + 8 * i + 8, :]
            right = right_ref[BAND + 8 * i : BAND + 8 * i + 8, :]
            own = pltpu.roll(own, (8 - 2 * band) % 8, 0) if band else own
            left = pltpu.roll(left, (2 - 2 * band - 1 + 16) % 8, 0)
            right = pltpu.roll(right, (3 - 2 * band + 16) % 8, 0)
            picked = jnp.where(sub < 2, own, jnp.where(sub == 2, left, right))
            ref[base + 8 * i : base + 8 * i + 8, :] = picked


def smooth(res_ref, inv_ref, ops, est_refs, step_ref, finish):
    first, pairs = chebyshev_plan(SWEEPS)

    def start_strip(start, rows):
        inv, res = load(inv_ref, start, rows), load(res_ref, start, rows)
        value = [first * (inv[b] * res[b]) for b in range(BLK)]
        store(step_ref, start, rows, value)
        store(est_refs[0], start, rows, value)

    for_strips(start_strip)
    for k, (c1, c2) in enumerate(pairs):
        src, dst = est_refs[k % 2], est_refs[(k + 1) % 2]

        def strip(start, rows, src=src, dst=dst, c1=c1, c2=c2, last=k == len(pairs) - 1):
            here, applied = operate(src, *ops, start, rows)
            inv, res, step = load(inv_ref, start, rows), load(res_ref, start, rows), load(step_ref, start, rows)
            step = [c1 * step[b] + c2 * (inv[b] * (res[b] - applied[b])) for b in range(BLK)]
            value = [here[b] + step[b] for b in range(BLK)]
            if last:
                finish(start, rows, value)
            else:
                store(step_ref, start, rows, step)
                store(dst, start, rows, value)

        for_strips(strip)


def setup_kernel(
    wet_in, res_in, weight_in, left_ref, right_ref, below_ref, above_ref, geo_ref,
    wet_ref, res_ref, weight_ref, east_ref, west_ref, north_ref, inv_ref, smooth_ref,
    est_a, est_b, step_ref,
):
    outs = (wet_ref, res_ref, weight_ref)
    for f, ref in enumerate(outs):
        for b in range(BLK):
            at = (f * BLK + b) * HY
            ref[b, 0:HY, :] = below_ref[at : at + HY, :]
            ref[b, HY + NY : ROWS, :] = above_ref[at : at + HY, :]

    def fill(g, start):
        for f, value in enumerate(unpack_columns(left_ref, right_ref, g, start - g * BAND, STEP)):
            outs[f][2, HY + start : HY + start + STEP, :] = value

    for_own(fill)

    def east_west(start, rows):
        wet = load(wet_ref, start, rows)
        over = geo_ref[0, pl.ds(start, rows), :]
        nxt = east_of(wet)
        face = [jnp.minimum(wet[b], nxt[b]) * over for b in range(BLK)]
        store(east_ref, start, rows, face)
        store(west_ref, start, rows, west_of(face))

    def north(start, rows):
        wet, nxt = load(wet_ref, start, rows), load(wet_ref, start + 1, rows)
        cosine = geo_ref[1, pl.ds(start, rows), :]
        store(north_ref, start, rows, [jnp.minimum(wet[b], nxt[b]) * cosine for b in range(BLK)])

    for_strips(east_west)
    north(0, 8)
    for_strips(north)
    shift_ref = geo_ref.at[2]

    def diagonal(start, rows):
        ef, wf = load(east_ref, start, rows), load(west_ref, start, rows)
        nf, sf = load(north_ref, start, rows), load(north_ref, start - 1, rows)
        shift = shift_ref[pl.ds(start, rows), :]
        store(inv_ref, start, rows, [1.0 / (shift + ef[b] + wf[b] + nf[b] + sf[b]) for b in range(BLK)])

    for_strips(diagonal)
    for ref in (est_a, est_b, smooth_ref):
        clear_ends(ref)

    def finish(start, rows, value):
        wet = load(wet_ref, start, rows)
        store(smooth_ref, start, rows, [jnp.where(wet[b] > 0.0, value[b], 0.0) for b in range(BLK)])

    smooth(res_ref, inv_ref, (east_ref, west_ref, north_ref, shift_ref), (est_a, est_b), step_ref, finish)


def coarse_solve(got_ref, inverse_ref, left_ref, right_ref, below_ref, above_ref):
    groups = inverse_ref.shape[1] // LANES
    count = got_ref.shape[0] // groups
    base = 3 * BLK * HY
    accs = [jnp.zeros((8, LANES), F32) for _ in range(5)]
    mine = lane_ids(count) // 8 == lax.broadcasted_iota(jnp.int32, (count, LANES), 0)
    for i in range(groups):
        vec = jnp.sum(jnp.where(mine, got_ref[i * count : (i + 1) * count, :], 0.0), axis=0, keepdims=True)
        at = slice(BAND + 8 * i, BAND + 8 * i + 8)
        band = slice(base + 8 * i, base + 8 * i + 8)
        parts = (
            inverse_ref[:, i * LANES : (i + 1) * LANES],
            left_ref[at, :],
            right_ref[at, :],
            below_ref[band, :],
            above_ref[band, :],
        )
        accs = [acc + part * vec for acc, part in zip(accs, parts)]
    own, left, right, below, above = [jnp.sum(acc, axis=1, keepdims=True) for acc in accs]
    low = lane_ids(1) < LANES // 2

    def spread(value):
        return jnp.broadcast_to(value, (1, LANES))

    def edge(x):
        halo = jnp.where(low, spread(x[3:4]), spread(x[2:3]))
        return [spread(x[0:1]), spread(x[1:2]), halo]

    rows = [edge(below)]
    for a in range(AGG_LAT):
        halo = jnp.where(low, spread(right[2 * a : 2 * a + 1]), spread(left[2 * a + 1 : 2 * a + 2]))
        rows.append([spread(own[2 * a : 2 * a + 1]), spread(own[2 * a + 1 : 2 * a + 2]), halo])
    rows.append(edge(above))
    return rows


def for_bands(fn):
    fn(0, HY, 0)
    for_own(lambda a, start: fn(HY + start, STEP, a + 1))
    fn(HY + NY, HY, AGG_LAT + 1)


def search_kernel(
    tile_ref, got_ref, inverse_ref, left_ref, right_ref, below_ref, above_ref,
    east_ref, west_ref, north_ref, basis_ref, smooth_ref, geo_ref, res_ref,
    send_ref, search_ref, applied_ref,
):
    coarse = coarse_solve(got_ref, inverse_ref, left_ref, right_ref, below_ref, above_ref)

    def direction(start, rows, band):
        part, weight = load(smooth_ref, start, rows), load(basis_ref, start, rows)
        store(search_ref, start, rows, [part[b] + weight[b] * coarse[band][b] for b in range(BLK)])

    for_bands(direction)
    ops = (east_ref, west_ref, north_ref, geo_ref.at[2])
    clear_ends(applied_ref)

    def apply(start, rows):
        here, out = operate(search_ref, *ops, start, rows)
        store(applied_ref, start, rows, out)
        return here, out

    apply(HY - 8, 8)
    zero = jnp.zeros((8, LANES), F32)
    sums = [zero] * (AGG_LAT * AGG_LON + 2)

    def own(a, start):
        start = HY + start
        here, out = apply(start, STEP)
        for b in range(AGG_LON):
            k, weight = a * AGG_LON + b, basis_ref[b, start : start + STEP, :]
            sums[k] = sums[k] + fold(weight * out[b])
            sums[-2] = sums[-2] + fold(here[b] * out[b])
            sums[-1] = sums[-1] + fold(here[b] * res_ref[b, start : start + STEP, :])

    for_own(own)
    apply(HY + NY, 8)
    sums = [total(x) for x in sums]
    fill_rows(send_ref, own_row(tile_ref, sums[:-2], sums[-2:]))


def second_kernel(
    applied_ref, inv_ref, east_ref, west_ref, north_ref, basis_ref, geo_ref,
    out_ref, est_a, est_b, step_ref,
):
    for ref in (est_a, est_b, out_ref):
        clear_ends(ref)

    def finish(start, rows, value):
        weight = load(basis_ref, start, rows)
        store(out_ref, start, rows, [jnp.where(weight[b] > 0.0, value[b], 0.0) for b in range(BLK)])

    smooth(applied_ref, inv_ref, (east_ref, west_ref, north_ref, geo_ref.at[2]), (est_a, est_b), step_ref, finish)


def sums_kernel(
    got_ref, inverse_ref, left_ref, right_ref, below_ref, above_ref,
    east_ref, west_ref, north_ref, basis_ref, smooth_ref, geo_ref, search_ref, applied_ref, res_ref,
    send_ref, known_ref, update_ref, operated_ref, rest_ref, full_ref,
):
    coarse = coarse_solve(got_ref, inverse_ref, left_ref, right_ref, below_ref, above_ref)
    curvature, projection = own_row_sums(got_ref, 2)
    lane = lane_ids(1)
    alpha = jnp.broadcast_to(projection, (1, LANES)) / jnp.broadcast_to(curvature, (1, LANES))
    known_ref[...] = jnp.broadcast_to(jnp.where(lane == 0, curvature, alpha), (8, LANES))

    def build(start, rows, band):
        part, weight = load(smooth_ref, start, rows), load(basis_ref, start, rows)
        search = load(search_ref, start, rows)
        store(
            full_ref, start, rows,
            [search[b] - alpha * (part[b] + weight[b] * coarse[band][b]) for b in range(BLK)],
        )

    for_bands(build)
    ops = (east_ref, west_ref, north_ref, geo_ref.at[2])

    accs = [jnp.zeros((8, LANES), F32)] * 4

    def own(a, start):
        at, start = slice(start, start + STEP), HY + start
        here, out = operate(full_ref, *ops, start, STEP)
        search, applied, res = load(search_ref, start, STEP), load(applied_ref, start, STEP), load(res_ref, start, STEP)
        for b in range(AGG_LON):
            rest = res[b] - alpha * applied[b]
            update_ref[b, at, :] = here[b]
            operated_ref[b, at, :] = out[b]
            rest_ref[b, at, :] = rest
            pairs = ((here[b], applied[b]), (here[b], out[b]), (here[b], rest), (search[b], rest))
            for k, (x, y) in enumerate(pairs):
                accs[k] = accs[k] + fold(x * y)

    for_own(own)
    row = jnp.zeros((1, LANES), F32)
    for k, acc in enumerate(accs):
        row = jnp.where(lane == k, total(acc), row)
    fill_rows(send_ref, row)


def final_kernel(got_ref, known_ref, search_ref, applied_ref, update_ref, operated_ref, rest_ref, field_ref, out_ref):
    sums = jnp.sum(got_ref[...], axis=0, keepdims=True)
    lane = lane_ids(1)

    def pick(row, k):
        return jnp.broadcast_to(jnp.sum(jnp.where(lane == k, row, 0.0), axis=1, keepdims=True), (1, LANES))

    u_ap, u_au, u_r, p_r = [pick(sums, k) for k in range(4)]
    p_ap, alpha = pick(known_ref[0:1, :], 0), pick(known_ref[0:1, :], 1)
    beta = -u_ap / p_ap
    curvature = u_au + 2.0 * beta * u_ap + beta * beta * p_ap
    step_size = (u_r + beta * p_r) / curvature
    along = alpha + step_size * beta
    back = step_size * beta

    def own(a, start):
        at, halo = slice(start, start + STEP), slice(HY + start, HY + start + STEP)
        for b in range(AGG_LON):
            out = (at, slice(b * LANES, (b + 1) * LANES))
            field_ref[out] = along * search_ref[b, halo, :] + step_size * update_ref[b, at, :]
            out_ref[out] = rest_ref[b, at, :] - step_size * operated_ref[b, at, :] - back * applied_ref[b, halo, :]

    for_own(own)


def call(kernel, outs, scratch=(), scalars=0, hbm=0, ins=0, flops=0, grant=6, aliases=None):
    spaces = [pltpu.SMEM] * scalars + [pltpu.HBM] * hbm + [pltpu.VMEM] * ins
    return pl.pallas_call(
        kernel,
        out_shape=[jax.ShapeDtypeStruct(s, F32) for s in outs],
        in_specs=[pl.BlockSpec(memory_space=space) for space in spaces],
        out_specs=[pl.BlockSpec(memory_space=pltpu.VMEM)] * len(outs),
        scratch_shapes=[pltpu.VMEM(s, F32) if isinstance(s, tuple) else s for s in scratch],
        input_output_aliases=aliases or {},
        compiler_params=pltpu.CompilerParams(vmem_limit_bytes=grant * 1024 * 1024),
        cost_estimate=pl.CostEstimate(flops=flops, bytes_accessed=4 * 1024 * 1024, transcendentals=0),
    )


def exchange(x):
    return lax.all_to_all(x, AXES, 0, 0, tiled=True)


def body(rhs, depth, mask, basis, inverse):
    n_lon, n_lat = lax.axis_size("lon"), lax.axis_size("lat")
    devices = n_lon * n_lat
    total_rows = NY * n_lat
    lat = lax.axis_index("lat")
    tile = (lax.axis_index("lon") * n_lat + lat).astype(jnp.int32).reshape(1)
    full = (BLK, ROWS, LANES)
    half = (AGG_LON, NY, LANES)
    rows8 = 8 * (inverse.shape[1] // LANES)
    own = (rhs, depth, mask, basis)

    row_index = lat * NY - HY + jnp.arange(ROWS, dtype=jnp.int32)
    latitude = (row_index.astype(F32) + 0.5) * (2.6 / total_rows) - 1.3
    inside = ((row_index >= 0) & (row_index <= total_rows - 2)).astype(F32)
    geo = jnp.stack(
        [1.0 / jnp.cos(latitude), jnp.cos(latitude + 1.3 / total_rows) * inside, SHIFT_SCALE * jnp.cos(latitude)]
    )
    geo = jnp.broadcast_to(geo[:, :, None], (3, ROWS, LANES))

    loads = [(NY, NX), (NY, NX), pltpu.VMEM((NY, NX), jnp.int32), (NY, NX), inverse.shape]
    gather, to_west, to_east, *fields = call(
        pack_kernel,
        [(devices, LANES), (BAND + rows8, LANES), (BAND + rows8, LANES), full, full, full],
        scratch=[*loads, pltpu.SemaphoreType.DMA((4 * AGG_LAT + 1,))], scalars=1, hbm=5,
    )(tile, *own, inverse)
    ring = [(i, (i + 1) % n_lon) for i in range(n_lon)]
    left = lax.ppermute(to_east, "lon", ring)
    right = lax.ppermute(to_west, "lon", [(j, i) for i, j in ring])
    got = exchange(gather)
    edge_rows = 3 * BLK * HY + rows8
    to_south, to_north = call(edge_kernel, [(edge_rows, LANES)] * 2, ins=6)(*fields, inverse, left, right)
    line = [(i, i + 1) for i in range(n_lat - 1)]
    below = lax.ppermute(to_north, "lat", line)
    above = lax.ppermute(to_south, "lat", [(j, i) for i, j in line])

    _, res, weight, east, west, north, inv, smoothed = call(
        setup_kernel, [full] * 8, scratch=[full] * 3, ins=8, flops=40000000, aliases={0: 0, 1: 1, 2: 2}
    )(*fields, left, right, below, above, geo)
    solver = (inverse, left, right, below, above)
    faces = (east, west, north, weight)
    send, search, applied = call(search_kernel, [(devices, LANES), full, full], scalars=1, ins=13, flops=8000000)(
        tile, got, *solver, *faces, smoothed, geo, res
    )
    got = exchange(send)
    (smoothed,) = call(second_kernel, [full], scratch=[full] * 3, ins=7, flops=20000000)(applied, inv, *faces, geo)
    send, known, *second = call(
        sums_kernel, [(devices, LANES), (8, LANES), half, half, half], scratch=[full], ins=15, flops=8000000
    )(got, *solver, *faces, smoothed, geo, search, applied, res)
    got = exchange(send)
    field, out = call(final_kernel, [(NY, NX)] * 2, ins=7, flops=1000000)(got, known, search, applied, *second)
    return field, out


def solution(mesh):
    tile = P("lat", "lon")
    return jax.shard_map(
        body,
        mesh=mesh,
        in_specs=(tile, tile, tile, tile, P(AXES, None)),
        out_specs=(tile, tile),
        check_vma=False,
    )
```

```python
import functools

import jax
import jax.numpy as jnp
from jax import lax
from jax.experimental import pallas as pl
from jax.experimental.pallas import tpu as pltpu
from jax.sharding import PartitionSpec as P

SWEEPS = 4
AGG_LAT = 4
AGG_LON = 2
LOW_EDGE = 0.1
HIGH_EDGE = 2.0
SHIFT_SCALE = 1.0e-5

NY = 512
NX = 256
HY = 16
WX = 9
ROWS = NY + 2 * HY
LANES = 128
BLK = 3
BAND = NY // AGG_LAT
STEP = 16
SWEEP = 24
CHUNKS = ((0, 152), (152, 128), (280, 128), (408, 136))
SLOTS = LANES // 8
AXES = ("lon", "lat")
F32 = jnp.float32


def chebyshev_plan(sweep_total):
    interval_mid = (HIGH_EDGE + LOW_EDGE) / 2.0
    interval_half = (HIGH_EDGE - LOW_EDGE) / 2.0
    mid_ratio = interval_mid / interval_half
    previous = 1.0 / mid_ratio
    pairs = []
    for _ in range(sweep_total - 1):
        fresh = 1.0 / (2.0 * mid_ratio - previous)
        pairs.append((fresh * previous, 2.0 * fresh / interval_half))
        previous = fresh
    return 1.0 / interval_mid, pairs


def lane_ids(rows):
    return lax.broadcasted_iota(jnp.int32, (rows, LANES), 1)


def east_of(blocks):
    lane = lane_ids(blocks[0].shape[0])
    rolled = [pltpu.roll(v, LANES - 1, 1) for v in blocks]
    return [jnp.where(lane == LANES - 1, rolled[(b + 1) % BLK], rolled[b]) for b in range(BLK)]


def west_of(blocks):
    lane = lane_ids(blocks[0].shape[0])
    rolled = [pltpu.roll(v, 1, 1) for v in blocks]
    return [jnp.where(lane == 0, rolled[(b + BLK - 1) % BLK], rolled[b]) for b in range(BLK)]


def load(ref, start, rows):
    return [ref[b, pl.ds(start, rows), :] for b in range(BLK)]


def store(ref, start, rows, blocks):
    for b in range(BLK):
        ref[b, pl.ds(start, rows), :] = blocks[b]


def for_strips(fn):
    for start in range(8, ROWS - 8, SWEEP):
        fn(start, min(SWEEP, ROWS - 8 - start))


def for_own(fn):
    for start in range(0, NY, STEP):
        fn(start // BAND, start)


def clear_ends(ref):
    zero = jnp.zeros((8, LANES), F32)
    for b in range(BLK):
        ref[b, 0:8, :] = zero
        ref[b, ROWS - 8 : ROWS, :] = zero


def operate(v_ref, east_ref, west_ref, north_ref, shift_ref, start, rows):
    here = load(v_ref, start, rows)
    up, down = load(v_ref, start + 1, rows), load(v_ref, start - 1, rows)
    right, left = east_of(here), west_of(here)
    ef, wf = load(east_ref, start, rows), load(west_ref, start, rows)
    nf, sf = load(north_ref, start, rows), load(north_ref, start - 1, rows)
    shift = shift_ref[pl.ds(start, rows), :]
    out = [
        shift * here[b]
        + ef[b] * (here[b] - right[b])
        + wf[b] * (here[b] - left[b])
        + nf[b] * (here[b] - up[b])
        + sf[b] * (here[b] - down[b])
        for b in range(BLK)
    ]
    return here, out


def fold(x):
    return jnp.sum(x.reshape(-1, 8, LANES), axis=0)


def total(x):
    return jnp.sum(jnp.sum(x, axis=1, keepdims=True), axis=0, keepdims=True)


def own_row(tile_ref, values, scalars=()):
    lane = lane_ids(1)
    base = (tile_ref[0] % SLOTS) * 8
    other = ((tile_ref[0] + SLOTS // 2) % SLOTS) * 8
    row = jnp.zeros((1, LANES), F32)
    for k, value in enumerate(values):
        row = jnp.where(lane == base + k, value, row)
    for k, value in enumerate(scalars):
        row = jnp.where(lane == other + k, value, row)
    return row


def own_row_sums(got_ref, count):
    rows = got_ref.shape[0]
    lane = lane_ids(rows)
    slot = lax.broadcasted_iota(jnp.int32, (rows, LANES), 0) % SLOTS
    other = ((slot + SLOTS // 2) % SLOTS) * 8
    got = got_ref[...]
    return [total(fold(jnp.where(lane == other + k, got, 0.0))) for k in range(count)]


def fill_rows(ref, row):
    ref[...] = jnp.broadcast_to(row, ref.shape)


def pack_kernel(
    tile_ref, rhs_hbm, depth_hbm, mask_hbm, basis_hbm, inverse_hbm,
    gather_ref, west_ref, east_ref, edge_ref, wet_ref, res_ref, weight_ref,
    rhs_ref, depth_ref, mask_ref, basis_ref, inverse_ref, sems,
):
    pairs = ((rhs_hbm, rhs_ref), (mask_hbm, mask_ref), (basis_hbm, basis_ref), (depth_hbm, depth_ref))
    copies = []
    for g in range(AGG_LAT):
        at = pl.ds(g * BAND, BAND)
        copies.append(
            [pltpu.make_async_copy(src.at[at], dst.at[at], sems.at[4 * g + k]) for k, (src, dst) in enumerate(pairs)]
        )
    last = pltpu.make_async_copy(inverse_hbm, inverse_ref, sems.at[4 * AGG_LAT])
    for copy in sum(copies, []) + [last]:
        copy.start()
    groups = inverse_ref.shape[1] // LANES
    lane = lane_ids(STEP)
    sums = []
    zero = jnp.zeros((8, LANES), F32)
    for g in range(AGG_LAT):
        for copy in copies[g]:
            copy.wait()
        accs = [zero] * AGG_LON
        for start in range(g * BAND, (g + 1) * BAND, STEP):
            out_row = start - g * BAND
            fields = []
            for b in range(AGG_LON):
                at = (pl.ds(start, STEP), pl.ds(b * LANES, LANES))
                mask = mask_ref[at].astype(F32)
                wet = depth_ref[at] * mask
                res = rhs_ref[at] * mask
                weight = basis_ref[at] * mask
                accs[b] = accs[b] + fold(weight * res)
                fields.append((wet, res, weight))
                for f, (ref, value) in enumerate(zip((wet_ref, res_ref, weight_ref), fields[b])):
                    ref[b, start : start + STEP, :] = value
                    for side, first in ((0, 0), (1, NY - HY)):
                        if start == first:
                            edge_ref[side, f, b] = value
            for ref, b, extra in ((west_ref, 0, 0), (east_ref, 1, WX)):
                packed = jnp.zeros((STEP, LANES), F32) if g == 0 else ref[out_row : out_row + STEP, :]
                for f in range(3):
                    lo = 32 * g + WX * f
                    moved = pltpu.roll(fields[b][f], (lo + extra) % LANES, 1)
                    packed = jnp.where((lane >= lo) & (lane < lo + WX), moved, packed)
                ref[out_row : out_row + STEP, :] = packed
        sums += [total(acc) for acc in accs]
    fill_rows(gather_ref, own_row(tile_ref, sums))
    last.wait()
    for g in range(groups):
        part = inverse_ref[:, g * LANES : (g + 1) * LANES]
        west_ref[BAND + 8 * g : BAND + 8 * g + 8, :] = part
        east_ref[BAND + 8 * g : BAND + 8 * g + 8, :] = part


def unpack_columns(left_ref, right_ref, g, start, rows):
    lane = lane_ids(rows)
    left, right = left_ref[pl.ds(start, rows), :], right_ref[pl.ds(start, rows), :]
    out = []
    for f in range(3):
        lo = 32 * g + WX * f
        from_right = pltpu.roll(right, (LANES - lo) % LANES, 1)
        from_left = pltpu.roll(left, (2 * LANES - lo - WX) % LANES, 1)
        out.append(jnp.where(lane < WX, from_right, jnp.where(lane >= LANES - WX, from_left, 0.0)))
    return out


def edge_kernel(edge_ref, inverse_ref, left_ref, right_ref, south_ref, north_ref):
    groups = inverse_ref.shape[1] // LANES
    sub = lax.broadcasted_iota(jnp.int32, (8, LANES), 0)
    for side, (ref, start, band) in enumerate(((south_ref, 0, 0), (north_ref, BAND - HY, AGG_LAT - 1))):
        halo = unpack_columns(left_ref, right_ref, band, start, HY)
        for f in range(3):
            for b in range(BLK):
                at = (f * BLK + b) * HY
                ref[at : at + HY, :] = edge_ref[side, f, b] if b < 2 else halo[f]
        base = 3 * BLK * HY
        for i in range(groups):
            own = inverse_ref[:, i * LANES : (i + 1) * LANES]
            left = left_ref[BAND + 8 * i : BAND + 8 * i + 8, :]
            right = right_ref[BAND + 8 * i : BAND + 8 * i + 8, :]
            own = pltpu.roll(own, (8 - 2 * band) % 8, 0) if band else own
            left = pltpu.roll(left, (2 - 2 * band - 1 + 16) % 8, 0)
            right = pltpu.roll(right, (3 - 2 * band + 16) % 8, 0)
            picked = jnp.where(sub < 2, own, jnp.where(sub == 2, left, right))
            ref[base + 8 * i : base + 8 * i + 8, :] = picked


def west_of_faces(east_ref, west_ref, start, rows):
    store(west_ref, start, rows, west_of(load(east_ref, start, rows)))


def first_step(res_ref, inv_ref, faces, est_ref, step_ref, start, rows):
    east_ref, west_ref, north_ref, shift_ref = faces
    ef, wf = load(east_ref, start, rows), load(west_ref, start, rows)
    nf, sf = load(north_ref, start, rows), load(north_ref, start - 1, rows)
    shift = shift_ref[pl.ds(start, rows), :]
    inv = [1.0 / (shift + ef[b] + wf[b] + nf[b] + sf[b]) for b in range(BLK)]
    store(inv_ref, start, rows, inv)
    res = load(res_ref, start, rows)
    value = [chebyshev_plan(SWEEPS)[0] * (inv[b] * res[b]) for b in range(BLK)]
    store(step_ref, start, rows, value)
    store(est_ref, start, rows, value)


def smooth(res_ref, inv_ref, faces, est_refs, step_ref, finish):
    _, pairs = chebyshev_plan(SWEEPS)
    for k, (c1, c2) in enumerate(pairs):
        src, dst = est_refs[k % 2], est_refs[(k + 1) % 2]
        last = k == len(pairs) - 1

        def strip(start, rows, band=None):
            here, applied = operate(src, *faces, start, rows)
            inv, res, step = load(inv_ref, start, rows), load(res_ref, start, rows), load(step_ref, start, rows)
            step = [c1 * step[b] + c2 * (inv[b] * (res[b] - applied[b])) for b in range(BLK)]
            value = [here[b] + step[b] for b in range(BLK)]
            if last:
                finish(start, rows, band, value)
            else:
                store(step_ref, start, rows, step)
                store(dst, start, rows, value)

        if last:
            for_bands(strip)
        else:
            for_strips(strip)


def coarse_solve(got_ref, inverse_ref, left_ref, right_ref, below_ref, above_ref):
    groups = inverse_ref.shape[1] // LANES
    count = got_ref.shape[0] // groups
    base = 3 * BLK * HY
    accs = [jnp.zeros((8, LANES), F32) for _ in range(5)]
    mine = lane_ids(count) // 8 == lax.broadcasted_iota(jnp.int32, (count, LANES), 0)
    for i in range(groups):
        vec = jnp.sum(jnp.where(mine, got_ref[i * count : (i + 1) * count, :], 0.0), axis=0, keepdims=True)
        at = slice(BAND + 8 * i, BAND + 8 * i + 8)
        band = slice(base + 8 * i, base + 8 * i + 8)
        parts = (
            inverse_ref[:, i * LANES : (i + 1) * LANES],
            left_ref[at, :],
            right_ref[at, :],
            below_ref[band, :],
            above_ref[band, :],
        )
        accs = [acc + part * vec for acc, part in zip(accs, parts)]
    own, left, right, below, above = [jnp.sum(acc, axis=1, keepdims=True) for acc in accs]
    low = lane_ids(1) < LANES // 2

    def spread(value):
        return jnp.broadcast_to(value, (1, LANES))

    def edge(x):
        halo = jnp.where(low, spread(x[3:4]), spread(x[2:3]))
        return [spread(x[0:1]), spread(x[1:2]), halo]

    rows = [edge(below)]
    for a in range(AGG_LAT):
        halo = jnp.where(low, spread(right[2 * a : 2 * a + 1]), spread(left[2 * a + 1 : 2 * a + 2]))
        rows.append([spread(own[2 * a : 2 * a + 1]), spread(own[2 * a + 1 : 2 * a + 2]), halo])
    rows.append(edge(above))
    return rows


def for_bands(fn):
    fn(HY - 8, 8, 0)
    for_own(lambda a, start: fn(HY + start, STEP, a + 1))
    fn(HY + NY, 8, AGG_LAT + 1)


class Stream:
    def __init__(self, pairs, sems, first=0):
        self.chunks, self.done, self.rows = [], 0, 0
        for start, rows in CHUNKS:
            chunk = []
            for src, dst in pairs:
                lo, hi = start, start + rows
                if src.shape[1] == NY:
                    lo, hi = min(max(lo - HY, 0), NY), min(max(hi - HY, 0), NY)
                at = (slice(None), pl.ds(lo, hi - lo), slice(None))
                chunk.append(pltpu.make_async_copy(src.at[at], dst.at[at], sems.at[first]))
                first += 1
            for copy in chunk:
                copy.start()
            self.chunks.append(chunk)

    def need(self, row):
        while self.rows < min(row, ROWS):
            for copy in self.chunks[self.done]:
                copy.wait()
            self.rows = sum(CHUNKS[self.done])
            self.done += 1


def send_out(src, dst, sem):
    copy = pltpu.make_async_copy(src, dst, sem)
    copy.start()
    return copy


def search_kernel(
    tile_ref, got_ref, inverse_ref, left_ref, right_ref, below_ref, above_ref,
    wet_in, res_in, weight_in, geo_ref, shift_ref,
    send_ref, east_out, north_out, weight_out, search_out, applied_out,
    wet_ref, res_ref, weight_ref, east_ref, west_ref, north_ref, inv_ref,
    est_a, est_b, step_ref, search_ref, applied_ref, sems,
):
    fields = (wet_ref, res_ref, weight_ref)
    for f, (src, ref) in enumerate(zip((wet_in, res_in, weight_in), fields)):
        for b in range(BLK):
            at = (f * BLK + b) * HY
            ref[b, 0:HY, :] = below_ref[at : at + HY, :]
            ref[b, HY + NY : ROWS, :] = above_ref[at : at + HY, :]

    def fill(g, start):
        at = slice(HY + start, HY + start + STEP)
        halo = unpack_columns(left_ref, right_ref, g, start - g * BAND, STEP)
        for f, (src, ref) in enumerate(zip((wet_in, res_in, weight_in), fields)):
            for b in range(2):
                ref[b, at, :] = src[b, start : start + STEP, :]
            ref[2, at, :] = halo[f]

    for_own(fill)
    outs = [send_out(weight_ref, weight_out, sems.at[0])]

    def east_west(start, rows):
        wet = load(wet_ref, start, rows)
        over = geo_ref[0, pl.ds(start, rows), :]
        nxt = east_of(wet)
        face = [jnp.minimum(wet[b], nxt[b]) * over for b in range(BLK)]
        store(east_ref, start, rows, face)
        store(west_ref, start, rows, west_of(face))

    def north(start, rows):
        wet, nxt = load(wet_ref, start, rows), load(wet_ref, start + 1, rows)
        cosine = geo_ref[1, pl.ds(start, rows), :]
        store(north_ref, start, rows, [jnp.minimum(wet[b], nxt[b]) * cosine for b in range(BLK)])

    north(0, 8)
    for ref in (est_a, est_b, search_ref, applied_ref, east_ref):
        clear_ends(ref)
    for b in range(BLK):
        north_ref[b, ROWS - 8 : ROWS, :] = jnp.zeros((8, LANES), F32)
    faces = (east_ref, west_ref, north_ref, shift_ref)

    def prepare(start, rows):
        east_west(start, rows)
        north(start, rows)
        first_step(res_ref, inv_ref, faces, est_a, step_ref, start, rows)

    for_strips(prepare)
    outs += [send_out(east_ref, east_out, sems.at[1]), send_out(north_ref, north_out, sems.at[2])]
    coarse = coarse_solve(got_ref, inverse_ref, left_ref, right_ref, below_ref, above_ref)

    def finish(start, rows, band, value):
        wet, weight = load(wet_ref, start, rows), load(weight_ref, start, rows)
        part = [jnp.where(wet[b] > 0.0, value[b], 0.0) for b in range(BLK)]
        store(search_ref, start, rows, [part[b] + weight[b] * coarse[band][b] for b in range(BLK)])

    smooth(res_ref, inv_ref, faces, (est_a, est_b), step_ref, finish)
    outs.append(send_out(search_ref, search_out, sems.at[3]))
    sums = [jnp.zeros((8, LANES), F32)] * (AGG_LAT * AGG_LON + 2)

    def apply(start, rows, band):
        here, out = operate(search_ref, *faces, start, rows)
        store(applied_ref, start, rows, out)
        if 0 < band <= AGG_LAT:
            for b in range(AGG_LON):
                k, at = (band - 1) * AGG_LON + b, (b, slice(start, start + rows))
                sums[k] = sums[k] + fold(weight_ref[at] * out[b])
                sums[-2] = sums[-2] + fold(here[b] * out[b])
                sums[-1] = sums[-1] + fold(here[b] * res_ref[at])

    for_bands(apply)
    outs.append(send_out(applied_ref, applied_out, sems.at[4]))
    values = [total(x) for x in sums]
    fill_rows(send_ref, own_row(tile_ref, values[:-2], values[-2:]))
    for copy in outs:
        copy.wait()


def second_kernel(
    applied_hbm, east_hbm, north_hbm, weight_hbm, shift_ref,
    out_ref,
    applied_ref, east_ref, north_ref, weight_ref, west_ref, inv_ref, est_a, est_b, step_ref, sems,
):
    stream = Stream(
        ((applied_hbm, applied_ref), (east_hbm, east_ref), (north_hbm, north_ref), (weight_hbm, weight_ref)), sems
    )
    for ref in (est_a, est_b, out_ref):
        clear_ends(ref)
    faces = (east_ref, west_ref, north_ref, shift_ref)

    def prepare(start, rows):
        stream.need(start + rows)
        west_of_faces(east_ref, west_ref, start, rows)
        first_step(applied_ref, inv_ref, faces, est_a, step_ref, start, rows)

    for_strips(prepare)
    stream.need(ROWS)

    def finish(start, rows, band, value):
        weight = load(weight_ref, start, rows)
        store(out_ref, start, rows, [jnp.where(weight[b] > 0.0, value[b], 0.0) for b in range(BLK)])

    smooth(applied_ref, inv_ref, faces, (est_a, est_b), step_ref, finish)


def sums_kernel(
    got_ref, inverse_ref, left_ref, right_ref, below_ref, above_ref, smooth_ref, shift_ref,
    east_hbm, north_hbm, weight_hbm, search_hbm, applied_hbm, res_hbm,
    send_ref, known_ref, search_out, applied_out, update_ref, operated_ref, rest_ref,
    east_ref, north_ref, weight_ref, search_ref, applied_ref, res_ref, full_ref, sems,
):
    stream = Stream(
        (
            (weight_hbm, weight_ref), (search_hbm, search_ref), (east_hbm, east_ref),
            (north_hbm, north_ref), (applied_hbm, applied_ref), (res_hbm, res_ref),
        ),
        sems,
    )
    coarse = coarse_solve(got_ref, inverse_ref, left_ref, right_ref, below_ref, above_ref)
    curvature, projection = own_row_sums(got_ref, 2)
    lane = lane_ids(1)
    alpha = jnp.broadcast_to(projection, (1, LANES)) / jnp.broadcast_to(curvature, (1, LANES))
    known_ref[...] = jnp.broadcast_to(jnp.where(lane == 0, curvature, alpha), (8, LANES))

    def build(start, rows, band):
        stream.need(start + rows)
        part, weight, search = [load(ref, start, rows) for ref in (smooth_ref, weight_ref, search_ref)]
        store(
            full_ref, start, rows,
            [search[b] - alpha * (part[b] + weight[b] * coarse[band][b]) for b in range(BLK)],
        )

    accs = [jnp.zeros((8, LANES), F32)] * 4

    def apply(start):
        at, start = slice(start, start + STEP), HY + start
        here = load(full_ref, start, STEP)
        up, down = load(full_ref, start + 1, STEP), load(full_ref, start - 1, STEP)
        right, left = east_of(here), west_of(here)
        ef = load(east_ref, start, STEP)
        wf = west_of(ef)
        nf, sf = load(north_ref, start, STEP), load(north_ref, start - 1, STEP)
        shift = shift_ref[pl.ds(start, STEP), :]
        for b in range(AGG_LON):
            out = (
                shift * here[b]
                + ef[b] * (here[b] - right[b])
                + wf[b] * (here[b] - left[b])
                + nf[b] * (here[b] - up[b])
                + sf[b] * (here[b] - down[b])
            )
            search, applied = search_ref[b, start : start + STEP, :], applied_ref[b, start : start + STEP, :]
            rest = res_ref[b, at, :] - alpha * applied
            search_out[b, at, :] = search
            applied_out[b, at, :] = applied
            update_ref[b, at, :] = here[b]
            operated_ref[b, at, :] = out
            rest_ref[b, at, :] = rest
            pairs = ((here[b], applied), (here[b], out), (here[b], rest), (search, rest))
            for k, (x, y) in enumerate(pairs):
                accs[k] = accs[k] + fold(x * y)

    waiting = []

    def step(start, rows, band):
        build(start, rows, band)
        for ready in waiting:
            apply(ready)
        waiting.clear()
        if 0 < band <= AGG_LAT:
            waiting.append(start - HY)

    for_bands(step)
    stream.need(ROWS)
    row = jnp.zeros((1, LANES), F32)
    for k, acc in enumerate(accs):
        row = jnp.where(lane == k, total(acc), row)
    fill_rows(send_ref, row)


def final_kernel(
    got_ref, known_ref, search_ref, applied_ref, update_ref, operated_ref, rest_ref,
    field_out, residual_out, field_ref, residual_ref, sems,
):
    sums = jnp.sum(got_ref[...], axis=0, keepdims=True)
    lane = lane_ids(1)

    def pick(row, k):
        return jnp.broadcast_to(jnp.sum(jnp.where(lane == k, row, 0.0), axis=1, keepdims=True), (1, LANES))

    u_ap, u_au, u_r, p_r = [pick(sums, k) for k in range(4)]
    p_ap, alpha = pick(known_ref[0:1, :], 0), pick(known_ref[0:1, :], 1)
    beta = -u_ap / p_ap
    curvature = u_au + 2.0 * beta * u_ap + beta * beta * p_ap
    step_size = (u_r + beta * p_r) / curvature
    along = alpha + step_size * beta
    back = step_size * beta
    copies = []

    def own(a, start):
        at = slice(start, start + STEP)
        for b in range(AGG_LON):
            out = (at, slice(b * LANES, (b + 1) * LANES))
            field_ref[out] = along * search_ref[b, at, :] + step_size * update_ref[b, at, :]
            residual_ref[out] = rest_ref[b, at, :] - step_size * operated_ref[b, at, :] - back * applied_ref[b, at, :]
        if (start + STEP) % BAND == 0:
            rows = pl.ds(a * BAND, BAND)
            copies.append(send_out(field_ref.at[rows], field_out.at[rows], sems.at[2 * a]))
            copies.append(send_out(residual_ref.at[rows], residual_out.at[rows], sems.at[2 * a + 1]))

    for_own(own)
    for copy in copies:
        copy.wait()


def call(kernel, args, outs, scratch=(), hbm_outs=(), sems=0, flops=0, grant=6, scalars=0, hbm=()):
    def spec(i, inside):
        space = pltpu.SMEM if inside and i < scalars else pl.ANY if i in (hbm if inside else hbm_outs) else pltpu.VMEM
        return pl.BlockSpec(memory_space=space)

    return pl.pallas_call(
        kernel,
        out_shape=[jax.ShapeDtypeStruct(s, F32) for s in outs],
        in_specs=[spec(i, True) for i in range(len(args))],
        out_specs=[spec(i, False) for i in range(len(outs))],
        scratch_shapes=[pltpu.VMEM(s, F32) if isinstance(s, tuple) else s for s in scratch]
        + ([pltpu.SemaphoreType.DMA((sems,))] if sems else []),
        compiler_params=pltpu.CompilerParams(vmem_limit_bytes=grant * 1024 * 1024),
        cost_estimate=pl.CostEstimate(flops=flops, bytes_accessed=4 * 1024 * 1024, transcendentals=0),
    )(*args)


def exchange(x):
    return lax.all_to_all(x, AXES, 0, 0, tiled=True)


def body(rhs, depth, mask, basis, inverse):
    n_lon, n_lat = lax.axis_size("lon"), lax.axis_size("lat")
    devices = n_lon * n_lat
    total_rows = NY * n_lat
    lat = lax.axis_index("lat")
    tile = (lax.axis_index("lon") * n_lat + lat).astype(jnp.int32).reshape(1)
    full = (BLK, ROWS, LANES)
    half = (AGG_LON, NY, LANES)
    rows8 = 8 * (inverse.shape[1] // LANES)
    row = (devices, LANES)

    row_index = lat * NY - HY + jnp.arange(ROWS, dtype=jnp.int32)
    latitude = (row_index.astype(F32) + 0.5) * (2.6 / total_rows) - 1.3
    inside = ((row_index >= 0) & (row_index <= total_rows - 2)).astype(F32)
    geo = jnp.stack([1.0 / jnp.cos(latitude), jnp.cos(latitude + 1.3 / total_rows) * inside])
    geo = jnp.broadcast_to(geo[:, :, None], (2, ROWS, LANES))
    shift = jnp.broadcast_to((SHIFT_SCALE * jnp.cos(latitude))[:, None], (ROWS, LANES))

    loads = [(NY, NX), (NY, NX), pltpu.VMEM((NY, NX), jnp.int32), (NY, NX), inverse.shape]
    pack = (BAND + rows8, LANES)
    gather, to_west, to_east, edges, *fields = call(
        pack_kernel, [tile, rhs, depth, mask, basis, inverse], [row, pack, pack, (2, 3, 2, HY, LANES), half, half, half],
        scratch=loads, sems=4 * AGG_LAT + 1, scalars=1, hbm=range(1, 6), grant=60,
    )
    ring = [(i, (i + 1) % n_lon) for i in range(n_lon)]
    left = lax.ppermute(to_east, "lon", ring)
    right = lax.ppermute(to_west, "lon", [(j, i) for i, j in ring])
    got = exchange(gather)
    edge = (3 * BLK * HY + rows8, LANES)
    to_south, to_north = call(edge_kernel, [edges, inverse, left, right], [edge, edge], grant=4)
    line = [(i, i + 1) for i in range(n_lat - 1)]
    below = lax.ppermute(to_north, "lat", line)
    above = lax.ppermute(to_south, "lat", [(j, i) for i, j in line])
    solver = (inverse, left, right, below, above)

    send, east, north, weight, search, applied = call(
        search_kernel, [tile, got, *solver, *fields, geo, shift], [row] + [full] * 5, hbm_outs=range(1, 6),
        scratch=[full] * 12, sems=5, scalars=1, flops=40000000, grant=59,
    )
    got = exchange(send)
    (smoothed,) = call(
        second_kernel, [applied, east, north, weight, shift], [full], hbm=range(4),
        scratch=[full] * 9, sems=4 * len(CHUNKS), flops=20000000, grant=60,
    )
    send, known, *state = call(
        sums_kernel,
        [got, *solver, smoothed, shift, east, north, weight, search, applied, fields[1]],
        [row, (8, LANES)] + [half] * 5, hbm=range(8, 14),
        scratch=[full] * 5 + [half, full], sems=6 * len(CHUNKS), flops=8000000, grant=58,
    )
    got = exchange(send)
    field, out = call(
        final_kernel, [got, known, *state], [(NY, NX)] * 2, hbm_outs=range(2), scratch=[(NY, NX)] * 2,
        sems=2 * AGG_LAT, flops=1000000, grant=4,
    )
    return field, out


def solution(mesh):
    tile = P("lat", "lon")
    return jax.shard_map(
        body,
        mesh=mesh,
        in_specs=(tile, tile, tile, tile, P(AXES, None)),
        out_specs=(tile, tile),
        check_vma=False,
    )
```

```python
import functools
import math

import jax
import jax.numpy as jnp
from jax import lax
from jax.experimental import pallas as pl
from jax.experimental.pallas import tpu as pltpu
from jax.sharding import PartitionSpec as P

SWEEPS = 4
AGG_LAT = 4
AGG_LON = 2
LOW_EDGE = 0.1
HIGH_EDGE = 2.0
SHIFT_SCALE = 1.0e-5

NY = 512
NX = 256
HY = 16
WX = 9
ROWS = NY + 2 * HY
LANES = 128
BLK = 3
BAND = NY // AGG_LAT
STEP = 16
SWEEP = 24
CHUNKS = ((0, 152), (152, 128), (280, 128), (408, 136))
SLOTS = LANES // 8
AXES = ("lon", "lat")
F32 = jnp.float32


def chebyshev_plan(sweep_total):
    interval_mid = (HIGH_EDGE + LOW_EDGE) / 2.0
    interval_half = (HIGH_EDGE - LOW_EDGE) / 2.0
    mid_ratio = interval_mid / interval_half
    previous = 1.0 / mid_ratio
    pairs = []
    for _ in range(sweep_total - 1):
        fresh = 1.0 / (2.0 * mid_ratio - previous)
        pairs.append((fresh * previous, 2.0 * fresh / interval_half))
        previous = fresh
    return 1.0 / interval_mid, pairs


def cosine(x):
    square = x * x
    out = jnp.full_like(x, -1.0 / math.factorial(14))
    for k in range(6, -1, -1):
        out = out * square + (-1.0) ** k / math.factorial(2 * k)
    return out


def place():
    lat = lax.axis_index("lat")
    return lax.axis_index("lon") * lax.axis_size("lat") + lat, lat * NY


def latitudes(spot, total_rows, start, rows):
    index = spot[1] - HY + start + lax.broadcasted_iota(jnp.int32, (rows, LANES), 0)
    inside = (index >= 0) & (index <= total_rows - 2)
    return (index.astype(F32) + 0.5) * (2.6 / total_rows) - 1.3, inside


def lane_ids(rows):
    return lax.broadcasted_iota(jnp.int32, (rows, LANES), 1)


def east_of(blocks):
    lane = lane_ids(blocks[0].shape[0])
    rolled = [pltpu.roll(v, LANES - 1, 1) for v in blocks]
    return [jnp.where(lane == LANES - 1, rolled[(b + 1) % BLK], rolled[b]) for b in range(BLK)]


def west_of(blocks):
    lane = lane_ids(blocks[0].shape[0])
    rolled = [pltpu.roll(v, 1, 1) for v in blocks]
    return [jnp.where(lane == 0, rolled[(b + BLK - 1) % BLK], rolled[b]) for b in range(BLK)]


def load(ref, start, rows):
    return [ref[b, pl.ds(start, rows), :] for b in range(BLK)]


def store(ref, start, rows, blocks):
    for b in range(BLK):
        ref[b, pl.ds(start, rows), :] = blocks[b]


def for_strips(fn):
    for start in range(8, ROWS - 8, SWEEP):
        fn(start, min(SWEEP, ROWS - 8 - start))


def for_own(fn):
    for start in range(0, NY, STEP):
        fn(start // BAND, start)


def clear_ends(ref):
    zero = jnp.zeros((8, LANES), F32)
    for b in range(BLK):
        ref[b, 0:8, :] = zero
        ref[b, ROWS - 8 : ROWS, :] = zero


def operate(v_ref, east_ref, west_ref, north_ref, shift_ref, start, rows):
    here = load(v_ref, start, rows)
    up, down = load(v_ref, start + 1, rows), load(v_ref, start - 1, rows)
    right, left = east_of(here), west_of(here)
    ef, wf = load(east_ref, start, rows), load(west_ref, start, rows)
    nf, sf = load(north_ref, start, rows), load(north_ref, start - 1, rows)
    shift = shift_ref[pl.ds(start, rows), :]
    out = [
        shift * here[b]
        + ef[b] * (here[b] - right[b])
        + wf[b] * (here[b] - left[b])
        + nf[b] * (here[b] - up[b])
        + sf[b] * (here[b] - down[b])
        for b in range(BLK)
    ]
    return here, out


def fold(x):
    return jnp.sum(x.reshape(-1, 8, LANES), axis=0)


def total(x):
    return jnp.sum(jnp.sum(x, axis=1, keepdims=True), axis=0, keepdims=True)


def own_row(spot, values, scalars=()):
    lane = lane_ids(1)
    base = (spot[0] % SLOTS) * 8
    other = ((spot[0] + SLOTS // 2) % SLOTS) * 8
    row = jnp.zeros((1, LANES), F32)
    for k, value in enumerate(values):
        row = jnp.where(lane == base + k, value, row)
    for k, value in enumerate(scalars):
        row = jnp.where(lane == other + k, value, row)
    return row


def own_row_sums(got_ref, count):
    rows = got_ref.shape[0]
    lane = lane_ids(rows)
    slot = lax.broadcasted_iota(jnp.int32, (rows, LANES), 0) % SLOTS
    other = ((slot + SLOTS // 2) % SLOTS) * 8
    got = got_ref[...]
    return [total(fold(jnp.where(lane == other + k, got, 0.0))) for k in range(count)]


def fill_rows(ref, row):
    ref[...] = jnp.broadcast_to(row, ref.shape)


def pack_kernel(
    rhs_hbm, depth_hbm, mask_hbm, basis_hbm, inverse_hbm,
    gather_ref, west_ref, east_ref, edge_ref, fields_out,
    rhs_ref, depth_ref, mask_ref, basis_ref, inverse_ref, fields_ref, sems,
):
    spot = place()
    pairs = ((rhs_hbm, rhs_ref), (mask_hbm, mask_ref), (basis_hbm, basis_ref), (depth_hbm, depth_ref))
    copies = []
    for g in range(AGG_LAT):
        at = pl.ds(g * BAND, BAND)
        copies.append(
            [pltpu.make_async_copy(src.at[at], dst.at[at], sems.at[4 * g + k]) for k, (src, dst) in enumerate(pairs)]
        )
    last = pltpu.make_async_copy(inverse_hbm, inverse_ref, sems.at[4 * AGG_LAT])
    for copy in sum(copies, []) + [last]:
        copy.start()
    groups = inverse_ref.shape[1] // LANES
    lane = lane_ids(STEP)
    sums, outs = [], []
    zero = jnp.zeros((8, LANES), F32)
    for g in range(AGG_LAT):
        for copy in copies[g]:
            copy.wait()
        accs = [zero] * AGG_LON
        for start in range(g * BAND, (g + 1) * BAND, STEP):
            out_row = start - g * BAND
            fields = []
            for b in range(AGG_LON):
                at = (pl.ds(start, STEP), pl.ds(b * LANES, LANES))
                mask = mask_ref[at].astype(F32)
                wet = depth_ref[at] * mask
                res = rhs_ref[at] * mask
                weight = basis_ref[at] * mask
                accs[b] = accs[b] + fold(weight * res)
                fields.append((wet, res, weight))
                for f, value in enumerate(fields[b]):
                    fields_ref[f, b, start : start + STEP, :] = value
                    for side, first in ((0, 0), (1, NY - HY)):
                        if start == first:
                            edge_ref[side, f, b] = value
            for ref, b, extra in ((west_ref, 0, 0), (east_ref, 1, WX)):
                packed = jnp.zeros((STEP, LANES), F32) if g == 0 else ref[out_row : out_row + STEP, :]
                for f in range(3):
                    lo = 32 * g + WX * f
                    moved = pltpu.roll(fields[b][f], (lo + extra) % LANES, 1)
                    packed = jnp.where((lane >= lo) & (lane < lo + WX), moved, packed)
                ref[out_row : out_row + STEP, :] = packed
        sums += [total(acc) for acc in accs]
        rows = (slice(None), slice(None), pl.ds(g * BAND, BAND))
        outs.append(send_out(fields_ref.at[rows], fields_out.at[rows], sems.at[4 * AGG_LAT + 1 + g]))
    fill_rows(gather_ref, own_row(spot, sums))
    last.wait()
    for g in range(groups):
        part = inverse_ref[:, g * LANES : (g + 1) * LANES]
        west_ref[BAND + 8 * g : BAND + 8 * g + 8, :] = part
        east_ref[BAND + 8 * g : BAND + 8 * g + 8, :] = part
    for copy in outs:
        copy.wait()


def unpack_columns(left_ref, right_ref, g, start, rows):
    lane = lane_ids(rows)
    left, right = left_ref[pl.ds(start, rows), :], right_ref[pl.ds(start, rows), :]
    out = []
    for f in range(3):
        lo = 32 * g + WX * f
        from_right = pltpu.roll(right, (LANES - lo) % LANES, 1)
        from_left = pltpu.roll(left, (2 * LANES - lo - WX) % LANES, 1)
        out.append(jnp.where(lane < WX, from_right, jnp.where(lane >= LANES - WX, from_left, 0.0)))
    return out


def edge_kernel(edge_hbm, pack_hbm, left_ref, right_ref, south_ref, north_ref, solver_ref, edge_ref, pack_ref, sems):
    for copy in fetch(((edge_hbm, edge_ref), (pack_hbm, pack_ref)), sems, 0):
        copy.wait()
    rows8 = pack_ref.shape[0] - BAND
    for k, ref in enumerate((pack_ref, left_ref, right_ref)):
        solver_ref[k * rows8 : (k + 1) * rows8, :] = ref[BAND:, :]
    groups = (pack_ref.shape[0] - BAND) // 8
    sub = lax.broadcasted_iota(jnp.int32, (8, LANES), 0)
    for side, (ref, start, band) in enumerate(((south_ref, 0, 0), (north_ref, BAND - HY, AGG_LAT - 1))):
        halo = unpack_columns(left_ref, right_ref, band, start, HY)
        for f in range(3):
            for b in range(BLK):
                at = (f * BLK + b) * HY
                ref[at : at + HY, :] = edge_ref[side, f, b] if b < 2 else halo[f]
        base = 3 * BLK * HY
        for i in range(groups):
            at = slice(BAND + 8 * i, BAND + 8 * i + 8)
            own, left, right = pack_ref[at, :], left_ref[at, :], right_ref[at, :]
            own = pltpu.roll(own, (8 - 2 * band) % 8, 0) if band else own
            left = pltpu.roll(left, (2 - 2 * band - 1 + 16) % 8, 0)
            right = pltpu.roll(right, (3 - 2 * band + 16) % 8, 0)
            picked = jnp.where(sub < 2, own, jnp.where(sub == 2, left, right))
            ref[base + 8 * i : base + 8 * i + 8, :] = picked


def north_faces(spot, total_rows, wet_ref, north_ref, start, rows):
    wet, nxt = load(wet_ref, start, rows), load(wet_ref, start + 1, rows)
    latitude, inside = latitudes(spot, total_rows, start, rows)
    cos_row = jnp.where(inside, cosine(latitude + 1.3 / total_rows), 0.0)
    store(north_ref, start, rows, [jnp.minimum(wet[b], nxt[b]) * cos_row for b in range(BLK)])


def all_faces(spot, total_rows, wet_ref, faces, start, rows):
    east_ref, west_ref, north_ref, shift_ref = faces
    wet = load(wet_ref, start, rows)
    cos_row = cosine(latitudes(spot, total_rows, start, rows)[0])
    shift_ref[pl.ds(start, rows), :] = SHIFT_SCALE * cos_row
    over = 1.0 / cos_row
    nxt = east_of(wet)
    face = [jnp.minimum(wet[b], nxt[b]) * over for b in range(BLK)]
    store(east_ref, start, rows, face)
    store(west_ref, start, rows, west_of(face))
    north_faces(spot, total_rows, wet_ref, north_ref, start, rows)


def first_step(res_ref, inv_ref, faces, est_ref, step_ref, start, rows):
    east_ref, west_ref, north_ref, shift_ref = faces
    ef, wf = load(east_ref, start, rows), load(west_ref, start, rows)
    nf, sf = load(north_ref, start, rows), load(north_ref, start - 1, rows)
    shift = shift_ref[pl.ds(start, rows), :]
    inv = [1.0 / (shift + ef[b] + wf[b] + nf[b] + sf[b]) for b in range(BLK)]
    store(inv_ref, start, rows, inv)
    res = load(res_ref, start, rows)
    value = [chebyshev_plan(SWEEPS)[0] * (inv[b] * res[b]) for b in range(BLK)]
    store(step_ref, start, rows, value)
    store(est_ref, start, rows, value)


def smooth(res_ref, inv_ref, faces, est_refs, step_ref, finish):
    _, pairs = chebyshev_plan(SWEEPS)
    for k, (c1, c2) in enumerate(pairs):
        src, dst = est_refs[k % 2], est_refs[(k + 1) % 2]
        last = k == len(pairs) - 1

        def strip(start, rows, band=None):
            here, applied = operate(src, *faces, start, rows)
            inv, res, step = load(inv_ref, start, rows), load(res_ref, start, rows), load(step_ref, start, rows)
            step = [c1 * step[b] + c2 * (inv[b] * (res[b] - applied[b])) for b in range(BLK)]
            value = [here[b] + step[b] for b in range(BLK)]
            if last:
                finish(start, rows, band, value)
            else:
                store(step_ref, start, rows, step)
                store(dst, start, rows, value)

        if last:
            for_bands(strip)
        else:
            for_strips(strip)


def fetch(pairs, sems, first):
    return [send_out(src, dst, sems.at[first + k]) for k, (src, dst) in enumerate(pairs)]


def coarse_solve(got_ref, parts):
    groups = got_ref.shape[0] // SLOTS
    accs = [jnp.zeros((8, LANES), F32) for _ in parts]
    mine = lane_ids(SLOTS) // 8 == lax.broadcasted_iota(jnp.int32, (SLOTS, LANES), 0)
    for i in range(groups):
        vec = jnp.sum(jnp.where(mine, got_ref[i * SLOTS : (i + 1) * SLOTS, :], 0.0), axis=0, keepdims=True)
        for k, (ref, first) in enumerate(parts):
            accs[k] = accs[k] + ref[first + 8 * i : first + 8 * i + 8, :] * vec
    own, left, right, below, above = [jnp.sum(acc, axis=1, keepdims=True) for acc in accs]
    low = lane_ids(1) < LANES // 2

    def spread(value):
        return jnp.broadcast_to(value, (1, LANES))

    def edge(x):
        halo = jnp.where(low, spread(x[3:4]), spread(x[2:3]))
        return [spread(x[0:1]), spread(x[1:2]), halo]

    rows = [edge(below)]
    for a in range(AGG_LAT):
        halo = jnp.where(low, spread(right[2 * a : 2 * a + 1]), spread(left[2 * a + 1 : 2 * a + 2]))
        rows.append([spread(own[2 * a : 2 * a + 1]), spread(own[2 * a + 1 : 2 * a + 2]), halo])
    rows.append(edge(above))
    return rows


def for_bands(fn):
    fn(HY - 8, 8, 0)
    for_own(lambda a, start: fn(HY + start, STEP, a + 1))
    fn(HY + NY, 8, AGG_LAT + 1)


class Stream:
    def __init__(self, src, refs, sems):
        self.chunks, self.done, self.rows = [], 0, 0
        for k, (start, rows) in enumerate(CHUNKS):
            chunk = []
            for i, dst in enumerate(refs):
                if dst.shape[0] == BLK:
                    lo, hi, shift = start, start + rows, 0
                else:
                    lo, hi, shift = max(start, HY), min(start + rows, HY + NY), HY
                chunk.append(
                    pltpu.make_async_copy(
                        src.at[i, 0 : dst.shape[0], lo:hi, :],
                        dst.at[:, lo - shift : hi - shift, :],
                        sems.at[k * len(refs) + i],
                    )
                )
            for copy in chunk:
                copy.start()
            self.chunks.append(chunk)

    def need(self, row):
        while self.rows < min(row, ROWS):
            for copy in self.chunks[self.done]:
                copy.wait()
            self.rows = sum(CHUNKS[self.done])
            self.done += 1


def send_out(src, dst, sem):
    copy = pltpu.make_async_copy(src, dst, sem)
    copy.start()
    return copy


def search_kernel(
    total_rows,
    got_ref, solver_ref, left_ref, right_ref, below_ref, above_ref, fields_hbm,
    send_ref, wet_ref, applied_ref, carry_out,
    fields_ref, east_ref, north_ref, res_ref, weight_ref, west_ref, inv_ref, est_a, est_b, step_ref, search_ref, shift_ref, sems,
):
    spot = place()
    fields = (wet_ref, res_ref, weight_ref)
    bands = [(slice(None), slice(None), pl.ds(a * BAND, BAND)) for a in range(AGG_LAT)]
    copies = [send_out(fields_hbm.at[at], fields_ref.at[at], sems.at[5 + a]) for a, at in enumerate(bands)]
    for f, ref in enumerate(fields):
        for b in range(BLK):
            at = (f * BLK + b) * HY
            ref[b, 0:HY, :] = below_ref[at : at + HY, :]
            ref[b, HY + NY : ROWS, :] = above_ref[at : at + HY, :]

    def fill(g, start):
        if start % BAND == 0:
            copies[g].wait()
        at = slice(HY + start, HY + start + STEP)
        halo = unpack_columns(left_ref, right_ref, g, start - g * BAND, STEP)
        for f, ref in enumerate(fields):
            for b in range(2):
                ref[b, at, :] = fields_ref[f, b, start : start + STEP, :]
            ref[2, at, :] = halo[f]

    for_own(fill)
    own_rows = (slice(0, AGG_LON), slice(HY, HY + NY))
    outs = [
        send_out(weight_ref, carry_out.at[0], sems.at[0]),
        send_out(res_ref.at[own_rows], carry_out.at[5].at[own_rows], sems.at[3]),
    ]
    base, rows8 = 3 * BLK * HY, solver_ref.shape[0] // 3
    outs += [
        send_out(solver_ref, carry_out.at[6, 0, 0 : 3 * rows8], sems.at[10]),
        send_out(below_ref.at[base : base + rows8], carry_out.at[6, 1, 0:rows8], sems.at[11]),
        send_out(above_ref.at[base : base + rows8], carry_out.at[6, 2, 0:rows8], sems.at[12]),
    ]

    north_faces(spot, total_rows, wet_ref, north_ref, 0, 8)
    for ref in (est_a, est_b, search_ref, applied_ref, east_ref):
        clear_ends(ref)
    for b in range(BLK):
        north_ref[b, ROWS - 8 : ROWS, :] = jnp.zeros((8, LANES), F32)
    faces = (east_ref, west_ref, north_ref, shift_ref)

    def prepare(start, rows):
        all_faces(spot, total_rows, wet_ref, faces, start, rows)
        first_step(res_ref, inv_ref, faces, est_a, step_ref, start, rows)

    for_strips(prepare)
    outs += [send_out(east_ref, carry_out.at[2], sems.at[4]), send_out(north_ref, carry_out.at[3], sems.at[9])]
    parts = [(solver_ref, k * rows8) for k in range(3)] + [(below_ref, base), (above_ref, base)]
    coarse = coarse_solve(got_ref, parts)

    def finish(start, rows, band, value):
        wet, weight = load(wet_ref, start, rows), load(weight_ref, start, rows)
        part = [jnp.where(wet[b] > 0.0, value[b], 0.0) for b in range(BLK)]
        store(search_ref, start, rows, [part[b] + weight[b] * coarse[band][b] for b in range(BLK)])

    smooth(res_ref, inv_ref, faces, (est_a, est_b), step_ref, finish)
    outs.append(send_out(search_ref, carry_out.at[1], sems.at[1]))
    sums = [jnp.zeros((8, LANES), F32)] * (AGG_LAT * AGG_LON + 2)

    def apply(start, rows, band):
        here, out = operate(search_ref, *faces, start, rows)
        store(applied_ref, start, rows, out)
        if 0 < band <= AGG_LAT:
            for b in range(AGG_LON):
                k, at = (band - 1) * AGG_LON + b, (b, slice(start, start + rows))
                sums[k] = sums[k] + fold(weight_ref[at] * out[b])
                sums[-2] = sums[-2] + fold(here[b] * out[b])
                sums[-1] = sums[-1] + fold(here[b] * res_ref[at])

    for_bands(apply)
    outs.append(send_out(applied_ref.at[own_rows], carry_out.at[4].at[own_rows], sems.at[2]))
    values = [total(x) for x in sums]
    fill_rows(send_ref, own_row(spot, values[:-2], values[-2:]))
    for copy in outs:
        copy.wait()


def second_kernel(
    total_rows,
    applied_ref, wet_ref,
    out_ref,
    east_ref, north_ref, west_ref, inv_ref, est_a, est_b, step_ref, shift_ref,
):
    spot = place()
    north_faces(spot, total_rows, wet_ref, north_ref, 0, 8)
    for ref in (est_a, est_b):
        clear_ends(ref)
    faces = (east_ref, west_ref, north_ref, shift_ref)

    def prepare(start, rows):
        all_faces(spot, total_rows, wet_ref, faces, start, rows)
        first_step(applied_ref, inv_ref, faces, est_a, step_ref, start, rows)

    for_strips(prepare)

    def finish(start, rows, band, value):
        store(out_ref, start, rows, value)

    smooth(applied_ref, inv_ref, faces, (est_a, est_b), step_ref, finish)


def sums_kernel(
    total_rows,
    got_ref, smooth_ref, carry_hbm,
    send_ref, known_ref, search_out, applied_ref, update_ref, operated_ref, rest_ref,
    solver_ref, weight_ref, search_ref, east_ref, north_ref, res_ref, full_ref, sems,
):
    spot = place()
    rows8 = solver_ref.shape[0] // 5
    pairs = [(carry_hbm.at[6, 0, 0 : 3 * rows8], solver_ref.at[0 : 3 * rows8])]
    for k in (1, 2):
        pairs.append((carry_hbm.at[6, k, 0:rows8], solver_ref.at[(k + 2) * rows8 : (k + 3) * rows8]))
    solver = fetch(pairs, sems, 6 * len(CHUNKS))
    stream = Stream(carry_hbm, (weight_ref, search_ref, east_ref, north_ref, applied_ref, res_ref), sems)
    for copy in solver:
        copy.wait()
    coarse = coarse_solve(got_ref, [(solver_ref, k * rows8) for k in range(5)])
    curvature, projection = own_row_sums(got_ref, 2)
    lane = lane_ids(1)
    alpha = jnp.broadcast_to(projection, (1, LANES)) / jnp.broadcast_to(curvature, (1, LANES))
    known_ref[...] = jnp.broadcast_to(jnp.where(lane == 0, curvature, alpha), (8, LANES))

    def build(start, rows, band):
        stream.need(start + rows)
        part, weight, search = [load(ref, start, rows) for ref in (smooth_ref, weight_ref, search_ref)]
        store(
            full_ref, start, rows,
            [
                search[b] - alpha * (jnp.where(weight[b] > 0.0, part[b], 0.0) + weight[b] * coarse[band][b])
                for b in range(BLK)
            ],
        )

    accs = [jnp.zeros((8, LANES), F32)] * 4

    def apply(start):
        at, start = slice(start, start + STEP), HY + start
        here = load(full_ref, start, STEP)
        up, down = load(full_ref, start + 1, STEP), load(full_ref, start - 1, STEP)
        right, left = east_of(here), west_of(here)
        ef = load(east_ref, start, STEP)
        wf = west_of(ef)
        nf, sf = load(north_ref, start, STEP), load(north_ref, start - 1, STEP)
        shift = SHIFT_SCALE * cosine(latitudes(spot, total_rows, start, STEP)[0])
        for b in range(AGG_LON):
            out = (
                shift * here[b]
                + ef[b] * (here[b] - right[b])
                + wf[b] * (here[b] - left[b])
                + nf[b] * (here[b] - up[b])
                + sf[b] * (here[b] - down[b])
            )
            search, applied = search_ref[b, start : start + STEP, :], applied_ref[b, at, :]
            rest = res_ref[b, at, :] - alpha * applied
            search_out[b, at, :] = search
            update_ref[b, at, :] = here[b]
            operated_ref[b, at, :] = out
            rest_ref[b, at, :] = rest
            pairs = ((here[b], applied), (here[b], out), (here[b], rest), (search, rest))
            for k, (x, y) in enumerate(pairs):
                accs[k] = accs[k] + fold(x * y)

    waiting = []

    def step(start, rows, band):
        build(start, rows, band)
        for ready in waiting:
            apply(ready)
        waiting.clear()
        if 0 < band <= AGG_LAT:
            waiting.append(start - HY)

    for_bands(step)
    stream.need(ROWS)
    row = jnp.zeros((1, LANES), F32)
    for k, acc in enumerate(accs):
        row = jnp.where(lane == k, total(acc), row)
    fill_rows(send_ref, row)


def final_kernel(
    got_ref, known_ref, search_ref, applied_ref, update_ref, operated_ref, rest_ref,
    field_out, residual_out, field_ref, residual_ref, sems,
):
    sums = jnp.sum(got_ref[...], axis=0, keepdims=True)
    lane = lane_ids(1)

    def pick(row, k):
        return jnp.broadcast_to(jnp.sum(jnp.where(lane == k, row, 0.0), axis=1, keepdims=True), (1, LANES))

    u_ap, u_au, u_r, p_r = [pick(sums, k) for k in range(4)]
    p_ap, alpha = pick(known_ref[0:1, :], 0), pick(known_ref[0:1, :], 1)
    beta = -u_ap / p_ap
    curvature = u_au + 2.0 * beta * u_ap + beta * beta * p_ap
    step_size = (u_r + beta * p_r) / curvature
    along = alpha + step_size * beta
    back = step_size * beta
    copies = []

    def own(a, start):
        at = slice(start, start + STEP)
        for b in range(AGG_LON):
            out = (at, slice(b * LANES, (b + 1) * LANES))
            field_ref[out] = along * search_ref[b, at, :] + step_size * update_ref[b, at, :]
            residual_ref[out] = rest_ref[b, at, :] - step_size * operated_ref[b, at, :] - back * applied_ref[b, at, :]
        if (start + STEP) % BAND == 0:
            rows = pl.ds(a * BAND, BAND)
            copies.append(send_out(field_ref.at[rows], field_out.at[rows], sems.at[2 * a]))
            copies.append(send_out(residual_ref.at[rows], residual_out.at[rows], sems.at[2 * a + 1]))

    for_own(own)
    for copy in copies:
        copy.wait()


def call(kernel, args, outs, scratch=(), hbm_outs=(), sems=0, flops=0, grant=6, hbm=()):
    def spec(i, inside):
        return pl.BlockSpec(memory_space=pl.ANY if i in (hbm if inside else hbm_outs) else pltpu.VMEM)

    return pl.pallas_call(
        kernel,
        out_shape=[jax.ShapeDtypeStruct(s, F32) for s in outs],
        in_specs=[spec(i, True) for i in range(len(args))],
        out_specs=[spec(i, False) for i in range(len(outs))],
        scratch_shapes=[pltpu.VMEM(s, F32) if isinstance(s, tuple) else s for s in scratch]
        + ([pltpu.SemaphoreType.DMA((sems,))] if sems else []),
        compiler_params=pltpu.CompilerParams(vmem_limit_bytes=int(grant * 1024 * 1024)),
        cost_estimate=pl.CostEstimate(flops=flops, bytes_accessed=4 * 1024 * 1024, transcendentals=0),
    )(*args)


def exchange(x):
    return lax.all_to_all(x, AXES, 0, 0, tiled=True)


def body(rhs, depth, mask, basis, inverse):
    n_lon, n_lat = lax.axis_size("lon"), lax.axis_size("lat")
    devices = n_lon * n_lat
    total_rows = NY * n_lat
    full = (BLK, ROWS, LANES)
    half = (AGG_LON, NY, LANES)
    rows8 = 8 * (inverse.shape[1] // LANES)
    row = (devices, LANES)

    loads = [(NY, NX), (NY, NX), pltpu.VMEM((NY, NX), jnp.int32), (NY, NX), inverse.shape]
    pack = (BAND + rows8, LANES)
    gather, to_west, to_east, edges, fields = call(
        pack_kernel, [rhs, depth, mask, basis, inverse], [row, pack, pack, (2, 3, 2, HY, LANES), (3, *half)], hbm_outs=(4,),
        scratch=[*loads, (3, *half)], sems=5 * AGG_LAT + 1, hbm=range(5), grant=56,
    )
    ring = [(i, (i + 1) % n_lon) for i in range(n_lon)]
    left = lax.ppermute(to_east, "lon", ring)
    right = lax.ppermute(to_west, "lon", [(j, i) for i, j in ring])
    got = exchange(gather)
    edge = (3 * BLK * HY + rows8, LANES)
    to_south, to_north, solver = call(
        edge_kernel, [edges, to_west, left, right], [edge, edge, (3 * rows8, LANES)], hbm=range(2),
        scratch=[edges.shape, pack], sems=2, grant=4,
    )
    line = [(i, i + 1) for i in range(n_lat - 1)]
    below = lax.ppermute(to_north, "lat", line)
    above = lax.ppermute(to_south, "lat", [(j, i) for i, j in line])

    send, wet, applied, carry = call(
        functools.partial(search_kernel, total_rows), [got, solver, left, right, below, above, fields],
        [row] + [full] * 2 + [(7, *full)], hbm=(6,), hbm_outs=(3,),
        scratch=[(3, *half)] + [full] * 10 + [full[1:]], sems=9 + AGG_LAT, flops=40000000, grant=50.5,
    )
    got = exchange(send)
    (smoothed,) = call(
        functools.partial(second_kernel, total_rows), [applied, wet], [full],
        scratch=[full] * 7 + [full[1:]], flops=20000000, grant=12,
    )
    send, known, *state = call(
        functools.partial(sums_kernel, total_rows), [got, smoothed, carry],
        [row, (8, LANES)] + [half] * 5, hbm=(2,),
        scratch=[(5 * rows8, LANES), full, full, full, full, half, full], sems=6 * len(CHUNKS) + 3, flops=8000000, grant=49,
    )
    got = exchange(send)
    field, out = call(
        final_kernel, [got, known, *state], [(NY, NX)] * 2, hbm_outs=range(2), scratch=[(NY, NX)] * 2,
        sems=2 * AGG_LAT, flops=1000000, grant=4,
    )
    return field, out


def solution(mesh):
    tile = P("lat", "lon")
    return jax.shard_map(
        body,
        mesh=mesh,
        in_specs=(tile, tile, tile, tile, P(AXES, None)),
        out_specs=(tile, tile),
        check_vma=False,
    )
```

```python
import functools
import math

import jax
import jax.numpy as jnp
from jax import lax
from jax.experimental import pallas as pl
from jax.experimental.pallas import tpu as pltpu
from jax.sharding import PartitionSpec as P

SWEEPS = 4
AGG_LAT = 4
AGG_LON = 2
LOW_EDGE = 0.1
HIGH_EDGE = 2.0
SHIFT_SCALE = 1.0e-5

NY = 512
NX = 256
HY = 16
WX = 9
ROWS = NY + 2 * HY
LANES = 128
BLK = 3
BAND = NY // AGG_LAT
STEP = 16
SWEEP = 24
CHUNKS = ((0, 152), (152, 128), (280, 128), (408, 136))
SLOTS = LANES // 8
AXES = ("lon", "lat")
F32 = jnp.float32


def chebyshev_plan(sweep_total):
    interval_mid = (HIGH_EDGE + LOW_EDGE) / 2.0
    interval_half = (HIGH_EDGE - LOW_EDGE) / 2.0
    mid_ratio = interval_mid / interval_half
    previous = 1.0 / mid_ratio
    pairs = []
    for _ in range(sweep_total - 1):
        fresh = 1.0 / (2.0 * mid_ratio - previous)
        pairs.append((fresh * previous, 2.0 * fresh / interval_half))
        previous = fresh
    return 1.0 / interval_mid, pairs


def cosine(x):
    square = x * x
    out = jnp.full_like(x, -1.0 / math.factorial(14))
    for k in range(6, -1, -1):
        out = out * square + (-1.0) ** k / math.factorial(2 * k)
    return out


def place():
    lat = lax.axis_index("lat")
    return lax.axis_index("lon") * lax.axis_size("lat") + lat, lat * NY


def latitudes(spot, total_rows, start, rows):
    index = spot[1] - HY + start + lax.broadcasted_iota(jnp.int32, (rows, LANES), 0)
    inside = (index >= 0) & (index <= total_rows - 2)
    return (index.astype(F32) + 0.5) * (2.6 / total_rows) - 1.3, inside


def lane_ids(rows):
    return lax.broadcasted_iota(jnp.int32, (rows, LANES), 1)


def east_of(blocks):
    lane = lane_ids(blocks[0].shape[0])
    rolled = [pltpu.roll(v, LANES - 1, 1) for v in blocks]
    return [jnp.where(lane == LANES - 1, rolled[(b + 1) % BLK], rolled[b]) for b in range(BLK)]


def west_of(blocks):
    lane = lane_ids(blocks[0].shape[0])
    rolled = [pltpu.roll(v, 1, 1) for v in blocks]
    return [jnp.where(lane == 0, rolled[(b + BLK - 1) % BLK], rolled[b]) for b in range(BLK)]


def load(ref, start, rows):
    return [ref[b, pl.ds(start, rows), :] for b in range(BLK)]


def store(ref, start, rows, blocks):
    for b in range(BLK):
        ref[b, pl.ds(start, rows), :] = blocks[b]


def for_strips(fn):
    for start in range(8, ROWS - 8, SWEEP):
        fn(start, min(SWEEP, ROWS - 8 - start))


def for_own(fn):
    for start in range(0, NY, STEP):
        fn(start // BAND, start)


def clear_ends(ref):
    zero = jnp.zeros((8, LANES), F32)
    for b in range(BLK):
        ref[b, 0:8, :] = zero
        ref[b, ROWS - 8 : ROWS, :] = zero


def operate(v_ref, east_ref, west_ref, north_ref, shift_ref, start, rows):
    here = load(v_ref, start, rows)
    up, down = load(v_ref, start + 1, rows), load(v_ref, start - 1, rows)
    right, left = east_of(here), west_of(here)
    ef, wf = load(east_ref, start, rows), load(west_ref, start, rows)
    nf, sf = load(north_ref, start, rows), load(north_ref, start - 1, rows)
    shift = shift_ref[pl.ds(start, rows), :]
    out = [
        shift * here[b]
        + ef[b] * (here[b] - right[b])
        + wf[b] * (here[b] - left[b])
        + nf[b] * (here[b] - up[b])
        + sf[b] * (here[b] - down[b])
        for b in range(BLK)
    ]
    return here, out


def fold(x):
    return jnp.sum(x.reshape(-1, 8, LANES), axis=0)


def total(x):
    return jnp.sum(jnp.sum(x, axis=1, keepdims=True), axis=0, keepdims=True)


def own_row(spot, values, scalars=()):
    lane = lane_ids(1)
    base = (spot[0] % SLOTS) * 8
    other = ((spot[0] + SLOTS // 2) % SLOTS) * 8
    row = jnp.zeros((1, LANES), F32)
    for k, value in enumerate(values):
        row = jnp.where(lane == base + k, value, row)
    for k, value in enumerate(scalars):
        row = jnp.where(lane == other + k, value, row)
    return row


def own_row_sums(got_ref, count):
    rows = got_ref.shape[0]
    lane = lane_ids(rows)
    slot = lax.broadcasted_iota(jnp.int32, (rows, LANES), 0) % SLOTS
    other = ((slot + SLOTS // 2) % SLOTS) * 8
    got = got_ref[...]
    return [total(fold(jnp.where(lane == other + k, got, 0.0))) for k in range(count)]


def fill_rows(ref, row):
    ref[...] = jnp.broadcast_to(row, ref.shape)


def pack_kernel(
    rhs_hbm, depth_hbm, mask_hbm, basis_hbm, inverse_hbm,
    gather_ref, west_ref, east_ref, fields_out,
    rhs_ref, depth_ref, mask_ref, basis_ref, inverse_ref, edge_ref, fields_ref, sems,
):
    spot = place()
    pairs = ((rhs_hbm, rhs_ref), (mask_hbm, mask_ref), (basis_hbm, basis_ref), (depth_hbm, depth_ref))
    copies = []
    for g in range(AGG_LAT):
        at = pl.ds(g * BAND, BAND)
        copies.append(
            [pltpu.make_async_copy(src.at[at], dst.at[at], sems.at[4 * g + k]) for k, (src, dst) in enumerate(pairs)]
        )
    last = pltpu.make_async_copy(inverse_hbm, inverse_ref, sems.at[4 * AGG_LAT])
    for copy in sum(copies, []) + [last]:
        copy.start()
    groups = inverse_ref.shape[1] // LANES
    lane = lane_ids(STEP)
    sums, outs = [], []
    zero = jnp.zeros((8, LANES), F32)
    for g in range(AGG_LAT):
        for copy in copies[g]:
            copy.wait()
        accs = [zero] * AGG_LON
        for start in range(g * BAND, (g + 1) * BAND, STEP):
            out_row = start - g * BAND
            fields = []
            for b in range(AGG_LON):
                at = (pl.ds(start, STEP), pl.ds(b * LANES, LANES))
                mask = mask_ref[at].astype(F32)
                wet = depth_ref[at] * mask
                res = rhs_ref[at] * mask
                weight = basis_ref[at] * mask
                accs[b] = accs[b] + fold(weight * res)
                fields.append((wet, res, weight))
                for f, value in enumerate(fields[b]):
                    fields_ref[f, b, start : start + STEP, :] = value
                    for side, first in ((0, 0), (1, NY - HY)):
                        if start == first:
                            at = ((side * 3 + f) * 2 + b) * HY
                            edge_ref[at : at + HY, :] = value
            for ref, b, extra in ((west_ref, 0, 0), (east_ref, 1, WX)):
                packed = jnp.zeros((STEP, LANES), F32) if g == 0 else ref[out_row : out_row + STEP, :]
                for f in range(3):
                    lo = 32 * g + WX * f
                    moved = pltpu.roll(fields[b][f], (lo + extra) % LANES, 1)
                    packed = jnp.where((lane >= lo) & (lane < lo + WX), moved, packed)
                ref[out_row : out_row + STEP, :] = packed
        sums += [total(acc) for acc in accs]
        rows = (slice(None), slice(None), pl.ds(g * BAND, BAND))
        outs.append(send_out(fields_ref.at[rows], fields_out.at[0:3].at[rows], sems.at[4 * AGG_LAT + 1 + g]))
    fill_rows(gather_ref, own_row(spot, sums))
    last.wait()
    for g in range(groups):
        part = inverse_ref[:, g * LANES : (g + 1) * LANES]
        west_ref[BAND + 8 * g : BAND + 8 * g + 8, :] = part
        east_ref[BAND + 8 * g : BAND + 8 * g + 8, :] = part
    outs.append(send_out(edge_ref, fields_out.at[3, 0, 0 : edge_ref.shape[0]], sems.at[5 * AGG_LAT + 1]))
    outs.append(send_out(west_ref.at[BAND:], fields_out.at[3, 1, 0 : 8 * groups], sems.at[5 * AGG_LAT + 2]))
    for copy in outs:
        copy.wait()


def unpack_columns(left_ref, right_ref, g, start, rows):
    lane = lane_ids(rows)
    left, right = left_ref[pl.ds(start, rows), :], right_ref[pl.ds(start, rows), :]
    out = []
    for f in range(3):
        lo = 32 * g + WX * f
        from_right = pltpu.roll(right, (LANES - lo) % LANES, 1)
        from_left = pltpu.roll(left, (2 * LANES - lo - WX) % LANES, 1)
        out.append(jnp.where(lane < WX, from_right, jnp.where(lane >= LANES - WX, from_left, 0.0)))
    return out


def edge_kernel(fields_hbm, left_ref, right_ref, south_ref, north_ref, solver_ref, edge_ref, own_ref, sems):
    rows8 = own_ref.shape[0]
    groups = rows8 // 8
    pairs = ((fields_hbm.at[3, 0, 0 : edge_ref.shape[0]], edge_ref), (fields_hbm.at[3, 1, 0:rows8], own_ref))
    copies = fetch(pairs, sems, 0)
    for k, ref in ((1, left_ref), (2, right_ref)):
        solver_ref[k * rows8 : (k + 1) * rows8, :] = ref[BAND:, :]
    for copy in copies:
        copy.wait()
    solver_ref[0:rows8, :] = own_ref[...]
    sub = lax.broadcasted_iota(jnp.int32, (8, LANES), 0)
    for side, (ref, start, band) in enumerate(((south_ref, 0, 0), (north_ref, BAND - HY, AGG_LAT - 1))):
        halo = unpack_columns(left_ref, right_ref, band, start, HY)
        for f in range(3):
            for b in range(BLK):
                at = (f * BLK + b) * HY
                row = ((side * 3 + f) * 2 + b) * HY
                ref[at : at + HY, :] = edge_ref[row : row + HY, :] if b < 2 else halo[f]
        base = 3 * BLK * HY
        for i in range(groups):
            at = slice(BAND + 8 * i, BAND + 8 * i + 8)
            own, left, right = own_ref[8 * i : 8 * i + 8, :], left_ref[at, :], right_ref[at, :]
            own = pltpu.roll(own, (8 - 2 * band) % 8, 0) if band else own
            left = pltpu.roll(left, (2 - 2 * band - 1 + 16) % 8, 0)
            right = pltpu.roll(right, (3 - 2 * band + 16) % 8, 0)
            picked = jnp.where(sub < 2, own, jnp.where(sub == 2, left, right))
            ref[base + 8 * i : base + 8 * i + 8, :] = picked


def north_faces(spot, total_rows, wet_ref, north_ref, start, rows):
    wet, nxt = load(wet_ref, start, rows), load(wet_ref, start + 1, rows)
    latitude, inside = latitudes(spot, total_rows, start, rows)
    cos_row = jnp.where(inside, cosine(latitude + 1.3 / total_rows), 0.0)
    store(north_ref, start, rows, [jnp.minimum(wet[b], nxt[b]) * cos_row for b in range(BLK)])


def all_faces(spot, total_rows, wet_ref, faces, start, rows):
    east_ref, west_ref, north_ref, shift_ref = faces
    wet = load(wet_ref, start, rows)
    cos_row = cosine(latitudes(spot, total_rows, start, rows)[0])
    shift_ref[pl.ds(start, rows), :] = SHIFT_SCALE * cos_row
    over = 1.0 / cos_row
    nxt = east_of(wet)
    face = [jnp.minimum(wet[b], nxt[b]) * over for b in range(BLK)]
    store(east_ref, start, rows, face)
    store(west_ref, start, rows, west_of(face))
    north_faces(spot, total_rows, wet_ref, north_ref, start, rows)


def first_step(res_ref, inv_ref, faces, est_ref, step_ref, start, rows):
    east_ref, west_ref, north_ref, shift_ref = faces
    ef, wf = load(east_ref, start, rows), load(west_ref, start, rows)
    nf, sf = load(north_ref, start, rows), load(north_ref, start - 1, rows)
    shift = shift_ref[pl.ds(start, rows), :]
    inv = [1.0 / (shift + ef[b] + wf[b] + nf[b] + sf[b]) for b in range(BLK)]
    store(inv_ref, start, rows, inv)
    res = load(res_ref, start, rows)
    value = [chebyshev_plan(SWEEPS)[0] * (inv[b] * res[b]) for b in range(BLK)]
    store(step_ref, start, rows, value)
    store(est_ref, start, rows, value)


def smooth(res_ref, inv_ref, faces, est_refs, step_ref, finish):
    _, pairs = chebyshev_plan(SWEEPS)
    for k, (c1, c2) in enumerate(pairs):
        src, dst = est_refs[k % 2], est_refs[(k + 1) % 2]
        last = k == len(pairs) - 1

        def strip(start, rows, band=None):
            here, applied = operate(src, *faces, start, rows)
            inv, res, step = load(inv_ref, start, rows), load(res_ref, start, rows), load(step_ref, start, rows)
            step = [c1 * step[b] + c2 * (inv[b] * (res[b] - applied[b])) for b in range(BLK)]
            value = [here[b] + step[b] for b in range(BLK)]
            if last:
                finish(start, rows, band, value)
            else:
                store(step_ref, start, rows, step)
                store(dst, start, rows, value)

        if last:
            for_bands(strip)
        else:
            for_strips(strip)


def fetch(pairs, sems, first):
    return [send_out(src, dst, sems.at[first + k]) for k, (src, dst) in enumerate(pairs)]


def coarse_solve(got_ref, parts):
    groups = got_ref.shape[0] // SLOTS
    accs = [jnp.zeros((8, LANES), F32) for _ in parts]
    mine = lane_ids(SLOTS) // 8 == lax.broadcasted_iota(jnp.int32, (SLOTS, LANES), 0)
    for i in range(groups):
        vec = jnp.sum(jnp.where(mine, got_ref[i * SLOTS : (i + 1) * SLOTS, :], 0.0), axis=0, keepdims=True)
        for k, (ref, first) in enumerate(parts):
            accs[k] = accs[k] + ref[first + 8 * i : first + 8 * i + 8, :] * vec
    own, left, right, below, above = [jnp.sum(acc, axis=1, keepdims=True) for acc in accs]
    low = lane_ids(1) < LANES // 2

    def spread(value):
        return jnp.broadcast_to(value, (1, LANES))

    def edge(x):
        halo = jnp.where(low, spread(x[3:4]), spread(x[2:3]))
        return [spread(x[0:1]), spread(x[1:2]), halo]

    rows = [edge(below)]
    for a in range(AGG_LAT):
        halo = jnp.where(low, spread(right[2 * a : 2 * a + 1]), spread(left[2 * a + 1 : 2 * a + 2]))
        rows.append([spread(own[2 * a : 2 * a + 1]), spread(own[2 * a + 1 : 2 * a + 2]), halo])
    rows.append(edge(above))
    return rows


def for_bands(fn):
    fn(HY - 8, 8, 0)
    for_own(lambda a, start: fn(HY + start, STEP, a + 1))
    fn(HY + NY, 8, AGG_LAT + 1)


class Stream:
    def __init__(self, src, refs, sems):
        self.chunks, self.done, self.rows = [], 0, 0
        for k, (start, rows) in enumerate(CHUNKS):
            chunk = []
            for i, dst in enumerate(refs):
                if dst.shape[0] == BLK:
                    lo, hi, shift = start, start + rows, 0
                else:
                    lo, hi, shift = max(start, HY), min(start + rows, HY + NY), HY
                chunk.append(
                    pltpu.make_async_copy(
                        src.at[i, 0 : dst.shape[0], lo:hi, :],
                        dst.at[:, lo - shift : hi - shift, :],
                        sems.at[k * len(refs) + i],
                    )
                )
            for copy in chunk:
                copy.start()
            self.chunks.append(chunk)

    def need(self, row):
        while self.rows < min(row, ROWS):
            for copy in self.chunks[self.done]:
                copy.wait()
            self.rows = sum(CHUNKS[self.done])
            self.done += 1


def send_out(src, dst, sem):
    copy = pltpu.make_async_copy(src, dst, sem)
    copy.start()
    return copy


def search_kernel(
    total_rows,
    got_ref, solver_ref, left_ref, right_ref, below_ref, above_ref, fields_hbm,
    send_ref, wet_ref, applied_ref, carry_out,
    fields_ref, east_ref, north_ref, res_ref, weight_ref, west_ref, inv_ref, est_a, est_b, step_ref, search_ref, shift_ref, sems,
):
    spot = place()
    fields = (wet_ref, res_ref, weight_ref)
    bands = [(slice(None), slice(None), pl.ds(a * BAND, BAND)) for a in range(AGG_LAT)]
    copies = [send_out(fields_hbm.at[0:3].at[at], fields_ref.at[at], sems.at[5 + a]) for a, at in enumerate(bands)]
    for f, ref in enumerate(fields):
        for b in range(BLK):
            at = (f * BLK + b) * HY
            ref[b, 0:HY, :] = below_ref[at : at + HY, :]
            ref[b, HY + NY : ROWS, :] = above_ref[at : at + HY, :]

    def fill(g, start):
        if start % BAND == 0:
            copies[g].wait()
        at = slice(HY + start, HY + start + STEP)
        halo = unpack_columns(left_ref, right_ref, g, start - g * BAND, STEP)
        for f, ref in enumerate(fields):
            for b in range(2):
                ref[b, at, :] = fields_ref[f, b, start : start + STEP, :]
            ref[2, at, :] = halo[f]

    for_own(fill)
    own_rows = (slice(0, AGG_LON), slice(HY, HY + NY))
    outs = [
        send_out(weight_ref, carry_out.at[0], sems.at[0]),
        send_out(res_ref.at[own_rows], carry_out.at[4].at[own_rows], sems.at[3]),
    ]
    base, rows8 = 3 * BLK * HY, solver_ref.shape[0] // 3
    outs += [
        send_out(solver_ref, carry_out.at[5, 0, 0 : 3 * rows8], sems.at[10]),
        send_out(below_ref.at[base : base + rows8], carry_out.at[5, 1, 0:rows8], sems.at[11]),
        send_out(above_ref.at[base : base + rows8], carry_out.at[5, 2, 0:rows8], sems.at[12]),
    ]

    north_faces(spot, total_rows, wet_ref, north_ref, 0, 8)
    for ref in (est_a, est_b, search_ref, applied_ref, east_ref):
        clear_ends(ref)
    for b in range(BLK):
        north_ref[b, ROWS - 8 : ROWS, :] = jnp.zeros((8, LANES), F32)
    faces = (east_ref, west_ref, north_ref, shift_ref)

    def prepare(start, rows):
        all_faces(spot, total_rows, wet_ref, faces, start, rows)
        first_step(res_ref, inv_ref, faces, est_a, step_ref, start, rows)

    for_strips(prepare)
    outs += [send_out(east_ref, carry_out.at[2], sems.at[4]), send_out(north_ref, carry_out.at[3], sems.at[9])]
    parts = [(solver_ref, k * rows8) for k in range(3)] + [(below_ref, base), (above_ref, base)]
    coarse = coarse_solve(got_ref, parts)

    def finish(start, rows, band, value):
        wet, weight = load(wet_ref, start, rows), load(weight_ref, start, rows)
        part = [jnp.where(wet[b] > 0.0, value[b], 0.0) for b in range(BLK)]
        store(search_ref, start, rows, [part[b] + weight[b] * coarse[band][b] for b in range(BLK)])

    smooth(res_ref, inv_ref, faces, (est_a, est_b), step_ref, finish)
    outs.append(send_out(search_ref, carry_out.at[1], sems.at[1]))
    sums = [jnp.zeros((8, LANES), F32)] * (AGG_LAT * AGG_LON + 2)

    def apply(start, rows, band):
        here, out = operate(search_ref, *faces, start, rows)
        store(applied_ref, start, rows, out)
        if 0 < band <= AGG_LAT:
            for b in range(AGG_LON):
                k, at = (band - 1) * AGG_LON + b, (b, slice(start, start + rows))
                sums[k] = sums[k] + fold(weight_ref[at] * out[b])
                sums[-2] = sums[-2] + fold(here[b] * out[b])
                sums[-1] = sums[-1] + fold(here[b] * res_ref[at])

    for_bands(apply)
    values = [total(x) for x in sums]
    fill_rows(send_ref, own_row(spot, values[:-2], values[-2:]))
    for copy in outs:
        copy.wait()


def second_kernel(
    total_rows,
    applied_ref, wet_ref,
    out_ref,
    east_ref, north_ref, west_ref, inv_ref, est_a, est_b, step_ref, shift_ref,
):
    spot = place()
    north_faces(spot, total_rows, wet_ref, north_ref, 0, 8)
    for ref in (est_a, est_b):
        clear_ends(ref)
    faces = (east_ref, west_ref, north_ref, shift_ref)

    def prepare(start, rows):
        all_faces(spot, total_rows, wet_ref, faces, start, rows)
        first_step(applied_ref, inv_ref, faces, est_a, step_ref, start, rows)

    for_strips(prepare)

    def finish(start, rows, band, value):
        store(out_ref, start, rows, value)

    smooth(applied_ref, inv_ref, faces, (est_a, est_b), step_ref, finish)


def sums_kernel(
    total_rows,
    got_ref, smooth_ref, applied_ref, carry_hbm,
    send_ref, known_ref, search_out, applied_out, update_ref, operated_ref, rest_ref,
    solver_ref, weight_ref, search_ref, east_ref, north_ref, res_ref, full_ref, sems,
):
    spot = place()
    rows8 = solver_ref.shape[0] // 5
    pairs = [(carry_hbm.at[5, 0, 0 : 3 * rows8], solver_ref.at[0 : 3 * rows8])]
    for k in (1, 2):
        pairs.append((carry_hbm.at[5, k, 0:rows8], solver_ref.at[(k + 2) * rows8 : (k + 3) * rows8]))
    solver = fetch(pairs, sems, 5 * len(CHUNKS))
    stream = Stream(carry_hbm, (weight_ref, search_ref, east_ref, north_ref, res_ref), sems)
    for copy in solver:
        copy.wait()
    coarse = coarse_solve(got_ref, [(solver_ref, k * rows8) for k in range(5)])
    curvature, projection = own_row_sums(got_ref, 2)
    lane = lane_ids(1)
    alpha = jnp.broadcast_to(projection, (1, LANES)) / jnp.broadcast_to(curvature, (1, LANES))
    known_ref[...] = jnp.broadcast_to(jnp.where(lane == 0, curvature, alpha), (8, LANES))

    def build(start, rows, band):
        stream.need(start + rows)
        part, weight, search = [load(ref, start, rows) for ref in (smooth_ref, weight_ref, search_ref)]
        store(
            full_ref, start, rows,
            [
                search[b] - alpha * (jnp.where(weight[b] > 0.0, part[b], 0.0) + weight[b] * coarse[band][b])
                for b in range(BLK)
            ],
        )

    accs = [jnp.zeros((8, LANES), F32)] * 4

    def apply(start):
        at, start = slice(start, start + STEP), HY + start
        here = load(full_ref, start, STEP)
        up, down = load(full_ref, start + 1, STEP), load(full_ref, start - 1, STEP)
        right, left = east_of(here), west_of(here)
        ef = load(east_ref, start, STEP)
        wf = west_of(ef)
        nf, sf = load(north_ref, start, STEP), load(north_ref, start - 1, STEP)
        shift = SHIFT_SCALE * cosine(latitudes(spot, total_rows, start, STEP)[0])
        for b in range(AGG_LON):
            out = (
                shift * here[b]
                + ef[b] * (here[b] - right[b])
                + wf[b] * (here[b] - left[b])
                + nf[b] * (here[b] - up[b])
                + sf[b] * (here[b] - down[b])
            )
            search, applied = search_ref[b, start : start + STEP, :], applied_ref[b, start : start + STEP, :]
            rest = res_ref[b, at, :] - alpha * applied
            search_out[b, at, :] = search
            applied_out[b, at, :] = applied
            update_ref[b, at, :] = here[b]
            operated_ref[b, at, :] = out
            rest_ref[b, at, :] = rest
            pairs = ((here[b], applied), (here[b], out), (here[b], rest), (search, rest))
            for k, (x, y) in enumerate(pairs):
                accs[k] = accs[k] + fold(x * y)

    waiting = []

    def step(start, rows, band):
        build(start, rows, band)
        for ready in waiting:
            apply(ready)
        waiting.clear()
        if 0 < band <= AGG_LAT:
            waiting.append(start - HY)

    for_bands(step)
    stream.need(ROWS)
    row = jnp.zeros((1, LANES), F32)
    for k, acc in enumerate(accs):
        row = jnp.where(lane == k, total(acc), row)
    fill_rows(send_ref, row)


def final_kernel(
    got_ref, known_ref, search_ref, applied_ref, update_ref, operated_ref, rest_ref,
    field_out, residual_out, field_ref, residual_ref, sems,
):
    sums = jnp.sum(got_ref[...], axis=0, keepdims=True)
    lane = lane_ids(1)

    def pick(row, k):
        return jnp.broadcast_to(jnp.sum(jnp.where(lane == k, row, 0.0), axis=1, keepdims=True), (1, LANES))

    u_ap, u_au, u_r, p_r = [pick(sums, k) for k in range(4)]
    p_ap, alpha = pick(known_ref[0:1, :], 0), pick(known_ref[0:1, :], 1)
    beta = -u_ap / p_ap
    curvature = u_au + 2.0 * beta * u_ap + beta * beta * p_ap
    step_size = (u_r + beta * p_r) / curvature
    along = alpha + step_size * beta
    back = step_size * beta
    copies = []

    def own(a, start):
        at = slice(start, start + STEP)
        for b in range(AGG_LON):
            out = (at, slice(b * LANES, (b + 1) * LANES))
            field_ref[out] = along * search_ref[b, at, :] + step_size * update_ref[b, at, :]
            residual_ref[out] = rest_ref[b, at, :] - step_size * operated_ref[b, at, :] - back * applied_ref[b, at, :]
        if (start + STEP) % BAND == 0:
            rows = pl.ds(a * BAND, BAND)
            copies.append(send_out(field_ref.at[rows], field_out.at[rows], sems.at[2 * a]))
            copies.append(send_out(residual_ref.at[rows], residual_out.at[rows], sems.at[2 * a + 1]))

    for_own(own)
    for copy in copies:
        copy.wait()


def call(kernel, args, outs, scratch=(), hbm_outs=(), sems=0, flops=0, grant=6, hbm=()):
    def spec(i, inside):
        return pl.BlockSpec(memory_space=pl.ANY if i in (hbm if inside else hbm_outs) else pltpu.VMEM)

    return pl.pallas_call(
        kernel,
        out_shape=[jax.ShapeDtypeStruct(s, F32) for s in outs],
        in_specs=[spec(i, True) for i in range(len(args))],
        out_specs=[spec(i, False) for i in range(len(outs))],
        scratch_shapes=[pltpu.VMEM(s, F32) if isinstance(s, tuple) else s for s in scratch]
        + ([pltpu.SemaphoreType.DMA((sems,))] if sems else []),
        compiler_params=pltpu.CompilerParams(vmem_limit_bytes=int(grant * 1024 * 1024)),
        cost_estimate=pl.CostEstimate(flops=flops, bytes_accessed=4 * 1024 * 1024, transcendentals=0),
    )(*args)


def exchange(x):
    return lax.all_to_all(x, AXES, 0, 0, tiled=True)


def body(rhs, depth, mask, basis, inverse):
    n_lon, n_lat = lax.axis_size("lon"), lax.axis_size("lat")
    devices = n_lon * n_lat
    total_rows = NY * n_lat
    full = (BLK, ROWS, LANES)
    half = (AGG_LON, NY, LANES)
    rows8 = 8 * (inverse.shape[1] // LANES)
    row = (devices, LANES)

    loads = [(NY, NX), (NY, NX), pltpu.VMEM((NY, NX), jnp.int32), (NY, NX), inverse.shape]
    pack = (BAND + rows8, LANES)
    gather, to_west, to_east, fields = call(
        pack_kernel, [rhs, depth, mask, basis, inverse], [row, pack, pack, (4, *half)], hbm_outs=(3,),
        scratch=[*loads, (12 * HY, LANES), (3, *half)], sems=5 * AGG_LAT + 3, hbm=range(5), grant=56,
    )
    ring = [(i, (i + 1) % n_lon) for i in range(n_lon)]
    left = lax.ppermute(to_east, "lon", ring)
    right = lax.ppermute(to_west, "lon", [(j, i) for i, j in ring])
    got = exchange(gather)
    edge = (3 * BLK * HY + rows8, LANES)
    to_south, to_north, solver = call(
        edge_kernel, [fields, left, right], [edge, edge, (3 * rows8, LANES)], hbm=(0,),
        scratch=[(12 * HY, LANES), (rows8, LANES)], sems=2, grant=52.5,
    )
    line = [(i, i + 1) for i in range(n_lat - 1)]
    below = lax.ppermute(to_north, "lat", line)
    above = lax.ppermute(to_south, "lat", [(j, i) for i, j in line])

    send, wet, applied, carry = call(
        functools.partial(search_kernel, total_rows), [got, solver, left, right, below, above, fields],
        [row] + [full] * 2 + [(6, *full)], hbm=(6,), hbm_outs=(3,),
        scratch=[(3, *half)] + [full] * 10 + [full[1:]], sems=9 + AGG_LAT, flops=40000000, grant=50.5,
    )
    got = exchange(send)
    (smoothed,) = call(
        functools.partial(second_kernel, total_rows), [applied, wet], [full],
        scratch=[full] * 7 + [full[1:]], flops=20000000, grant=12,
    )
    send, known, *state = call(
        functools.partial(sums_kernel, total_rows), [got, smoothed, applied, carry],
        [row, (8, LANES)] + [half] * 5, hbm=(3,),
        scratch=[(5 * rows8, LANES), full, full, full, full, half, full], sems=5 * len(CHUNKS) + 3, flops=8000000, grant=48.5,
    )
    got = exchange(send)
    field, out = call(
        final_kernel, [got, known, *state], [(NY, NX)] * 2, hbm_outs=range(2), scratch=[(NY, NX)] * 2,
        sems=2 * AGG_LAT, flops=1000000, grant=4,
    )
    return field, out


def solution(mesh):
    tile = P("lat", "lon")
    return jax.shard_map(
        body,
        mesh=mesh,
        in_specs=(tile, tile, tile, tile, P(AXES, None)),
        out_specs=(tile, tile),
        check_vma=False,
    )
```

```python
import functools
import math

import jax
import jax.numpy as jnp
from jax import lax
from jax.experimental import pallas as pl
from jax.experimental.pallas import tpu as pltpu
from jax.sharding import PartitionSpec as P

SWEEPS = 4
AGG_LAT = 4
AGG_LON = 2
LOW_EDGE = 0.1
HIGH_EDGE = 2.0
SHIFT_SCALE = 1.0e-5

NY = 512
NX = 256
HY = 16
WX = 9
ROWS = NY + 2 * HY
LANES = 128
BLK = 3
BAND = NY // AGG_LAT
STEP = 16
SWEEP = 24
CHUNKS = ((0, 152), (152, 128), (280, 128), (408, 136))
SLOTS = LANES // 8
AXES = ("lon", "lat")
F32 = jnp.float32


def chebyshev_plan(sweep_total):
    interval_mid = (HIGH_EDGE + LOW_EDGE) / 2.0
    interval_half = (HIGH_EDGE - LOW_EDGE) / 2.0
    mid_ratio = interval_mid / interval_half
    previous = 1.0 / mid_ratio
    pairs = []
    for _ in range(sweep_total - 1):
        fresh = 1.0 / (2.0 * mid_ratio - previous)
        pairs.append((fresh * previous, 2.0 * fresh / interval_half))
        previous = fresh
    return 1.0 / interval_mid, pairs


def cosine(x):
    square = x * x
    out = jnp.full_like(x, -1.0 / math.factorial(14))
    for k in range(6, -1, -1):
        out = out * square + (-1.0) ** k / math.factorial(2 * k)
    return out


def place():
    lat = lax.axis_index("lat")
    return lax.axis_index("lon") * lax.axis_size("lat") + lat, lat * NY


def latitudes(spot, total_rows, start, rows):
    index = spot[1] - HY + start + lax.broadcasted_iota(jnp.int32, (rows, LANES), 0)
    inside = (index >= 0) & (index <= total_rows - 2)
    return (index.astype(F32) + 0.5) * (2.6 / total_rows) - 1.3, inside


def lane_ids(rows):
    return lax.broadcasted_iota(jnp.int32, (rows, LANES), 1)


def east_of(blocks):
    lane = lane_ids(blocks[0].shape[0])
    rolled = [pltpu.roll(v, LANES - 1, 1) for v in blocks]
    return [jnp.where(lane == LANES - 1, rolled[(b + 1) % BLK], rolled[b]) for b in range(BLK)]


def west_of(blocks):
    lane = lane_ids(blocks[0].shape[0])
    rolled = [pltpu.roll(v, 1, 1) for v in blocks]
    return [jnp.where(lane == 0, rolled[(b + BLK - 1) % BLK], rolled[b]) for b in range(BLK)]


def load(ref, start, rows):
    return [ref[b, pl.ds(start, rows), :] for b in range(BLK)]


def store(ref, start, rows, blocks):
    for b in range(BLK):
        ref[b, pl.ds(start, rows), :] = blocks[b]


def for_strips(fn):
    for start in range(8, ROWS - 8, SWEEP):
        fn(start, min(SWEEP, ROWS - 8 - start))


def for_own(fn):
    for start in range(0, NY, STEP):
        fn(start // BAND, start)


def clear_ends(ref):
    zero = jnp.zeros((8, LANES), F32)
    for b in range(BLK):
        ref[b, 0:8, :] = zero
        ref[b, ROWS - 8 : ROWS, :] = zero


def operate(v_ref, east_ref, west_ref, north_ref, shift_ref, start, rows):
    here = load(v_ref, start, rows)
    up, down = load(v_ref, start + 1, rows), load(v_ref, start - 1, rows)
    right, left = east_of(here), west_of(here)
    ef, wf = load(east_ref, start, rows), load(west_ref, start, rows)
    nf, sf = load(north_ref, start, rows), load(north_ref, start - 1, rows)
    shift = shift_ref[pl.ds(start, rows), :]
    out = [
        shift * here[b]
        + ef[b] * (here[b] - right[b])
        + wf[b] * (here[b] - left[b])
        + nf[b] * (here[b] - up[b])
        + sf[b] * (here[b] - down[b])
        for b in range(BLK)
    ]
    return here, out


def fold(x):
    return jnp.sum(x.reshape(-1, 8, LANES), axis=0)


def total(x):
    return jnp.sum(jnp.sum(x, axis=1, keepdims=True), axis=0, keepdims=True)


def own_row(spot, values, scalars=()):
    lane = lane_ids(1)
    base = (spot[0] % SLOTS) * 8
    other = ((spot[0] + SLOTS // 2) % SLOTS) * 8
    row = jnp.zeros((1, LANES), F32)
    for k, value in enumerate(values):
        row = jnp.where(lane == base + k, value, row)
    for k, value in enumerate(scalars):
        row = jnp.where(lane == other + k, value, row)
    return row


def own_row_sums(got_ref, count):
    rows = got_ref.shape[0]
    lane = lane_ids(rows)
    slot = lax.broadcasted_iota(jnp.int32, (rows, LANES), 0) % SLOTS
    other = ((slot + SLOTS // 2) % SLOTS) * 8
    got = got_ref[...]
    return [total(fold(jnp.where(lane == other + k, got, 0.0))) for k in range(count)]


def fill_rows(ref, row):
    ref[...] = jnp.broadcast_to(row, ref.shape)


def pack_kernel(
    rhs_hbm, depth_hbm, mask_hbm, basis_hbm, inverse_hbm,
    gather_ref, west_ref, east_ref, fields_out,
    rhs_ref, depth_ref, mask_ref, basis_ref, inverse_ref, edge_ref, fields_ref, sems,
):
    spot = place()
    pairs = ((rhs_hbm, rhs_ref), (mask_hbm, mask_ref), (basis_hbm, basis_ref), (depth_hbm, depth_ref))
    copies = []
    for g in range(AGG_LAT):
        at = pl.ds(g * BAND, BAND)
        copies.append(
            [pltpu.make_async_copy(src.at[at], dst.at[at], sems.at[4 * g + k]) for k, (src, dst) in enumerate(pairs)]
        )
    last = pltpu.make_async_copy(inverse_hbm, inverse_ref, sems.at[4 * AGG_LAT])
    for copy in sum(copies, []) + [last]:
        copy.start()
    groups = inverse_ref.shape[1] // LANES
    lane = lane_ids(STEP)
    sums, outs = [], []
    zero = jnp.zeros((8, LANES), F32)
    for g in range(AGG_LAT):
        for copy in copies[g]:
            copy.wait()
        accs = [zero] * AGG_LON
        for start in range(g * BAND, (g + 1) * BAND, STEP):
            out_row = start - g * BAND
            fields = []
            for b in range(AGG_LON):
                at = (pl.ds(start, STEP), pl.ds(b * LANES, LANES))
                mask = mask_ref[at].astype(F32)
                wet = depth_ref[at] * mask
                res = rhs_ref[at] * mask
                weight = basis_ref[at] * mask
                accs[b] = accs[b] + fold(weight * res)
                fields.append((wet, res, weight))
                for f, value in enumerate(fields[b]):
                    fields_ref[f, b, start : start + STEP, :] = value
                    for side, first in ((0, 0), (1, NY - HY)):
                        if start == first:
                            at = ((side * 3 + f) * 2 + b) * HY
                            edge_ref[at : at + HY, :] = value
            for ref, b, extra in ((west_ref, 0, 0), (east_ref, 1, WX)):
                packed = jnp.zeros((STEP, LANES), F32) if g == 0 else ref[out_row : out_row + STEP, :]
                for f in range(3):
                    lo = 32 * g + WX * f
                    moved = pltpu.roll(fields[b][f], (lo + extra) % LANES, 1)
                    packed = jnp.where((lane >= lo) & (lane < lo + WX), moved, packed)
                ref[out_row : out_row + STEP, :] = packed
        sums += [total(acc) for acc in accs]
        rows = (slice(None), slice(None), pl.ds(g * BAND, BAND))
        outs.append(send_out(fields_ref.at[rows], fields_out.at[0:3].at[rows], sems.at[4 * AGG_LAT + 1 + g]))
    fill_rows(gather_ref, own_row(spot, sums))
    last.wait()
    for g in range(groups):
        part = inverse_ref[:, g * LANES : (g + 1) * LANES]
        west_ref[BAND + 8 * g : BAND + 8 * g + 8, :] = part
        east_ref[BAND + 8 * g : BAND + 8 * g + 8, :] = part
    outs.append(send_out(edge_ref, fields_out.at[3, 0, 0 : edge_ref.shape[0]], sems.at[5 * AGG_LAT + 1]))
    outs.append(send_out(west_ref.at[BAND:], fields_out.at[3, 1, 0 : 8 * groups], sems.at[5 * AGG_LAT + 2]))
    for copy in outs:
        copy.wait()


def unpack_columns(left_ref, right_ref, g, start, rows):
    lane = lane_ids(rows)
    left, right = left_ref[pl.ds(start, rows), :], right_ref[pl.ds(start, rows), :]
    out = []
    for f in range(3):
        lo = 32 * g + WX * f
        from_right = pltpu.roll(right, (LANES - lo) % LANES, 1)
        from_left = pltpu.roll(left, (2 * LANES - lo - WX) % LANES, 1)
        out.append(jnp.where(lane < WX, from_right, jnp.where(lane >= LANES - WX, from_left, 0.0)))
    return out


def edge_kernel(fields_hbm, left_ref, right_ref, south_ref, north_ref, solver_ref, edge_ref, own_ref, sems):
    rows8 = own_ref.shape[0]
    groups = rows8 // 8
    pairs = ((fields_hbm.at[3, 0, 0 : edge_ref.shape[0]], edge_ref), (fields_hbm.at[3, 1, 0:rows8], own_ref))
    copies = fetch(pairs, sems, 0)
    for k, ref in ((1, left_ref), (2, right_ref)):
        solver_ref[k * rows8 : (k + 1) * rows8, :] = ref[BAND:, :]
    for copy in copies:
        copy.wait()
    solver_ref[0:rows8, :] = own_ref[...]
    sub = lax.broadcasted_iota(jnp.int32, (8, LANES), 0)
    for side, (ref, start, band) in enumerate(((south_ref, 0, 0), (north_ref, BAND - HY, AGG_LAT - 1))):
        halo = unpack_columns(left_ref, right_ref, band, start, HY)
        for f in range(3):
            for b in range(BLK):
                at = (f * BLK + b) * HY
                row = ((side * 3 + f) * 2 + b) * HY
                ref[at : at + HY, :] = edge_ref[row : row + HY, :] if b < 2 else halo[f]
        base = 3 * BLK * HY
        for i in range(groups):
            at = slice(BAND + 8 * i, BAND + 8 * i + 8)
            own, left, right = own_ref[8 * i : 8 * i + 8, :], left_ref[at, :], right_ref[at, :]
            own = pltpu.roll(own, (8 - 2 * band) % 8, 0) if band else own
            left = pltpu.roll(left, (2 - 2 * band - 1 + 16) % 8, 0)
            right = pltpu.roll(right, (3 - 2 * band + 16) % 8, 0)
            picked = jnp.where(sub < 2, own, jnp.where(sub == 2, left, right))
            ref[base + 8 * i : base + 8 * i + 8, :] = picked


def north_faces(spot, total_rows, wet_ref, north_ref, start, rows):
    wet, nxt = load(wet_ref, start, rows), load(wet_ref, start + 1, rows)
    latitude, inside = latitudes(spot, total_rows, start, rows)
    cos_row = jnp.where(inside, cosine(latitude + 1.3 / total_rows), 0.0)
    store(north_ref, start, rows, [jnp.minimum(wet[b], nxt[b]) * cos_row for b in range(BLK)])


def all_faces(spot, total_rows, wet_ref, faces, start, rows):
    east_ref, west_ref, north_ref, shift_ref = faces
    wet = load(wet_ref, start, rows)
    cos_row = cosine(latitudes(spot, total_rows, start, rows)[0])
    shift_ref[pl.ds(start, rows), :] = SHIFT_SCALE * cos_row
    over = 1.0 / cos_row
    nxt = east_of(wet)
    face = [jnp.minimum(wet[b], nxt[b]) * over for b in range(BLK)]
    store(east_ref, start, rows, face)
    store(west_ref, start, rows, west_of(face))
    north_faces(spot, total_rows, wet_ref, north_ref, start, rows)


def first_step(res_ref, inv_ref, faces, est_ref, step_ref, start, rows):
    east_ref, west_ref, north_ref, shift_ref = faces
    ef, wf = load(east_ref, start, rows), load(west_ref, start, rows)
    nf, sf = load(north_ref, start, rows), load(north_ref, start - 1, rows)
    shift = shift_ref[pl.ds(start, rows), :]
    inv = [1.0 / (shift + ef[b] + wf[b] + nf[b] + sf[b]) for b in range(BLK)]
    store(inv_ref, start, rows, inv)
    res = load(res_ref, start, rows)
    value = [chebyshev_plan(SWEEPS)[0] * (inv[b] * res[b]) for b in range(BLK)]
    store(step_ref, start, rows, value)
    store(est_ref, start, rows, value)


def smooth(res_ref, inv_ref, faces, est_refs, step_ref, finish):
    _, pairs = chebyshev_plan(SWEEPS)
    for k, (c1, c2) in enumerate(pairs):
        src, dst = est_refs[k % 2], est_refs[(k + 1) % 2]
        last = k == len(pairs) - 1

        def strip(start, rows, band=None):
            here, applied = operate(src, *faces, start, rows)
            inv, res, step = load(inv_ref, start, rows), load(res_ref, start, rows), load(step_ref, start, rows)
            step = [c1 * step[b] + c2 * (inv[b] * (res[b] - applied[b])) for b in range(BLK)]
            value = [here[b] + step[b] for b in range(BLK)]
            if last:
                finish(start, rows, band, value)
            else:
                store(step_ref, start, rows, step)
                store(dst, start, rows, value)

        if last:
            for_bands(strip)
        else:
            for_strips(strip)


def fetch(pairs, sems, first):
    return [send_out(src, dst, sems.at[first + k]) for k, (src, dst) in enumerate(pairs)]


def coarse_solve(got_ref, parts):
    groups = got_ref.shape[0] // SLOTS
    accs = [jnp.zeros((8, LANES), F32) for _ in parts]
    mine = lane_ids(SLOTS) // 8 == lax.broadcasted_iota(jnp.int32, (SLOTS, LANES), 0)
    for i in range(groups):
        vec = jnp.sum(jnp.where(mine, got_ref[i * SLOTS : (i + 1) * SLOTS, :], 0.0), axis=0, keepdims=True)
        for k, (ref, first) in enumerate(parts):
            accs[k] = accs[k] + ref[first + 8 * i : first + 8 * i + 8, :] * vec
    own, left, right, below, above = [jnp.sum(acc, axis=1, keepdims=True) for acc in accs]
    low = lane_ids(1) < LANES // 2

    def spread(value):
        return jnp.broadcast_to(value, (1, LANES))

    def edge(x):
        halo = jnp.where(low, spread(x[3:4]), spread(x[2:3]))
        return [spread(x[0:1]), spread(x[1:2]), halo]

    rows = [edge(below)]
    for a in range(AGG_LAT):
        halo = jnp.where(low, spread(right[2 * a : 2 * a + 1]), spread(left[2 * a + 1 : 2 * a + 2]))
        rows.append([spread(own[2 * a : 2 * a + 1]), spread(own[2 * a + 1 : 2 * a + 2]), halo])
    rows.append(edge(above))
    return rows


def for_bands(fn):
    fn(HY - 8, 8, 0)
    for_own(lambda a, start: fn(HY + start, STEP, a + 1))
    fn(HY + NY, 8, AGG_LAT + 1)


class Stream:
    def __init__(self, src, refs, sems):
        self.chunks, self.done, self.rows = [], 0, 0
        for k, (start, rows) in enumerate(CHUNKS):
            chunk = []
            for i, dst in enumerate(refs):
                if dst.shape[0] == BLK:
                    lo, hi, shift = start, start + rows, 0
                else:
                    lo, hi, shift = max(start, HY), min(start + rows, HY + NY), HY
                chunk.append(
                    pltpu.make_async_copy(
                        src.at[i, 0 : dst.shape[0], lo:hi, :],
                        dst.at[:, lo - shift : hi - shift, :],
                        sems.at[k * len(refs) + i],
                    )
                )
            for copy in chunk:
                copy.start()
            self.chunks.append(chunk)

    def need(self, row):
        while self.rows < min(row, ROWS):
            for copy in self.chunks[self.done]:
                copy.wait()
            self.rows = sum(CHUNKS[self.done])
            self.done += 1


def send_out(src, dst, sem):
    copy = pltpu.make_async_copy(src, dst, sem)
    copy.start()
    return copy


def fill_from(fields_hbm, which, refs, bufs, left_ref, right_ref, sems):
    bands = [(slice(None), pl.ds(a * BAND, BAND)) for a in range(AGG_LAT)]
    copies = [
        fetch([(fields_hbm.at[f].at[at], buf.at[at]) for f, buf in zip(which, bufs)], sems, a * len(which))
        for a, at in enumerate(bands)
    ]

    def fill(g, start):
        if start % BAND == 0:
            for copy in copies[g]:
                copy.wait()
        at = slice(HY + start, HY + start + STEP)
        halo = unpack_columns(left_ref, right_ref, g, start - g * BAND, STEP)
        for f, ref, buf in zip(which, refs, bufs):
            for b in range(2):
                ref[b, at, :] = buf[b, start : start + STEP, :]
            ref[2, at, :] = halo[f]

    return lambda: for_own(fill)


def fill_rows_around(f, ref, below_ref, above_ref):
    for b in range(BLK):
        at = (f * BLK + b) * HY
        ref[b, 0:HY, :] = below_ref[at : at + HY, :]
        ref[b, HY + NY : ROWS, :] = above_ref[at : at + HY, :]


def fill_kernel(left_ref, right_ref, fields_hbm, wet_ref, res_ref, buf_a, buf_b, sems):
    fill_from(fields_hbm, (0, 1), (wet_ref, res_ref), (buf_a, buf_b), left_ref, right_ref, sems)()


def search_kernel(
    total_rows,
    wet_in, res_in, got_ref, solver_ref, left_ref, right_ref, below_ref, above_ref, fields_hbm,
    wet_ref, res_ref, send_ref, applied_ref, carry_out,
    buf_ref, search_ref, weight_ref, east_ref, north_ref, west_ref, inv_ref, est_a, est_b, step_ref, shift_ref, sems,
):
    spot = place()
    fill_weight = fill_from(fields_hbm, (2,), (weight_ref,), (buf_ref,), left_ref, right_ref, sems.at[8:12])
    for f, ref in enumerate((wet_ref, res_ref, weight_ref)):
        fill_rows_around(f, ref, below_ref, above_ref)
    own_rows = (slice(0, AGG_LON), slice(HY, HY + NY))
    outs = [
        send_out(wet_ref, carry_out.at[5], sems.at[7]),
        send_out(res_ref.at[own_rows], carry_out.at[3].at[own_rows], sems.at[3]),
    ]
    base, rows8 = 3 * BLK * HY, solver_ref.shape[0] // 3
    outs += [
        send_out(solver_ref, carry_out.at[6, 0, 0 : 3 * rows8], sems.at[1]),
        send_out(below_ref.at[base : base + rows8], carry_out.at[6, 1, 0:rows8], sems.at[2]),
        send_out(above_ref.at[base : base + rows8], carry_out.at[6, 2, 0:rows8], sems.at[5]),
    ]

    north_faces(spot, total_rows, wet_ref, north_ref, 0, 8)
    for ref in (est_a, est_b, search_ref, applied_ref, east_ref):
        clear_ends(ref)
    for b in range(BLK):
        north_ref[b, ROWS - 8 : ROWS, :] = jnp.zeros((8, LANES), F32)
    faces = (east_ref, west_ref, north_ref, shift_ref)

    def prepare(start, rows):
        all_faces(spot, total_rows, wet_ref, faces, start, rows)
        first_step(res_ref, inv_ref, faces, est_a, step_ref, start, rows)

    for_strips(prepare)
    outs += [send_out(east_ref, carry_out.at[1], sems.at[4]), send_out(north_ref, carry_out.at[2], sems.at[6])]
    fill_weight()
    outs.append(send_out(weight_ref, carry_out.at[0], sems.at[0]))
    parts = [(solver_ref, k * rows8) for k in range(3)] + [(below_ref, base), (above_ref, base)]
    coarse = coarse_solve(got_ref, parts)

    def finish(start, rows, band, value):
        wet, weight = load(wet_ref, start, rows), load(weight_ref, start, rows)
        part = [jnp.where(wet[b] > 0.0, value[b], 0.0) for b in range(BLK)]
        store(search_ref, start, rows, [part[b] + weight[b] * coarse[band][b] for b in range(BLK)])

    smooth(res_ref, inv_ref, faces, (est_a, est_b), step_ref, finish)
    outs.append(send_out(search_ref, carry_out.at[4], sems.at[12]))
    sums = [jnp.zeros((8, LANES), F32)] * (AGG_LAT * AGG_LON + 2)

    def apply(start, rows, band):
        here, out = operate(search_ref, *faces, start, rows)
        store(applied_ref, start, rows, out)
        if 0 < band <= AGG_LAT:
            for b in range(AGG_LON):
                k, at = (band - 1) * AGG_LON + b, (b, slice(start, start + rows))
                sums[k] = sums[k] + fold(weight_ref[at] * out[b])
                sums[-2] = sums[-2] + fold(here[b] * out[b])
                sums[-1] = sums[-1] + fold(here[b] * res_ref[at])

    for_bands(apply)
    values = [total(x) for x in sums]
    fill_rows(send_ref, own_row(spot, values[:-2], values[-2:]))
    for copy in outs:
        copy.wait()


def second_kernel(
    total_rows,
    applied_ref, carry_hbm,
    out_ref,
    wet_ref, east_ref, north_ref, west_ref, inv_ref, est_a, est_b, step_ref, shift_ref, sems,
):
    spot = place()
    stream = Stream(carry_hbm.at[5:6], (wet_ref,), sems)
    stream.need(HY)
    north_faces(spot, total_rows, wet_ref, north_ref, 0, 8)
    for ref in (est_a, est_b):
        clear_ends(ref)
    faces = (east_ref, west_ref, north_ref, shift_ref)

    def prepare(start, rows):
        stream.need(start + rows + 1)
        all_faces(spot, total_rows, wet_ref, faces, start, rows)
        first_step(applied_ref, inv_ref, faces, est_a, step_ref, start, rows)

    for_strips(prepare)

    def finish(start, rows, band, value):
        store(out_ref, start, rows, value)

    smooth(applied_ref, inv_ref, faces, (est_a, est_b), step_ref, finish)


def sums_kernel(
    total_rows,
    got_ref, smooth_ref, applied_ref, carry_hbm,
    send_ref, known_ref, search_out, applied_out, update_ref, operated_ref, rest_ref,
    solver_ref, weight_ref, east_ref, north_ref, res_ref, search_ref, full_ref, sems,
):
    spot = place()
    rows8 = solver_ref.shape[0] // 5
    pairs = [(carry_hbm.at[6, 0, 0 : 3 * rows8], solver_ref.at[0 : 3 * rows8])]
    for k in (1, 2):
        pairs.append((carry_hbm.at[6, k, 0:rows8], solver_ref.at[(k + 2) * rows8 : (k + 3) * rows8]))
    solver = fetch(pairs, sems, 5 * len(CHUNKS))
    stream = Stream(carry_hbm, (weight_ref, east_ref, north_ref, res_ref, search_ref), sems)
    for copy in solver:
        copy.wait()
    coarse = coarse_solve(got_ref, [(solver_ref, k * rows8) for k in range(5)])
    curvature, projection = own_row_sums(got_ref, 2)
    lane = lane_ids(1)
    alpha = jnp.broadcast_to(projection, (1, LANES)) / jnp.broadcast_to(curvature, (1, LANES))
    known_ref[...] = jnp.broadcast_to(jnp.where(lane == 0, curvature, alpha), (8, LANES))

    def build(start, rows, band):
        stream.need(start + rows)
        part, weight, search = [load(ref, start, rows) for ref in (smooth_ref, weight_ref, search_ref)]
        store(
            full_ref, start, rows,
            [
                search[b] - alpha * (jnp.where(weight[b] > 0.0, part[b], 0.0) + weight[b] * coarse[band][b])
                for b in range(BLK)
            ],
        )

    accs = [jnp.zeros((8, LANES), F32)] * 4

    def apply(start):
        at, start = slice(start, start + STEP), HY + start
        here = load(full_ref, start, STEP)
        up, down = load(full_ref, start + 1, STEP), load(full_ref, start - 1, STEP)
        right, left = east_of(here), west_of(here)
        ef = load(east_ref, start, STEP)
        wf = west_of(ef)
        nf, sf = load(north_ref, start, STEP), load(north_ref, start - 1, STEP)
        shift = SHIFT_SCALE * cosine(latitudes(spot, total_rows, start, STEP)[0])
        for b in range(AGG_LON):
            out = (
                shift * here[b]
                + ef[b] * (here[b] - right[b])
                + wf[b] * (here[b] - left[b])
                + nf[b] * (here[b] - up[b])
                + sf[b] * (here[b] - down[b])
            )
            search, applied = search_ref[b, start : start + STEP, :], applied_ref[b, start : start + STEP, :]
            rest = res_ref[b, at, :] - alpha * applied
            search_out[b, at, :] = search
            applied_out[b, at, :] = applied
            update_ref[b, at, :] = here[b]
            operated_ref[b, at, :] = out
            rest_ref[b, at, :] = rest
            pairs = ((here[b], applied), (here[b], out), (here[b], rest), (search, rest))
            for k, (x, y) in enumerate(pairs):
                accs[k] = accs[k] + fold(x * y)

    waiting = []

    def step(start, rows, band):
        build(start, rows, band)
        for ready in waiting:
            apply(ready)
        waiting.clear()
        if 0 < band <= AGG_LAT:
            waiting.append(start - HY)

    for_bands(step)
    stream.need(ROWS)
    row = jnp.zeros((1, LANES), F32)
    for k, acc in enumerate(accs):
        row = jnp.where(lane == k, total(acc), row)
    fill_rows(send_ref, row)


def final_kernel(
    got_ref, known_ref, search_ref, applied_ref, update_ref, operated_ref, rest_ref,
    field_out, residual_out, field_ref, residual_ref, sems,
):
    sums = jnp.sum(got_ref[...], axis=0, keepdims=True)
    lane = lane_ids(1)

    def pick(row, k):
        return jnp.broadcast_to(jnp.sum(jnp.where(lane == k, row, 0.0), axis=1, keepdims=True), (1, LANES))

    u_ap, u_au, u_r, p_r = [pick(sums, k) for k in range(4)]
    p_ap, alpha = pick(known_ref[0:1, :], 0), pick(known_ref[0:1, :], 1)
    beta = -u_ap / p_ap
    curvature = u_au + 2.0 * beta * u_ap + beta * beta * p_ap
    step_size = (u_r + beta * p_r) / curvature
    along = alpha + step_size * beta
    back = step_size * beta
    copies = []

    def own(a, start):
        at = slice(start, start + STEP)
        for b in range(AGG_LON):
            out = (at, slice(b * LANES, (b + 1) * LANES))
            field_ref[out] = along * search_ref[b, at, :] + step_size * update_ref[b, at, :]
            residual_ref[out] = rest_ref[b, at, :] - step_size * operated_ref[b, at, :] - back * applied_ref[b, at, :]
        if (start + STEP) % BAND == 0:
            rows = pl.ds(a * BAND, BAND)
            copies.append(send_out(field_ref.at[rows], field_out.at[rows], sems.at[2 * a]))
            copies.append(send_out(residual_ref.at[rows], residual_out.at[rows], sems.at[2 * a + 1]))

    for_own(own)
    for copy in copies:
        copy.wait()


def call(kernel, args, outs, scratch=(), hbm_outs=(), sems=0, flops=0, grant=6, hbm=(), aliases=None):
    def spec(i, inside):
        return pl.BlockSpec(memory_space=pl.ANY if i in (hbm if inside else hbm_outs) else pltpu.VMEM)

    return pl.pallas_call(
        kernel,
        out_shape=[jax.ShapeDtypeStruct(s, F32) for s in outs],
        in_specs=[spec(i, True) for i in range(len(args))],
        out_specs=[spec(i, False) for i in range(len(outs))],
        scratch_shapes=[pltpu.VMEM(s, F32) if isinstance(s, tuple) else s for s in scratch]
        + ([pltpu.SemaphoreType.DMA((sems,))] if sems else []),
        input_output_aliases=aliases or {},
        compiler_params=pltpu.CompilerParams(vmem_limit_bytes=int(grant * 1024 * 1024)),
        cost_estimate=pl.CostEstimate(flops=flops, bytes_accessed=4 * 1024 * 1024, transcendentals=0),
    )(*args)


def exchange(x):
    return lax.all_to_all(x, AXES, 0, 0, tiled=True)


def body(rhs, depth, mask, basis, inverse):
    n_lon, n_lat = lax.axis_size("lon"), lax.axis_size("lat")
    devices = n_lon * n_lat
    total_rows = NY * n_lat
    full = (BLK, ROWS, LANES)
    half = (AGG_LON, NY, LANES)
    rows8 = 8 * (inverse.shape[1] // LANES)
    row = (devices, LANES)

    loads = [(NY, NX), (NY, NX), pltpu.VMEM((NY, NX), jnp.int32), (NY, NX), inverse.shape]
    pack = (BAND + rows8, LANES)
    gather, to_west, to_east, fields = call(
        pack_kernel, [rhs, depth, mask, basis, inverse], [row, pack, pack, (4, *half)], hbm_outs=(3,),
        scratch=[*loads, (12 * HY, LANES), (3, *half)], sems=5 * AGG_LAT + 3, hbm=range(5), grant=56,
    )
    ring = [(i, (i + 1) % n_lon) for i in range(n_lon)]
    left = lax.ppermute(to_east, "lon", ring)
    right = lax.ppermute(to_west, "lon", [(j, i) for i, j in ring])
    got = exchange(gather)
    edge = (3 * BLK * HY + rows8, LANES)
    to_south, to_north, solver = call(
        edge_kernel, [fields, left, right], [edge, edge, (3 * rows8, LANES)], hbm=(0,),
        scratch=[(12 * HY, LANES), (rows8, LANES)], sems=2, grant=52.5,
    )
    line = [(i, i + 1) for i in range(n_lat - 1)]
    below = lax.ppermute(to_north, "lat", line)
    above = lax.ppermute(to_south, "lat", [(j, i) for i, j in line])

    ext = call(
        fill_kernel, [left, right, fields], [full] * 2, hbm=(2,), scratch=[half, half], sems=2 * AGG_LAT,
        flops=20000000, grant=50.5,
    )
    _, _, send, applied, carry = call(
        functools.partial(search_kernel, total_rows), [*ext, got, solver, left, right, below, above, fields],
        [full] * 2 + [row, full, (7, *full)], hbm=(8,), hbm_outs=(4,), aliases={0: 0, 1: 1},
        scratch=[half] + [full] * 9 + [full[1:]], sems=13, flops=40000000, grant=49.5,
    )
    got = exchange(send)
    (smoothed,) = call(
        functools.partial(second_kernel, total_rows), [applied, carry], [full], hbm=(1,),
        scratch=[full] * 8 + [full[1:]], sems=len(CHUNKS), flops=20000000, grant=50,
    )
    send, known, *state = call(
        functools.partial(sums_kernel, total_rows), [got, smoothed, applied, carry],
        [row, (8, LANES)] + [half] * 5, hbm=(3,),
        scratch=[(5 * rows8, LANES), full, full, full, half, full, full], sems=5 * len(CHUNKS) + 3, flops=8000000, grant=48.5,
    )
    got = exchange(send)
    field, out = call(
        final_kernel, [got, known, *state], [(NY, NX)] * 2, hbm_outs=range(2), scratch=[(NY, NX)] * 2,
        sems=2 * AGG_LAT, flops=1000000, grant=4,
    )
    return field, out


def solution(mesh):
    tile = P("lat", "lon")
    return jax.shard_map(
        body,
        mesh=mesh,
        in_specs=(tile, tile, tile, tile, P(AXES, None)),
        out_specs=(tile, tile),
        check_vma=False,
    )
```

```python
import functools
import math

import jax
import jax.numpy as jnp
from jax import lax
from jax.experimental import pallas as pl
from jax.experimental.pallas import tpu as pltpu
from jax.sharding import PartitionSpec as P

SWEEPS = 4
AGG_LAT = 4
AGG_LON = 2
LOW_EDGE = 0.1
HIGH_EDGE = 2.0
SHIFT_SCALE = 1.0e-5

NY = 512
NX = 256
HY = 16
WX = 9
ROWS = NY + 2 * HY
LANES = 128
BLK = 3
BAND = NY // AGG_LAT
STEP = 16
SWEEP = 24
CHUNKS = ((0, 152), (152, 128), (280, 128), (408, 136))
SLOTS = LANES // 8
AXES = ("lon", "lat")
F32 = jnp.float32


def chebyshev_plan(sweep_total):
    interval_mid = (HIGH_EDGE + LOW_EDGE) / 2.0
    interval_half = (HIGH_EDGE - LOW_EDGE) / 2.0
    mid_ratio = interval_mid / interval_half
    previous = 1.0 / mid_ratio
    pairs = []
    for _ in range(sweep_total - 1):
        fresh = 1.0 / (2.0 * mid_ratio - previous)
        pairs.append((fresh * previous, 2.0 * fresh / interval_half))
        previous = fresh
    return 1.0 / interval_mid, pairs


def cosine(x):
    square = x * x
    out = jnp.full_like(x, -1.0 / math.factorial(14))
    for k in range(6, -1, -1):
        out = out * square + (-1.0) ** k / math.factorial(2 * k)
    return out


def place():
    lat = lax.axis_index("lat")
    return lax.axis_index("lon") * lax.axis_size("lat") + lat, lat * NY


def latitudes(spot, total_rows, start, rows):
    index = spot[1] - HY + start + lax.broadcasted_iota(jnp.int32, (rows, LANES), 0)
    inside = (index >= 0) & (index <= total_rows - 2)
    return (index.astype(F32) + 0.5) * (2.6 / total_rows) - 1.3, inside


def lane_ids(rows):
    return lax.broadcasted_iota(jnp.int32, (rows, LANES), 1)


def east_of(blocks):
    lane = lane_ids(blocks[0].shape[0])
    rolled = [pltpu.roll(v, LANES - 1, 1) for v in blocks]
    return [jnp.where(lane == LANES - 1, rolled[(b + 1) % BLK], rolled[b]) for b in range(BLK)]


def west_of(blocks):
    lane = lane_ids(blocks[0].shape[0])
    rolled = [pltpu.roll(v, 1, 1) for v in blocks]
    return [jnp.where(lane == 0, rolled[(b + BLK - 1) % BLK], rolled[b]) for b in range(BLK)]


def load(ref, start, rows):
    return [ref[b, pl.ds(start, rows), :] for b in range(BLK)]


def store(ref, start, rows, blocks):
    for b in range(BLK):
        ref[b, pl.ds(start, rows), :] = blocks[b]


def for_strips(fn):
    for start in range(8, ROWS - 8, SWEEP):
        fn(start, min(SWEEP, ROWS - 8 - start))


def for_own(fn):
    for start in range(0, NY, STEP):
        fn(start // BAND, start)


def clear_ends(ref):
    zero = jnp.zeros((8, LANES), F32)
    for b in range(BLK):
        ref[b, 0:8, :] = zero
        ref[b, ROWS - 8 : ROWS, :] = zero


def operate(v_ref, east_ref, west_ref, north_ref, shift_ref, start, rows):
    here = load(v_ref, start, rows)
    up, down = load(v_ref, start + 1, rows), load(v_ref, start - 1, rows)
    right, left = east_of(here), west_of(here)
    ef, wf = load(east_ref, start, rows), load(west_ref, start, rows)
    nf, sf = load(north_ref, start, rows), load(north_ref, start - 1, rows)
    shift = shift_ref[pl.ds(start, rows), :]
    out = [
        shift * here[b]
        + ef[b] * (here[b] - right[b])
        + wf[b] * (here[b] - left[b])
        + nf[b] * (here[b] - up[b])
        + sf[b] * (here[b] - down[b])
        for b in range(BLK)
    ]
    return here, out


def fold(x):
    return jnp.sum(x.reshape(-1, 8, LANES), axis=0)


def total(x):
    return jnp.sum(jnp.sum(x, axis=1, keepdims=True), axis=0, keepdims=True)


def own_row(spot, values, scalars=()):
    lane = lane_ids(1)
    base = (spot[0] % SLOTS) * 8
    other = ((spot[0] + SLOTS // 2) % SLOTS) * 8
    row = jnp.zeros((1, LANES), F32)
    for k, value in enumerate(values):
        row = jnp.where(lane == base + k, value, row)
    for k, value in enumerate(scalars):
        row = jnp.where(lane == other + k, value, row)
    return row


def own_row_sums(got_ref, count):
    rows = got_ref.shape[0]
    lane = lane_ids(rows)
    slot = lax.broadcasted_iota(jnp.int32, (rows, LANES), 0) % SLOTS
    other = ((slot + SLOTS // 2) % SLOTS) * 8
    got = got_ref[...]
    return [total(fold(jnp.where(lane == other + k, got, 0.0))) for k in range(count)]


def fill_rows(ref, row):
    ref[...] = jnp.broadcast_to(row, ref.shape)


def pack_kernel(
    rhs_hbm, depth_hbm, mask_hbm, basis_hbm, inverse_hbm,
    gather_ref, west_ref, east_ref, fields_out,
    rhs_ref, depth_ref, mask_ref, basis_ref, inverse_ref, edge_ref, fields_ref, sems,
):
    spot = place()
    pairs = ((rhs_hbm, rhs_ref), (mask_hbm, mask_ref), (basis_hbm, basis_ref), (depth_hbm, depth_ref))
    copies = []
    for g in range(AGG_LAT):
        at = pl.ds(g * BAND, BAND)
        copies.append(
            [pltpu.make_async_copy(src.at[at], dst.at[at], sems.at[4 * g + k]) for k, (src, dst) in enumerate(pairs)]
        )
    last = pltpu.make_async_copy(inverse_hbm, inverse_ref, sems.at[4 * AGG_LAT])
    for copy in sum(copies, []) + [last]:
        copy.start()
    groups = inverse_ref.shape[1] // LANES
    lane = lane_ids(STEP)
    sums, outs = [], []
    zero = jnp.zeros((8, LANES), F32)
    for g in range(AGG_LAT):
        for copy in copies[g]:
            copy.wait()
        accs = [zero] * AGG_LON
        for start in range(g * BAND, (g + 1) * BAND, STEP):
            out_row = start - g * BAND
            fields = []
            for b in range(AGG_LON):
                at = (pl.ds(start, STEP), pl.ds(b * LANES, LANES))
                mask = mask_ref[at].astype(F32)
                wet = depth_ref[at] * mask
                res = rhs_ref[at] * mask
                weight = basis_ref[at] * mask
                accs[b] = accs[b] + fold(weight * res)
                fields.append((wet, res, weight))
                for f, value in enumerate(fields[b]):
                    fields_ref[f, b, start : start + STEP, :] = value
                    for side, first in ((0, 0), (1, NY - HY)):
                        if start == first:
                            at = ((side * 3 + f) * 2 + b) * HY
                            edge_ref[at : at + HY, :] = value
            for ref, b, extra in ((west_ref, 0, 0), (east_ref, 1, WX)):
                packed = jnp.zeros((STEP, LANES), F32) if g == 0 else ref[out_row : out_row + STEP, :]
                for f in range(3):
                    lo = 32 * g + WX * f
                    moved = pltpu.roll(fields[b][f], (lo + extra) % LANES, 1)
                    packed = jnp.where((lane >= lo) & (lane < lo + WX), moved, packed)
                ref[out_row : out_row + STEP, :] = packed
        sums += [total(acc) for acc in accs]
        rows = (slice(None), slice(None), pl.ds(g * BAND, BAND))
        outs.append(send_out(fields_ref.at[rows], fields_out.at[0:3].at[rows], sems.at[4 * AGG_LAT + 1 + g]))
    fill_rows(gather_ref, own_row(spot, sums))
    last.wait()
    for g in range(groups):
        part = inverse_ref[:, g * LANES : (g + 1) * LANES]
        west_ref[BAND + 8 * g : BAND + 8 * g + 8, :] = part
        east_ref[BAND + 8 * g : BAND + 8 * g + 8, :] = part
    outs.append(send_out(edge_ref, fields_out.at[3, 0, 0 : edge_ref.shape[0]], sems.at[5 * AGG_LAT + 1]))
    outs.append(send_out(west_ref.at[BAND:], fields_out.at[3, 1, 0 : 8 * groups], sems.at[5 * AGG_LAT + 2]))
    for copy in outs:
        copy.wait()


def unpack_columns(left_ref, right_ref, g, start, rows):
    lane = lane_ids(rows)
    left, right = left_ref[pl.ds(start, rows), :], right_ref[pl.ds(start, rows), :]
    out = []
    for f in range(3):
        lo = 32 * g + WX * f
        from_right = pltpu.roll(right, (LANES - lo) % LANES, 1)
        from_left = pltpu.roll(left, (2 * LANES - lo - WX) % LANES, 1)
        out.append(jnp.where(lane < WX, from_right, jnp.where(lane >= LANES - WX, from_left, 0.0)))
    return out


def edge_kernel(fields_hbm, left_ref, right_ref, south_ref, north_ref, solver_ref, edge_ref, own_ref, sems):
    rows8 = own_ref.shape[0]
    groups = rows8 // 8
    pairs = ((fields_hbm.at[3, 0, 0 : edge_ref.shape[0]], edge_ref), (fields_hbm.at[3, 1, 0:rows8], own_ref))
    copies = fetch(pairs, sems, 0)
    for k, ref in ((1, left_ref), (2, right_ref)):
        solver_ref[k * rows8 : (k + 1) * rows8, :] = ref[BAND:, :]
    for copy in copies:
        copy.wait()
    solver_ref[0:rows8, :] = own_ref[...]
    sub = lax.broadcasted_iota(jnp.int32, (8, LANES), 0)
    for side, (ref, start, band) in enumerate(((south_ref, 0, 0), (north_ref, BAND - HY, AGG_LAT - 1))):
        halo = unpack_columns(left_ref, right_ref, band, start, HY)
        for f in range(3):
            for b in range(BLK):
                at = (f * BLK + b) * HY
                row = ((side * 3 + f) * 2 + b) * HY
                ref[at : at + HY, :] = edge_ref[row : row + HY, :] if b < 2 else halo[f]
        base = 3 * BLK * HY
        for i in range(groups):
            at = slice(BAND + 8 * i, BAND + 8 * i + 8)
            own, left, right = own_ref[8 * i : 8 * i + 8, :], left_ref[at, :], right_ref[at, :]
            own = pltpu.roll(own, (8 - 2 * band) % 8, 0) if band else own
            left = pltpu.roll(left, (2 - 2 * band - 1 + 16) % 8, 0)
            right = pltpu.roll(right, (3 - 2 * band + 16) % 8, 0)
            picked = jnp.where(sub < 2, own, jnp.where(sub == 2, left, right))
            ref[base + 8 * i : base + 8 * i + 8, :] = picked


def north_faces(spot, total_rows, wet_ref, north_ref, start, rows):
    wet, nxt = load(wet_ref, start, rows), load(wet_ref, start + 1, rows)
    latitude, inside = latitudes(spot, total_rows, start, rows)
    cos_row = jnp.where(inside, cosine(latitude + 1.3 / total_rows), 0.0)
    store(north_ref, start, rows, [jnp.minimum(wet[b], nxt[b]) * cos_row for b in range(BLK)])


def all_faces(spot, total_rows, wet_ref, faces, start, rows):
    east_ref, west_ref, north_ref, shift_ref = faces
    wet = load(wet_ref, start, rows)
    cos_row = cosine(latitudes(spot, total_rows, start, rows)[0])
    shift_ref[pl.ds(start, rows), :] = SHIFT_SCALE * cos_row
    over = 1.0 / cos_row
    nxt = east_of(wet)
    face = [jnp.minimum(wet[b], nxt[b]) * over for b in range(BLK)]
    store(east_ref, start, rows, face)
    store(west_ref, start, rows, west_of(face))
    north_faces(spot, total_rows, wet_ref, north_ref, start, rows)


def first_step(res_ref, inv_ref, faces, est_ref, step_ref, start, rows):
    east_ref, west_ref, north_ref, shift_ref = faces
    ef, wf = load(east_ref, start, rows), load(west_ref, start, rows)
    nf, sf = load(north_ref, start, rows), load(north_ref, start - 1, rows)
    shift = shift_ref[pl.ds(start, rows), :]
    inv = [1.0 / (shift + ef[b] + wf[b] + nf[b] + sf[b]) for b in range(BLK)]
    store(inv_ref, start, rows, inv)
    res = load(res_ref, start, rows)
    value = [chebyshev_plan(SWEEPS)[0] * (inv[b] * res[b]) for b in range(BLK)]
    store(step_ref, start, rows, value)
    store(est_ref, start, rows, value)


def smooth(res_ref, inv_ref, faces, est_refs, step_ref, finish):
    _, pairs = chebyshev_plan(SWEEPS)
    for k, (c1, c2) in enumerate(pairs):
        src, dst = est_refs[k % 2], est_refs[(k + 1) % 2]
        last = k == len(pairs) - 1

        def strip(start, rows, band=None):
            here, applied = operate(src, *faces, start, rows)
            inv, res, step = load(inv_ref, start, rows), load(res_ref, start, rows), load(step_ref, start, rows)
            step = [c1 * step[b] + c2 * (inv[b] * (res[b] - applied[b])) for b in range(BLK)]
            value = [here[b] + step[b] for b in range(BLK)]
            if last:
                finish(start, rows, band, value)
            else:
                store(step_ref, start, rows, step)
                store(dst, start, rows, value)

        if last:
            for_bands(strip)
        else:
            for_strips(strip)


def fetch(pairs, sems, first):
    return [send_out(src, dst, sems.at[first + k]) for k, (src, dst) in enumerate(pairs)]


def coarse_solve(got_ref, parts):
    groups = got_ref.shape[0] // SLOTS
    accs = [jnp.zeros((8, LANES), F32) for _ in parts]
    mine = lane_ids(SLOTS) // 8 == lax.broadcasted_iota(jnp.int32, (SLOTS, LANES), 0)
    for i in range(groups):
        vec = jnp.sum(jnp.where(mine, got_ref[i * SLOTS : (i + 1) * SLOTS, :], 0.0), axis=0, keepdims=True)
        for k, (ref, first) in enumerate(parts):
            accs[k] = accs[k] + ref[first + 8 * i : first + 8 * i + 8, :] * vec
    own, left, right, below, above = [jnp.sum(acc, axis=1, keepdims=True) for acc in accs]
    low = lane_ids(1) < LANES // 2

    def spread(value):
        return jnp.broadcast_to(value, (1, LANES))

    def edge(x):
        halo = jnp.where(low, spread(x[3:4]), spread(x[2:3]))
        return [spread(x[0:1]), spread(x[1:2]), halo]

    rows = [edge(below)]
    for a in range(AGG_LAT):
        halo = jnp.where(low, spread(right[2 * a : 2 * a + 1]), spread(left[2 * a + 1 : 2 * a + 2]))
        rows.append([spread(own[2 * a : 2 * a + 1]), spread(own[2 * a + 1 : 2 * a + 2]), halo])
    rows.append(edge(above))
    return rows


def for_bands(fn):
    fn(HY - 8, 8, 0)
    for_own(lambda a, start: fn(HY + start, STEP, a + 1))
    fn(HY + NY, 8, AGG_LAT + 1)


class Stream:
    def __init__(self, src, refs, sems):
        self.chunks, self.done, self.rows = [], 0, 0
        for k, (start, rows) in enumerate(CHUNKS):
            chunk = []
            for i, dst in enumerate(refs):
                if dst.shape[0] == BLK:
                    lo, hi, shift = start, start + rows, 0
                else:
                    lo, hi, shift = max(start, HY), min(start + rows, HY + NY), HY
                chunk.append(
                    pltpu.make_async_copy(
                        src.at[i, 0 : dst.shape[0], lo:hi, :],
                        dst.at[:, lo - shift : hi - shift, :],
                        sems.at[k * len(refs) + i],
                    )
                )
            for copy in chunk:
                copy.start()
            self.chunks.append(chunk)

    def need(self, row):
        while self.rows < min(row, ROWS):
            for copy in self.chunks[self.done]:
                copy.wait()
            self.rows = sum(CHUNKS[self.done])
            self.done += 1


def send_out(src, dst, sem):
    copy = pltpu.make_async_copy(src, dst, sem)
    copy.start()
    return copy


def fill_from(fields_hbm, which, refs, bufs, left_ref, right_ref, sems):
    bands = [(slice(None), pl.ds(a * BAND, BAND)) for a in range(AGG_LAT)]
    copies = [
        fetch([(fields_hbm.at[f].at[at], buf.at[at]) for f, buf in zip(which, bufs)], sems, a * len(which))
        for a, at in enumerate(bands)
    ]

    def fill(g, start):
        if start % BAND == 0:
            for copy in copies[g]:
                copy.wait()
        at = slice(HY + start, HY + start + STEP)
        halo = unpack_columns(left_ref, right_ref, g, start - g * BAND, STEP)
        for f, ref, buf in zip(which, refs, bufs):
            for b in range(2):
                ref[b, at, :] = buf[b, start : start + STEP, :]
            ref[2, at, :] = halo[f]

    return lambda: for_own(fill)


def fill_rows_around(f, ref, below_ref, above_ref):
    for b in range(BLK):
        at = (f * BLK + b) * HY
        ref[b, 0:HY, :] = below_ref[at : at + HY, :]
        ref[b, HY + NY : ROWS, :] = above_ref[at : at + HY, :]


def fill_kernel(left_ref, right_ref, fields_hbm, wet_ref, res_ref, buf_a, buf_b, sems):
    fill_from(fields_hbm, (0, 1), (wet_ref, res_ref), (buf_a, buf_b), left_ref, right_ref, sems)()


def search_kernel(
    total_rows,
    wet_in, res_in, got_ref, solver_ref, left_ref, right_ref, below_ref, above_ref, fields_hbm,
    wet_ref, res_ref, send_ref, applied_ref, carry_out,
    buf_ref, search_ref, weight_ref, east_ref, north_ref, west_ref, inv_ref, est_a, est_b, step_ref, shift_ref, sems,
):
    spot = place()
    fill_weight = fill_from(fields_hbm, (2,), (weight_ref,), (buf_ref,), left_ref, right_ref, sems.at[8:12])
    for f, ref in enumerate((wet_ref, res_ref, weight_ref)):
        fill_rows_around(f, ref, below_ref, above_ref)
    own_rows = (slice(0, AGG_LON), slice(HY, HY + NY))
    outs = [
        send_out(wet_ref, carry_out.at[5], sems.at[7]),
        send_out(res_ref.at[own_rows], carry_out.at[3].at[own_rows], sems.at[3]),
    ]
    base, rows8 = 3 * BLK * HY, solver_ref.shape[0] // 3
    outs += [
        send_out(solver_ref, carry_out.at[6, 0, 0 : 3 * rows8], sems.at[1]),
        send_out(below_ref.at[base : base + rows8], carry_out.at[6, 1, 0:rows8], sems.at[2]),
        send_out(above_ref.at[base : base + rows8], carry_out.at[6, 2, 0:rows8], sems.at[5]),
    ]

    north_faces(spot, total_rows, wet_ref, north_ref, 0, 8)
    for ref in (est_a, est_b, search_ref, applied_ref, east_ref):
        clear_ends(ref)
    for b in range(BLK):
        north_ref[b, ROWS - 8 : ROWS, :] = jnp.zeros((8, LANES), F32)
    faces = (east_ref, west_ref, north_ref, shift_ref)

    def prepare(start, rows):
        all_faces(spot, total_rows, wet_ref, faces, start, rows)
        first_step(res_ref, inv_ref, faces, est_a, step_ref, start, rows)

    for_strips(prepare)
    outs += [send_out(east_ref, carry_out.at[1], sems.at[4]), send_out(north_ref, carry_out.at[2], sems.at[6])]
    fill_weight()
    outs.append(send_out(weight_ref, carry_out.at[0], sems.at[0]))
    parts = [(solver_ref, k * rows8) for k in range(3)] + [(below_ref, base), (above_ref, base)]
    coarse = coarse_solve(got_ref, parts)

    def finish(start, rows, band, value):
        wet, weight = load(wet_ref, start, rows), load(weight_ref, start, rows)
        part = [jnp.where(wet[b] > 0.0, value[b], 0.0) for b in range(BLK)]
        store(search_ref, start, rows, [part[b] + weight[b] * coarse[band][b] for b in range(BLK)])

    smooth(res_ref, inv_ref, faces, (est_a, est_b), step_ref, finish)
    outs.append(send_out(search_ref, carry_out.at[4], sems.at[12]))
    sums = [jnp.zeros((8, LANES), F32)] * (AGG_LAT * AGG_LON + 2)

    def apply(start, rows, band):
        here, out = operate(search_ref, *faces, start, rows)
        store(applied_ref, start, rows, out)
        if 0 < band <= AGG_LAT:
            for b in range(AGG_LON):
                k, at = (band - 1) * AGG_LON + b, (b, slice(start, start + rows))
                sums[k] = sums[k] + fold(weight_ref[at] * out[b])
                sums[-2] = sums[-2] + fold(here[b] * out[b])
                sums[-1] = sums[-1] + fold(here[b] * res_ref[at])

    for_bands(apply)
    values = [total(x) for x in sums]
    fill_rows(send_ref, own_row(spot, values[:-2], values[-2:]))
    for copy in outs:
        copy.wait()


def second_kernel(
    total_rows,
    applied_ref, carry_hbm,
    out_ref, search_ref, rows_ref,
    wet_ref, east_ref, north_ref, west_ref, inv_ref, est_a, est_b, step_ref, shift_ref, sems,
):
    spot = place()
    stream = Stream(carry_hbm.at[5:6], (wet_ref,), sems)
    rows8 = rows_ref.shape[0] // 5
    pairs = [
        (carry_hbm.at[6, 0, 0 : 3 * rows8], rows_ref.at[0 : 3 * rows8]),
        (carry_hbm.at[6, 1, 0:rows8], rows_ref.at[3 * rows8 : 4 * rows8]),
        (carry_hbm.at[6, 2, 0:rows8], rows_ref.at[4 * rows8 : 5 * rows8]),
        (carry_hbm.at[4], search_ref),
    ]
    back = fetch(pairs, sems, len(CHUNKS))
    stream.need(HY)
    north_faces(spot, total_rows, wet_ref, north_ref, 0, 8)
    for ref in (est_a, est_b):
        clear_ends(ref)
    faces = (east_ref, west_ref, north_ref, shift_ref)

    def prepare(start, rows):
        stream.need(start + rows + 1)
        all_faces(spot, total_rows, wet_ref, faces, start, rows)
        first_step(applied_ref, inv_ref, faces, est_a, step_ref, start, rows)

    for_strips(prepare)

    def finish(start, rows, band, value):
        store(out_ref, start, rows, value)

    smooth(applied_ref, inv_ref, faces, (est_a, est_b), step_ref, finish)
    for copy in back:
        copy.wait()


def sums_kernel(
    total_rows,
    got_ref, smooth_ref, applied_ref, search_ref, rows_ref, carry_hbm,
    send_ref, known_ref, search_out, applied_out, update_ref, operated_ref, rest_ref,
    weight_ref, east_ref, north_ref, res_ref, full_ref, sems,
):
    spot = place()
    rows8 = rows_ref.shape[0] // 5
    stream = Stream(carry_hbm, (weight_ref, east_ref, north_ref, res_ref), sems)
    coarse = coarse_solve(got_ref, [(rows_ref, k * rows8) for k in range(5)])
    curvature, projection = own_row_sums(got_ref, 2)
    lane = lane_ids(1)
    alpha = jnp.broadcast_to(projection, (1, LANES)) / jnp.broadcast_to(curvature, (1, LANES))
    known_ref[...] = jnp.broadcast_to(jnp.where(lane == 0, curvature, alpha), (8, LANES))

    def build(start, rows, band):
        stream.need(start + rows)
        part, weight, search = [load(ref, start, rows) for ref in (smooth_ref, weight_ref, search_ref)]
        store(
            full_ref, start, rows,
            [
                search[b] - alpha * (jnp.where(weight[b] > 0.0, part[b], 0.0) + weight[b] * coarse[band][b])
                for b in range(BLK)
            ],
        )

    accs = [jnp.zeros((8, LANES), F32)] * 4

    def apply(start):
        at, start = slice(start, start + STEP), HY + start
        here = load(full_ref, start, STEP)
        up, down = load(full_ref, start + 1, STEP), load(full_ref, start - 1, STEP)
        right, left = east_of(here), west_of(here)
        ef = load(east_ref, start, STEP)
        wf = west_of(ef)
        nf, sf = load(north_ref, start, STEP), load(north_ref, start - 1, STEP)
        shift = SHIFT_SCALE * cosine(latitudes(spot, total_rows, start, STEP)[0])
        for b in range(AGG_LON):
            out = (
                shift * here[b]
                + ef[b] * (here[b] - right[b])
                + wf[b] * (here[b] - left[b])
                + nf[b] * (here[b] - up[b])
                + sf[b] * (here[b] - down[b])
            )
            search, applied = search_ref[b, start : start + STEP, :], applied_ref[b, start : start + STEP, :]
            rest = res_ref[b, at, :] - alpha * applied
            search_out[b, at, :] = search
            applied_out[b, at, :] = applied
            update_ref[b, at, :] = here[b]
            operated_ref[b, at, :] = out
            rest_ref[b, at, :] = rest
            pairs = ((here[b], applied), (here[b], out), (here[b], rest), (search, rest))
            for k, (x, y) in enumerate(pairs):
                accs[k] = accs[k] + fold(x * y)

    waiting = []

    def step(start, rows, band):
        build(start, rows, band)
        for ready in waiting:
            apply(ready)
        waiting.clear()
        if 0 < band <= AGG_LAT:
            waiting.append(start - HY)

    for_bands(step)
    stream.need(ROWS)
    row = jnp.zeros((1, LANES), F32)
    for k, acc in enumerate(accs):
        row = jnp.where(lane == k, total(acc), row)
    fill_rows(send_ref, row)


def final_kernel(
    got_ref, known_ref, search_ref, applied_ref, update_ref, operated_ref, rest_ref,
    field_out, residual_out, field_ref, residual_ref, sems,
):
    sums = jnp.sum(got_ref[...], axis=0, keepdims=True)
    lane = lane_ids(1)

    def pick(row, k):
        return jnp.broadcast_to(jnp.sum(jnp.where(lane == k, row, 0.0), axis=1, keepdims=True), (1, LANES))

    u_ap, u_au, u_r, p_r = [pick(sums, k) for k in range(4)]
    p_ap, alpha = pick(known_ref[0:1, :], 0), pick(known_ref[0:1, :], 1)
    beta = -u_ap / p_ap
    curvature = u_au + 2.0 * beta * u_ap + beta * beta * p_ap
    step_size = (u_r + beta * p_r) / curvature
    along = alpha + step_size * beta
    back = step_size * beta
    copies = []

    def own(a, start):
        at = slice(start, start + STEP)
        for b in range(AGG_LON):
            out = (at, slice(b * LANES, (b + 1) * LANES))
            field_ref[out] = along * search_ref[b, at, :] + step_size * update_ref[b, at, :]
            residual_ref[out] = rest_ref[b, at, :] - step_size * operated_ref[b, at, :] - back * applied_ref[b, at, :]
        if (start + STEP) % BAND == 0:
            rows = pl.ds(a * BAND, BAND)
            copies.append(send_out(field_ref.at[rows], field_out.at[rows], sems.at[2 * a]))
            copies.append(send_out(residual_ref.at[rows], residual_out.at[rows], sems.at[2 * a + 1]))

    for_own(own)
    for copy in copies:
        copy.wait()


def call(kernel, args, outs, scratch=(), hbm_outs=(), sems=0, flops=0, grant=6, hbm=(), aliases=None):
    def spec(i, inside):
        return pl.BlockSpec(memory_space=pl.ANY if i in (hbm if inside else hbm_outs) else pltpu.VMEM)

    return pl.pallas_call(
        kernel,
        out_shape=[jax.ShapeDtypeStruct(s, F32) for s in outs],
        in_specs=[spec(i, True) for i in range(len(args))],
        out_specs=[spec(i, False) for i in range(len(outs))],
        scratch_shapes=[pltpu.VMEM(s, F32) if isinstance(s, tuple) else s for s in scratch]
        + ([pltpu.SemaphoreType.DMA((sems,))] if sems else []),
        input_output_aliases=aliases or {},
        compiler_params=pltpu.CompilerParams(vmem_limit_bytes=int(grant * 1024 * 1024)),
        cost_estimate=pl.CostEstimate(flops=flops, bytes_accessed=4 * 1024 * 1024, transcendentals=0),
    )(*args)


def exchange(x):
    return lax.all_to_all(x, AXES, 0, 0, tiled=True)


def body(rhs, depth, mask, basis, inverse):
    n_lon, n_lat = lax.axis_size("lon"), lax.axis_size("lat")
    devices = n_lon * n_lat
    total_rows = NY * n_lat
    full = (BLK, ROWS, LANES)
    half = (AGG_LON, NY, LANES)
    rows8 = 8 * (inverse.shape[1] // LANES)
    row = (devices, LANES)

    loads = [(NY, NX), (NY, NX), pltpu.VMEM((NY, NX), jnp.int32), (NY, NX), inverse.shape]
    pack = (BAND + rows8, LANES)
    gather, to_west, to_east, fields = call(
        pack_kernel, [rhs, depth, mask, basis, inverse], [row, pack, pack, (4, *half)], hbm_outs=(3,),
        scratch=[*loads, (12 * HY, LANES), (3, *half)], sems=5 * AGG_LAT + 3, hbm=range(5), grant=56,
    )
    ring = [(i, (i + 1) % n_lon) for i in range(n_lon)]
    left = lax.ppermute(to_east, "lon", ring)
    right = lax.ppermute(to_west, "lon", [(j, i) for i, j in ring])
    got = exchange(gather)
    edge = (3 * BLK * HY + rows8, LANES)
    to_south, to_north, solver = call(
        edge_kernel, [fields, left, right], [edge, edge, (3 * rows8, LANES)], hbm=(0,),
        scratch=[(12 * HY, LANES), (rows8, LANES)], sems=2, grant=52.5,
    )
    line = [(i, i + 1) for i in range(n_lat - 1)]
    below = lax.ppermute(to_north, "lat", line)
    above = lax.ppermute(to_south, "lat", [(j, i) for i, j in line])

    ext = call(
        fill_kernel, [left, right, fields], [full] * 2, hbm=(2,), scratch=[half, half], sems=2 * AGG_LAT,
        flops=20000000, grant=50.5,
    )
    _, _, send, applied, carry = call(
        functools.partial(search_kernel, total_rows), [*ext, got, solver, left, right, below, above, fields],
        [full] * 2 + [row, full, (7, *full)], hbm=(8,), hbm_outs=(4,), aliases={0: 0, 1: 1},
        scratch=[half] + [full] * 9 + [full[1:]], sems=13, flops=40000000, grant=49.5,
    )
    got = exchange(send)
    smoothed, search, solver = call(
        functools.partial(second_kernel, total_rows), [applied, carry],
        [full, full, (5 * rows8, LANES)], hbm=(1,), scratch=[full] * 8 + [full[1:]], sems=len(CHUNKS) + 4, flops=20000000, grant=50,
    )
    send, known, *state = call(
        functools.partial(sums_kernel, total_rows), [got, smoothed, applied, search, solver, carry],
        [row, (8, LANES)] + [half] * 5, hbm=(5,),
        scratch=[full, full, full, half, full], sems=4 * len(CHUNKS), flops=8000000, grant=48,
    )
    got = exchange(send)
    field, out = call(
        final_kernel, [got, known, *state], [(NY, NX)] * 2, hbm_outs=range(2), scratch=[(NY, NX)] * 2,
        sems=2 * AGG_LAT, flops=1000000, grant=4,
    )
    return field, out


def solution(mesh):
    tile = P("lat", "lon")
    return jax.shard_map(
        body,
        mesh=mesh,
        in_specs=(tile, tile, tile, tile, P(AXES, None)),
        out_specs=(tile, tile),
        check_vma=False,
    )
```

```python
import functools
import math

import jax
import jax.numpy as jnp
from jax import lax
from jax.experimental import pallas as pl
from jax.experimental.pallas import tpu as pltpu
from jax.sharding import PartitionSpec as P

SWEEPS = 4
AGG_LAT = 4
AGG_LON = 2
LOW_EDGE = 0.1
HIGH_EDGE = 2.0
SHIFT_SCALE = 1.0e-5

NY = 512
NX = 256
HY = 16
WX = 9
ROWS = NY + 2 * HY
LANES = 128
BLK = 3
BAND = NY // AGG_LAT
STEP = 16
SWEEP = 16
CHUNKS = ((0, 152), (152, 128), (280, 128), (408, 136))
SLOTS = LANES // 8
AXES = ("lon", "lat")
F32 = jnp.float32


def chebyshev_plan(sweep_total):
    interval_mid = (HIGH_EDGE + LOW_EDGE) / 2.0
    interval_half = (HIGH_EDGE - LOW_EDGE) / 2.0
    mid_ratio = interval_mid / interval_half
    previous = 1.0 / mid_ratio
    pairs = []
    for _ in range(sweep_total - 1):
        fresh = 1.0 / (2.0 * mid_ratio - previous)
        pairs.append((fresh * previous, 2.0 * fresh / interval_half))
        previous = fresh
    return 1.0 / interval_mid, pairs


def cosine(x):
    square = x * x
    out = jnp.full_like(x, -1.0 / math.factorial(14))
    for k in range(6, -1, -1):
        out = out * square + (-1.0) ** k / math.factorial(2 * k)
    return out


def place():
    lat = lax.axis_index("lat")
    return lax.axis_index("lon") * lax.axis_size("lat") + lat, lat * NY


def latitudes(spot, total_rows, start, rows):
    index = spot[1] - HY + start + lax.broadcasted_iota(jnp.int32, (rows, LANES), 0)
    inside = (index >= 0) & (index <= total_rows - 2)
    return (index.astype(F32) + 0.5) * (2.6 / total_rows) - 1.3, inside


def lane_ids(rows):
    return lax.broadcasted_iota(jnp.int32, (rows, LANES), 1)


def east_of(blocks):
    lane = lane_ids(blocks[0].shape[0])
    rolled = [pltpu.roll(v, LANES - 1, 1) for v in blocks]
    return [jnp.where(lane == LANES - 1, rolled[(b + 1) % BLK], rolled[b]) for b in range(BLK)]


def west_of(blocks):
    lane = lane_ids(blocks[0].shape[0])
    rolled = [pltpu.roll(v, 1, 1) for v in blocks]
    return [jnp.where(lane == 0, rolled[(b + BLK - 1) % BLK], rolled[b]) for b in range(BLK)]


def load(ref, start, rows):
    return [ref[b, pl.ds(start, rows), :] for b in range(BLK)]


def store(ref, start, rows, blocks):
    for b in range(BLK):
        ref[b, pl.ds(start, rows), :] = blocks[b]


def for_strips(fn):
    for start in range(8, ROWS - 8, SWEEP):
        fn(start, min(SWEEP, ROWS - 8 - start))


def for_own(fn):
    for start in range(0, NY, STEP):
        fn(start // BAND, start)


def clear_ends(ref):
    zero = jnp.zeros((8, LANES), F32)
    for b in range(BLK):
        ref[b, 0:8, :] = zero
        ref[b, ROWS - 8 : ROWS, :] = zero


def operate(v_ref, east_ref, west_ref, north_ref, shift_ref, start, rows):
    here = load(v_ref, start, rows)
    up, down = load(v_ref, start + 1, rows), load(v_ref, start - 1, rows)
    right, left = east_of(here), west_of(here)
    ef, wf = load(east_ref, start, rows), load(west_ref, start, rows)
    nf, sf = load(north_ref, start, rows), load(north_ref, start - 1, rows)
    shift = shift_ref[pl.ds(start, rows), :]
    out = [
        shift * here[b]
        + ef[b] * (here[b] - right[b])
        + wf[b] * (here[b] - left[b])
        + nf[b] * (here[b] - up[b])
        + sf[b] * (here[b] - down[b])
        for b in range(BLK)
    ]
    return here, out


def fold(x):
    return jnp.sum(x.reshape(-1, 8, LANES), axis=0)


def total(x):
    return jnp.sum(jnp.sum(x, axis=1, keepdims=True), axis=0, keepdims=True)


def own_row(spot, values, scalars=()):
    lane = lane_ids(1)
    base = (spot[0] % SLOTS) * 8
    other = ((spot[0] + SLOTS // 2) % SLOTS) * 8
    row = jnp.zeros((1, LANES), F32)
    for k, value in enumerate(values):
        row = jnp.where(lane == base + k, value, row)
    for k, value in enumerate(scalars):
        row = jnp.where(lane == other + k, value, row)
    return row


def own_row_sums(got_ref, count):
    rows = got_ref.shape[0]
    lane = lane_ids(rows)
    slot = lax.broadcasted_iota(jnp.int32, (rows, LANES), 0) % SLOTS
    other = ((slot + SLOTS // 2) % SLOTS) * 8
    got = got_ref[...]
    return [total(fold(jnp.where(lane == other + k, got, 0.0))) for k in range(count)]


def fill_rows(ref, row):
    ref[...] = jnp.broadcast_to(row, ref.shape)


def pack_kernel(
    rhs_hbm, depth_hbm, mask_hbm, basis_hbm, inverse_hbm,
    gather_ref, west_ref, east_ref, fields_out,
    rhs_ref, depth_ref, mask_ref, basis_ref, inverse_ref, edge_ref, fields_ref, sems,
):
    spot = place()
    pairs = ((rhs_hbm, rhs_ref), (mask_hbm, mask_ref), (basis_hbm, basis_ref), (depth_hbm, depth_ref))
    copies = []
    for g in range(AGG_LAT):
        at = pl.ds(g * BAND, BAND)
        copies.append(
            [pltpu.make_async_copy(src.at[at], dst.at[at], sems.at[4 * g + k]) for k, (src, dst) in enumerate(pairs)]
        )
    last = pltpu.make_async_copy(inverse_hbm, inverse_ref, sems.at[4 * AGG_LAT])
    for copy in sum(copies, []) + [last]:
        copy.start()
    groups = inverse_ref.shape[1] // LANES
    lane = lane_ids(STEP)
    sums, outs = [], []
    zero = jnp.zeros((8, LANES), F32)
    for g in range(AGG_LAT):
        for copy in copies[g]:
            copy.wait()
        accs = [zero] * AGG_LON
        for start in range(g * BAND, (g + 1) * BAND, STEP):
            out_row = start - g * BAND
            fields = []
            for b in range(AGG_LON):
                at = (pl.ds(start, STEP), pl.ds(b * LANES, LANES))
                mask = mask_ref[at].astype(F32)
                wet = depth_ref[at] * mask
                res = rhs_ref[at] * mask
                weight = basis_ref[at] * mask
                accs[b] = accs[b] + fold(weight * res)
                fields.append((wet, res, weight))
                for f, value in enumerate(fields[b]):
                    fields_ref[f, b, start : start + STEP, :] = value
                    for side, first in ((0, 0), (1, NY - HY)):
                        if start == first:
                            at = ((side * 3 + f) * 2 + b) * HY
                            edge_ref[at : at + HY, :] = value
            for ref, b, extra in ((west_ref, 0, 0), (east_ref, 1, WX)):
                packed = jnp.zeros((STEP, LANES), F32) if g == 0 else ref[out_row : out_row + STEP, :]
                for f in range(3):
                    lo = 32 * g + WX * f
                    moved = pltpu.roll(fields[b][f], (lo + extra) % LANES, 1)
                    packed = jnp.where((lane >= lo) & (lane < lo + WX), moved, packed)
                ref[out_row : out_row + STEP, :] = packed
        sums += [total(acc) for acc in accs]
        rows = (slice(None), slice(None), pl.ds(g * BAND, BAND))
        outs.append(send_out(fields_ref.at[rows], fields_out.at[0:3].at[rows], sems.at[4 * AGG_LAT + 1 + g]))
    fill_rows(gather_ref, own_row(spot, sums))
    last.wait()
    for g in range(groups):
        part = inverse_ref[:, g * LANES : (g + 1) * LANES]
        west_ref[BAND + 8 * g : BAND + 8 * g + 8, :] = part
        east_ref[BAND + 8 * g : BAND + 8 * g + 8, :] = part
    outs.append(send_out(edge_ref, fields_out.at[3, 0, 0 : edge_ref.shape[0]], sems.at[5 * AGG_LAT + 1]))
    outs.append(send_out(west_ref.at[BAND:], fields_out.at[3, 1, 0 : 8 * groups], sems.at[5 * AGG_LAT + 2]))
    for copy in outs:
        copy.wait()


def unpack_columns(left_ref, right_ref, g, start, rows):
    lane = lane_ids(rows)
    left, right = left_ref[pl.ds(start, rows), :], right_ref[pl.ds(start, rows), :]
    out = []
    for f in range(3):
        lo = 32 * g + WX * f
        from_right = pltpu.roll(right, (LANES - lo) % LANES, 1)
        from_left = pltpu.roll(left, (2 * LANES - lo - WX) % LANES, 1)
        out.append(jnp.where(lane < WX, from_right, jnp.where(lane >= LANES - WX, from_left, 0.0)))
    return out


def edge_kernel(fields_hbm, left_ref, right_ref, south_ref, north_ref, solver_ref, edge_ref, own_ref, sems):
    rows8 = own_ref.shape[0]
    groups = rows8 // 8
    pairs = ((fields_hbm.at[3, 0, 0 : edge_ref.shape[0]], edge_ref), (fields_hbm.at[3, 1, 0:rows8], own_ref))
    copies = fetch(pairs, sems, 0)
    for k, ref in ((1, left_ref), (2, right_ref)):
        solver_ref[k * rows8 : (k + 1) * rows8, :] = ref[BAND:, :]
    for copy in copies:
        copy.wait()
    solver_ref[0:rows8, :] = own_ref[...]
    sub = lax.broadcasted_iota(jnp.int32, (8, LANES), 0)
    for side, (ref, start, band) in enumerate(((south_ref, 0, 0), (north_ref, BAND - HY, AGG_LAT - 1))):
        halo = unpack_columns(left_ref, right_ref, band, start, HY)
        for f in range(3):
            for b in range(BLK):
                at = (f * BLK + b) * HY
                row = ((side * 3 + f) * 2 + b) * HY
                ref[at : at + HY, :] = edge_ref[row : row + HY, :] if b < 2 else halo[f]
        base = 3 * BLK * HY
        for i in range(groups):
            at = slice(BAND + 8 * i, BAND + 8 * i + 8)
            own, left, right = own_ref[8 * i : 8 * i + 8, :], left_ref[at, :], right_ref[at, :]
            own = pltpu.roll(own, (8 - 2 * band) % 8, 0) if band else own
            left = pltpu.roll(left, (2 - 2 * band - 1 + 16) % 8, 0)
            right = pltpu.roll(right, (3 - 2 * band + 16) % 8, 0)
            picked = jnp.where(sub < 2, own, jnp.where(sub == 2, left, right))
            ref[base + 8 * i : base + 8 * i + 8, :] = picked


def north_faces(spot, total_rows, wet_ref, north_ref, start, rows):
    wet, nxt = load(wet_ref, start, rows), load(wet_ref, start + 1, rows)
    latitude, inside = latitudes(spot, total_rows, start, rows)
    cos_row = jnp.where(inside, cosine(latitude + 1.3 / total_rows), 0.0)
    store(north_ref, start, rows, [jnp.minimum(wet[b], nxt[b]) * cos_row for b in range(BLK)])


def all_faces(spot, total_rows, wet_ref, faces, start, rows):
    east_ref, west_ref, north_ref, shift_ref = faces
    wet = load(wet_ref, start, rows)
    cos_row = cosine(latitudes(spot, total_rows, start, rows)[0])
    shift_ref[pl.ds(start, rows), :] = SHIFT_SCALE * cos_row
    over = 1.0 / cos_row
    nxt = east_of(wet)
    face = [jnp.minimum(wet[b], nxt[b]) * over for b in range(BLK)]
    store(east_ref, start, rows, face)
    store(west_ref, start, rows, west_of(face))
    north_faces(spot, total_rows, wet_ref, north_ref, start, rows)


def first_step(res_ref, inv_ref, faces, est_ref, step_ref, start, rows):
    east_ref, west_ref, north_ref, shift_ref = faces
    ef, wf = load(east_ref, start, rows), load(west_ref, start, rows)
    nf, sf = load(north_ref, start, rows), load(north_ref, start - 1, rows)
    shift = shift_ref[pl.ds(start, rows), :]
    inv = [1.0 / (shift + ef[b] + wf[b] + nf[b] + sf[b]) for b in range(BLK)]
    store(inv_ref, start, rows, inv)
    res = load(res_ref, start, rows)
    value = [chebyshev_plan(SWEEPS)[0] * (inv[b] * res[b]) for b in range(BLK)]
    store(step_ref, start, rows, value)
    store(est_ref, start, rows, value)


def smooth(res_ref, inv_ref, faces, est_refs, step_ref, finish):
    _, pairs = chebyshev_plan(SWEEPS)
    for k, (c1, c2) in enumerate(pairs):
        src, dst = est_refs[k % 2], est_refs[(k + 1) % 2]
        last = k == len(pairs) - 1

        def strip(start, rows, band=None):
            here, applied = operate(src, *faces, start, rows)
            inv, res, step = load(inv_ref, start, rows), load(res_ref, start, rows), load(step_ref, start, rows)
            step = [c1 * step[b] + c2 * (inv[b] * (res[b] - applied[b])) for b in range(BLK)]
            value = [here[b] + step[b] for b in range(BLK)]
            if last:
                finish(start, rows, band, value)
            else:
                store(step_ref, start, rows, step)
                store(dst, start, rows, value)

        if last:
            for_bands(strip)
        else:
            for_strips(strip)


def fetch(pairs, sems, first):
    return [send_out(src, dst, sems.at[first + k]) for k, (src, dst) in enumerate(pairs)]


def coarse_solve(got_ref, parts):
    groups = got_ref.shape[0] // SLOTS
    accs = [jnp.zeros((8, LANES), F32) for _ in parts]
    mine = lane_ids(SLOTS) // 8 == lax.broadcasted_iota(jnp.int32, (SLOTS, LANES), 0)
    for i in range(groups):
        vec = jnp.sum(jnp.where(mine, got_ref[i * SLOTS : (i + 1) * SLOTS, :], 0.0), axis=0, keepdims=True)
        for k, (ref, first) in enumerate(parts):
            accs[k] = accs[k] + ref[first + 8 * i : first + 8 * i + 8, :] * vec
    own, left, right, below, above = [jnp.sum(acc, axis=1, keepdims=True) for acc in accs]
    low = lane_ids(1) < LANES // 2

    def spread(value):
        return jnp.broadcast_to(value, (1, LANES))

    def edge(x):
        halo = jnp.where(low, spread(x[3:4]), spread(x[2:3]))
        return [spread(x[0:1]), spread(x[1:2]), halo]

    rows = [edge(below)]
    for a in range(AGG_LAT):
        halo = jnp.where(low, spread(right[2 * a : 2 * a + 1]), spread(left[2 * a + 1 : 2 * a + 2]))
        rows.append([spread(own[2 * a : 2 * a + 1]), spread(own[2 * a + 1 : 2 * a + 2]), halo])
    rows.append(edge(above))
    return rows


def for_bands(fn):
    fn(HY - 8, 8, 0)
    for_own(lambda a, start: fn(HY + start, STEP, a + 1))
    fn(HY + NY, 8, AGG_LAT + 1)


class Stream:
    def __init__(self, src, refs, sems):
        self.chunks, self.done, self.rows = [], 0, 0
        for k, (start, rows) in enumerate(CHUNKS):
            chunk = []
            for i, dst in enumerate(refs):
                if dst.shape[0] == BLK:
                    lo, hi, shift = start, start + rows, 0
                else:
                    lo, hi, shift = max(start, HY), min(start + rows, HY + NY), HY
                chunk.append(
                    pltpu.make_async_copy(
                        src.at[i, 0 : dst.shape[0], lo:hi, :],
                        dst.at[:, lo - shift : hi - shift, :],
                        sems.at[k * len(refs) + i],
                    )
                )
            for copy in chunk:
                copy.start()
            self.chunks.append(chunk)

    def need(self, row):
        while self.rows < min(row, ROWS):
            for copy in self.chunks[self.done]:
                copy.wait()
            self.rows = sum(CHUNKS[self.done])
            self.done += 1


def send_out(src, dst, sem):
    copy = pltpu.make_async_copy(src, dst, sem)
    copy.start()
    return copy


def fill_from(fields_hbm, which, refs, bufs, left_ref, right_ref, sems):
    bands = [(slice(None), pl.ds(a * BAND, BAND)) for a in range(AGG_LAT)]
    copies = [
        fetch([(fields_hbm.at[f].at[at], buf.at[at]) for f, buf in zip(which, bufs)], sems, a * len(which))
        for a, at in enumerate(bands)
    ]

    def fill(g, start):
        if start % BAND == 0:
            for copy in copies[g]:
                copy.wait()
        at = slice(HY + start, HY + start + STEP)
        halo = unpack_columns(left_ref, right_ref, g, start - g * BAND, STEP)
        for f, ref, buf in zip(which, refs, bufs):
            for b in range(2):
                ref[b, at, :] = buf[b, start : start + STEP, :]
            ref[2, at, :] = halo[f]

    return lambda: for_own(fill)


def fill_rows_around(f, ref, below_ref, above_ref):
    for b in range(BLK):
        at = (f * BLK + b) * HY
        ref[b, 0:HY, :] = below_ref[at : at + HY, :]
        ref[b, HY + NY : ROWS, :] = above_ref[at : at + HY, :]


def fill_kernel(left_ref, right_ref, fields_hbm, wet_ref, res_ref, buf_a, buf_b, sems):
    fill_from(fields_hbm, (0, 1), (wet_ref, res_ref), (buf_a, buf_b), left_ref, right_ref, sems)()


def search_kernel(
    total_rows,
    wet_in, res_in, got_ref, solver_ref, left_ref, right_ref, below_ref, above_ref, fields_hbm,
    wet_ref, res_ref, send_ref, applied_ref, carry_out,
    buf_ref, search_ref, weight_ref, east_ref, north_ref, west_ref, inv_ref, est_a, est_b, step_ref, shift_ref, sems,
):
    spot = place()
    fill_weight = fill_from(fields_hbm, (2,), (weight_ref,), (buf_ref,), left_ref, right_ref, sems.at[8:12])
    for f, ref in enumerate((wet_ref, res_ref, weight_ref)):
        fill_rows_around(f, ref, below_ref, above_ref)
    own_rows = (slice(0, AGG_LON), slice(HY, HY + NY))
    outs = [
        send_out(wet_ref, carry_out.at[5], sems.at[7]),
        send_out(res_ref.at[own_rows], carry_out.at[3].at[own_rows], sems.at[3]),
    ]
    base, rows8 = 3 * BLK * HY, solver_ref.shape[0] // 3
    outs += [
        send_out(solver_ref, carry_out.at[6, 0, 0 : 3 * rows8], sems.at[1]),
        send_out(below_ref.at[base : base + rows8], carry_out.at[6, 1, 0:rows8], sems.at[2]),
        send_out(above_ref.at[base : base + rows8], carry_out.at[6, 2, 0:rows8], sems.at[5]),
    ]

    north_faces(spot, total_rows, wet_ref, north_ref, 0, 8)
    for ref in (est_a, est_b, search_ref, applied_ref, east_ref):
        clear_ends(ref)
    for b in range(BLK):
        north_ref[b, ROWS - 8 : ROWS, :] = jnp.zeros((8, LANES), F32)
    faces = (east_ref, west_ref, north_ref, shift_ref)

    def prepare(start, rows):
        all_faces(spot, total_rows, wet_ref, faces, start, rows)
        first_step(res_ref, inv_ref, faces, est_a, step_ref, start, rows)

    for_strips(prepare)
    outs += [send_out(east_ref, carry_out.at[1], sems.at[4]), send_out(north_ref, carry_out.at[2], sems.at[6])]
    fill_weight()
    outs.append(send_out(weight_ref, carry_out.at[0], sems.at[0]))
    parts = [(solver_ref, k * rows8) for k in range(3)] + [(below_ref, base), (above_ref, base)]
    coarse = coarse_solve(got_ref, parts)

    def finish(start, rows, band, value):
        wet, weight = load(wet_ref, start, rows), load(weight_ref, start, rows)
        part = [jnp.where(wet[b] > 0.0, value[b], 0.0) for b in range(BLK)]
        store(search_ref, start, rows, [part[b] + weight[b] * coarse[band][b] for b in range(BLK)])

    smooth(res_ref, inv_ref, faces, (est_a, est_b), step_ref, finish)
    outs.append(send_out(search_ref, carry_out.at[4], sems.at[12]))
    sums = [jnp.zeros((8, LANES), F32)] * (AGG_LAT * AGG_LON + 2)

    def apply(start, rows, band):
        here, out = operate(search_ref, *faces, start, rows)
        store(applied_ref, start, rows, out)
        if 0 < band <= AGG_LAT:
            for b in range(AGG_LON):
                k, at = (band - 1) * AGG_LON + b, (b, slice(start, start + rows))
                sums[k] = sums[k] + fold(weight_ref[at] * out[b])
                sums[-2] = sums[-2] + fold(here[b] * out[b])
                sums[-1] = sums[-1] + fold(here[b] * res_ref[at])

    for_bands(apply)
    values = [total(x) for x in sums]
    fill_rows(send_ref, own_row(spot, values[:-2], values[-2:]))
    for copy in outs:
        copy.wait()


def second_kernel(
    total_rows,
    applied_ref, carry_hbm,
    out_ref, search_ref, rows_ref,
    wet_ref, east_ref, north_ref, west_ref, inv_ref, est_a, est_b, step_ref, shift_ref, sems,
):
    spot = place()
    stream = Stream(carry_hbm.at[5:6], (wet_ref,), sems)
    rows8 = rows_ref.shape[0] // 5
    pairs = [
        (carry_hbm.at[6, 0, 0 : 3 * rows8], rows_ref.at[0 : 3 * rows8]),
        (carry_hbm.at[6, 1, 0:rows8], rows_ref.at[3 * rows8 : 4 * rows8]),
        (carry_hbm.at[6, 2, 0:rows8], rows_ref.at[4 * rows8 : 5 * rows8]),
        (carry_hbm.at[4], search_ref),
    ]
    back = fetch(pairs, sems, len(CHUNKS))
    stream.need(HY)
    north_faces(spot, total_rows, wet_ref, north_ref, 0, 8)
    for ref in (est_a, est_b):
        clear_ends(ref)
    faces = (east_ref, west_ref, north_ref, shift_ref)

    def prepare(start, rows):
        stream.need(start + rows + 1)
        all_faces(spot, total_rows, wet_ref, faces, start, rows)
        first_step(applied_ref, inv_ref, faces, est_a, step_ref, start, rows)

    for_strips(prepare)

    def finish(start, rows, band, value):
        store(out_ref, start, rows, value)

    smooth(applied_ref, inv_ref, faces, (est_a, est_b), step_ref, finish)
    for copy in back:
        copy.wait()


def sums_kernel(
    total_rows,
    got_ref, smooth_ref, applied_ref, search_ref, rows_ref, carry_hbm,
    send_ref, known_ref, search_out, applied_out, update_ref, operated_ref, rest_ref,
    weight_ref, east_ref, north_ref, res_ref, full_ref, sems,
):
    spot = place()
    rows8 = rows_ref.shape[0] // 5
    stream = Stream(carry_hbm, (weight_ref, east_ref, north_ref, res_ref), sems)
    coarse = coarse_solve(got_ref, [(rows_ref, k * rows8) for k in range(5)])
    curvature, projection = own_row_sums(got_ref, 2)
    lane = lane_ids(1)
    alpha = jnp.broadcast_to(projection, (1, LANES)) / jnp.broadcast_to(curvature, (1, LANES))
    known_ref[...] = jnp.broadcast_to(jnp.where(lane == 0, curvature, alpha), (8, LANES))

    def build(start, rows, band):
        stream.need(start + rows)
        part, weight, search = [load(ref, start, rows) for ref in (smooth_ref, weight_ref, search_ref)]
        store(
            full_ref, start, rows,
            [
                search[b] - alpha * (jnp.where(weight[b] > 0.0, part[b], 0.0) + weight[b] * coarse[band][b])
                for b in range(BLK)
            ],
        )

    accs = [jnp.zeros((8, LANES), F32)] * 4

    def apply(start):
        at, start = slice(start, start + STEP), HY + start
        here = load(full_ref, start, STEP)
        up, down = load(full_ref, start + 1, STEP), load(full_ref, start - 1, STEP)
        right, left = east_of(here), west_of(here)
        ef = load(east_ref, start, STEP)
        wf = west_of(ef)
        nf, sf = load(north_ref, start, STEP), load(north_ref, start - 1, STEP)
        shift = SHIFT_SCALE * cosine(latitudes(spot, total_rows, start, STEP)[0])
        for b in range(AGG_LON):
            out = (
                shift * here[b]
                + ef[b] * (here[b] - right[b])
                + wf[b] * (here[b] - left[b])
                + nf[b] * (here[b] - up[b])
                + sf[b] * (here[b] - down[b])
            )
            search, applied = search_ref[b, start : start + STEP, :], applied_ref[b, start : start + STEP, :]
            rest = res_ref[b, at, :] - alpha * applied
            search_out[b, at, :] = search
            applied_out[b, at, :] = applied
            update_ref[b, at, :] = here[b]
            operated_ref[b, at, :] = out
            rest_ref[b, at, :] = rest
            pairs = ((here[b], applied), (here[b], out), (here[b], rest), (search, rest))
            for k, (x, y) in enumerate(pairs):
                accs[k] = accs[k] + fold(x * y)

    waiting = []

    def step(start, rows, band):
        build(start, rows, band)
        for ready in waiting:
            apply(ready)
        waiting.clear()
        if 0 < band <= AGG_LAT:
            waiting.append(start - HY)

    for_bands(step)
    stream.need(ROWS)
    row = jnp.zeros((1, LANES), F32)
    for k, acc in enumerate(accs):
        row = jnp.where(lane == k, total(acc), row)
    fill_rows(send_ref, row)


def final_kernel(
    got_ref, known_ref, search_ref, applied_ref, update_ref, operated_ref, rest_ref,
    field_out, residual_out, field_ref, residual_ref, sems,
):
    sums = jnp.sum(got_ref[...], axis=0, keepdims=True)
    lane = lane_ids(1)

    def pick(row, k):
        return jnp.broadcast_to(jnp.sum(jnp.where(lane == k, row, 0.0), axis=1, keepdims=True), (1, LANES))

    u_ap, u_au, u_r, p_r = [pick(sums, k) for k in range(4)]
    p_ap, alpha = pick(known_ref[0:1, :], 0), pick(known_ref[0:1, :], 1)
    beta = -u_ap / p_ap
    curvature = u_au + 2.0 * beta * u_ap + beta * beta * p_ap
    step_size = (u_r + beta * p_r) / curvature
    along = alpha + step_size * beta
    back = step_size * beta
    copies = []

    def own(a, start):
        at = slice(start, start + STEP)
        for b in range(AGG_LON):
            out = (at, slice(b * LANES, (b + 1) * LANES))
            field_ref[out] = along * search_ref[b, at, :] + step_size * update_ref[b, at, :]
            residual_ref[out] = rest_ref[b, at, :] - step_size * operated_ref[b, at, :] - back * applied_ref[b, at, :]
        if (start + STEP) % BAND == 0:
            rows = pl.ds(a * BAND, BAND)
            copies.append(send_out(field_ref.at[rows], field_out.at[rows], sems.at[2 * a]))
            copies.append(send_out(residual_ref.at[rows], residual_out.at[rows], sems.at[2 * a + 1]))

    for_own(own)
    for copy in copies:
        copy.wait()


def call(kernel, args, outs, scratch=(), hbm_outs=(), sems=0, flops=0, grant=6, hbm=(), aliases=None):
    def spec(i, inside):
        return pl.BlockSpec(memory_space=pl.ANY if i in (hbm if inside else hbm_outs) else pltpu.VMEM)

    return pl.pallas_call(
        kernel,
        out_shape=[jax.ShapeDtypeStruct(s, F32) for s in outs],
        in_specs=[spec(i, True) for i in range(len(args))],
        out_specs=[spec(i, False) for i in range(len(outs))],
        scratch_shapes=[pltpu.VMEM(s, F32) if isinstance(s, tuple) else s for s in scratch]
        + ([pltpu.SemaphoreType.DMA((sems,))] if sems else []),
        input_output_aliases=aliases or {},
        compiler_params=pltpu.CompilerParams(vmem_limit_bytes=int(grant * 1024 * 1024)),
        cost_estimate=pl.CostEstimate(flops=flops, bytes_accessed=4 * 1024 * 1024, transcendentals=0),
    )(*args)


def exchange(x):
    return lax.all_to_all(x, AXES, 0, 0, tiled=True)


def body(rhs, depth, mask, basis, inverse):
    n_lon, n_lat = lax.axis_size("lon"), lax.axis_size("lat")
    devices = n_lon * n_lat
    total_rows = NY * n_lat
    full = (BLK, ROWS, LANES)
    half = (AGG_LON, NY, LANES)
    rows8 = 8 * (inverse.shape[1] // LANES)
    row = (devices, LANES)

    loads = [(NY, NX), (NY, NX), pltpu.VMEM((NY, NX), jnp.int32), (NY, NX), inverse.shape]
    pack = (BAND + rows8, LANES)
    gather, to_west, to_east, fields = call(
        pack_kernel, [rhs, depth, mask, basis, inverse], [row, pack, pack, (4, *half)], hbm_outs=(3,),
        scratch=[*loads, (12 * HY, LANES), (3, *half)], sems=5 * AGG_LAT + 3, hbm=range(5), grant=56,
    )
    ring = [(i, (i + 1) % n_lon) for i in range(n_lon)]
    left = lax.ppermute(to_east, "lon", ring)
    right = lax.ppermute(to_west, "lon", [(j, i) for i, j in ring])
    got = exchange(gather)
    edge = (3 * BLK * HY + rows8, LANES)
    to_south, to_north, solver = call(
        edge_kernel, [fields, left, right], [edge, edge, (3 * rows8, LANES)], hbm=(0,),
        scratch=[(12 * HY, LANES), (rows8, LANES)], sems=2, grant=52.5,
    )
    line = [(i, i + 1) for i in range(n_lat - 1)]
    below = lax.ppermute(to_north, "lat", line)
    above = lax.ppermute(to_south, "lat", [(j, i) for i, j in line])

    ext = call(
        fill_kernel, [left, right, fields], [full] * 2, hbm=(2,), scratch=[half, half], sems=2 * AGG_LAT,
        flops=20000000, grant=50.5,
    )
    _, _, send, applied, carry = call(
        functools.partial(search_kernel, total_rows), [*ext, got, solver, left, right, below, above, fields],
        [full] * 2 + [row, full, (7, *full)], hbm=(8,), hbm_outs=(4,), aliases={0: 0, 1: 1},
        scratch=[half] + [full] * 9 + [full[1:]], sems=13, flops=40000000, grant=49.5,
    )
    got = exchange(send)
    smoothed, search, solver = call(
        functools.partial(second_kernel, total_rows), [applied, carry],
        [full, full, (5 * rows8, LANES)], hbm=(1,), scratch=[full] * 8 + [full[1:]], sems=len(CHUNKS) + 4, flops=20000000, grant=50,
    )
    send, known, *state = call(
        functools.partial(sums_kernel, total_rows), [got, smoothed, applied, search, solver, carry],
        [row, (8, LANES)] + [half] * 5, hbm=(5,),
        scratch=[full, full, full, half, full], sems=4 * len(CHUNKS), flops=8000000, grant=48,
    )
    got = exchange(send)
    field, out = call(
        final_kernel, [got, known, *state], [(NY, NX)] * 2, hbm_outs=range(2), scratch=[(NY, NX)] * 2,
        sems=2 * AGG_LAT, flops=1000000, grant=4,
    )
    return field, out


def solution(mesh):
    tile = P("lat", "lon")
    return jax.shard_map(
        body,
        mesh=mesh,
        in_specs=(tile, tile, tile, tile, P(AXES, None)),
        out_specs=(tile, tile),
        check_vma=False,
    )
```
